32 devices in a mesh: fsdp: 4 (over y, x), ctx: 4 (over z), tp: 2 (over core).
Axes of the slice: x: 2, y: 2, z: 4, core: 2. Of those that a mesh axis runs over, the one named last changes fastest.
Arguments:
- block_input: bfloat16 [8, 1024, 2560], P('fsdp', 'ctx'), may hold values from -6 to 6
- segments: int32 [8, 1024], P('fsdp', 'ctx'), may hold values from 0 to 4, as said below
- token_mask: int32 [8, 1024], P('fsdp', 'ctx'), may hold values from 0 to 1, as said below
- cotangent: bfloat16 [8, 1024, 2560], P('fsdp', 'ctx'), may hold values from -6 to 6
- norm_gains: float32 [2, 2560], replicated, may hold values from 0.1 to 1.9
- conv_taps: float32 [4, 2560], P(None, 'tp'), may hold values from -3 to 3
- conv_offset: float32 [2560], P('tp'), may hold values from -3 to 3
- gate_offset: float32 [2, 2560], P(None, 'tp'), may hold values from -4 to 4
- decay_logit: float32 [2560], P('tp'), may hold values from 4.5 to 10
- intake: bfloat16 [2560, 2, 2560], P(('fsdp', 'ctx'), None, 'tp'), may hold values from -0.125 to 0.125
- gate_blocks: bfloat16 [256, 2, 2560], P(('fsdp', 'ctx'), None, 'tp'), may hold values from -0.375 to 0.375
- outlet: bfloat16 [2560, 2560], P(('fsdp', 'ctx'), 'tp'), may hold values from -0.5 to 0.5
- expand: bfloat16 [2560, 2, 7680], P(('fsdp', 'ctx'), None, 'tp'), may hold values from -0.125 to 0.125
- contract: bfloat16 [2560, 7680], P(('fsdp', 'ctx'), 'tp'), may hold values from -0.125 to 0.125
Outputs:
- block_output: bfloat16 [8, 1024, 2560], P('fsdp', 'ctx')
- input_grad: float32 [8, 1024, 2560], P('fsdp', 'ctx')
- gains_grad: float32 [2, 2560], replicated
- taps_grad: float32 [4, 2560], P(None, 'tp')
- offset_grad: float32 [2560], P('tp')
- gating_grad: float32 [2, 2560], P(None, 'tp')
- decay_grad: float32 [2560], P('tp')
- intake_grad: float32 [2560, 2, 2560], P(('fsdp', 'ctx'), None, 'tp')
- blocks_grad: float32 [256, 2, 2560], P(('fsdp', 'ctx'), None, 'tp')
- outlet_grad: float32 [2560, 2560], P(('fsdp', 'ctx'), 'tp')
- expand_grad: float32 [2560, 2, 7680], P(('fsdp', 'ctx'), None, 'tp')
- contract_grad: float32 [2560, 7680], P(('fsdp', 'ctx'), 'tp')
The draws below stay inside these ranges and needn't reach their ends.
Inputs may be any that keep to these rules, and one draw needn't show every extreme that they name: `segments`: segment numbers never fall along a row. Every row holds exactly five documents, numbered 0 to 4; document 0 ends before position 64, document 1 begins before position 128, document 3 begins at or after position 896 and before position 960, and document 4 begins at or after position 960. `token_mask`: in every row the ones come first; the padding is a final run of 1 to 64 positions.
All inputs are finite; a program needn't handle non-finite values.
Results may differ from the reference program's by a relative error of at most 0.015.
Values may be sent and summed in bfloat16 or wider, within the bound.
A program may use at most 280 MiB of HBM per device.

```python
import jax
import jax.numpy as jnp
from jax import lax

D = 2560
HEAD_W = 256
F = 7680
SPAN = 256
ROWS_MB = 1
MICRO = 2
R = 2560
LEN = 1024
SEQS = 8


def draw_segments(key, part):
    key = jax.random.fold_in(key, 11)
    keys = jax.random.split(key, 4)
    quarter = SPAN // 4
    half = SPAN // 2
    positions = jnp.arange(LEN, dtype=jnp.int32)[None, :]
    first_cut = jax.random.randint(keys[0], (SEQS, 1), 1, quarter)
    second_cut = jax.random.randint(keys[1], (SEQS, 1), quarter, half)
    third_cut = jax.random.randint(keys[2], (SEQS, 1), LEN - half, LEN - quarter)
    fourth_cut = jax.random.randint(keys[3], (SEQS, 1), LEN - quarter, LEN)
    summed = (positions >= first_cut).astype(jnp.int32) + (positions >= second_cut).astype(jnp.int32)
    summed = summed + (positions >= third_cut).astype(jnp.int32) + (positions >= fourth_cut).astype(jnp.int32)
    return summed


def draw_token_mask(key, part):
    key = jax.random.fold_in(key, 23)
    quarter = SPAN // 4
    positions = jnp.arange(LEN, dtype=jnp.int32)[None, :]
    pad_start = jax.random.randint(key, (SEQS, 1), LEN - quarter, LEN)
    return (positions < pad_start).astype(jnp.int32)


def draw_decay_logit(key, part):
    key = jax.random.fold_in(key, 37)
    values = jax.random.uniform(key, (R,), jnp.float32, 4.5, 10.0)
    return values


def shard_levels(key, dims, cuts, smallest, top_value):
    gain, own = 1.0, jax.random.fold_in(key, 6)
    for dim, blocks in cuts:
        draws = jnp.exp(jax.random.uniform(jax.random.fold_in(own, dim), (blocks,), jnp.float32, smallest / len(cuts), top_value / len(cuts)))
        gain = gain * jnp.repeat(draws, dims[dim] // blocks).reshape([-1 if axis == dim else 1 for axis in range(len(dims))])
    return gain


def normal_values(own_key, shape, scale, reach, cuts=(), held_as=jnp.bfloat16):
    values = jax.random.normal(own_key, shape, jnp.float32) * scale
    if len(cuts) > 0:
        values = shard_levels(own_key, shape, cuts, -0.22, 0.18) * values
    return jnp.clip(values, min=-reach, max=reach).astype(held_as)


def setup_inputs(seed: int = 0) -> dict:
    streams_of = jax.random.split(jax.random.key(seed), 15)
    block_input = normal_values(streams_of[0], (SEQS, LEN, D), 1.0, 6.0, ((0, 4), (1, 4)))
    segments = draw_segments(jax.random.fold_in(streams_of[14], 71), 0)
    token_mask = draw_token_mask(jax.random.fold_in(streams_of[14], 71), 0)
    cotangent = normal_values(streams_of[3], (SEQS, LEN, D), 1.0, 6.0, ((0, 4), (1, 4)))
    norm_gains = jnp.clip(1.0 + 0.18 * jax.random.normal(streams_of[4], (2, D), jnp.float32), 0.1, 1.9)
    conv_taps = normal_values(streams_of[5], (4, R), 0.5, 3.0, ((1, 2),), jnp.float32)
    conv_offset = normal_values(streams_of[6], (R,), 0.5, 3.0, ((0, 2),), jnp.float32)
    gate_offset = normal_values(streams_of[7], (2, R), 1.0, 4.0, ((1, 2),), jnp.float32)
    decay_logit = draw_decay_logit(jax.random.fold_in(streams_of[14], 71), 0)
    intake = normal_values(streams_of[9], (D, 2, R), D ** -0.5, 0.125, ((0, 16), (2, 2)))
    gate_blocks = normal_values(streams_of[10], (HEAD_W, 2, R), HEAD_W ** -0.5, 0.375, ((0, 16), (2, 2)))
    outlet = normal_values(streams_of[11], (D, R), (R // 16) ** -0.5, 0.5, ((0, 16), (1, 2)))
    expand = normal_values(streams_of[12], (D, 2, F), D ** -0.5, 0.125, ((0, 16), (2, 2)))
    contract = normal_values(streams_of[13], (D, F), (F // 4) ** -0.5, 0.125, ((0, 16), (1, 2)))
    return {"block_input": block_input, "segments": segments, "token_mask": token_mask, "cotangent": cotangent, "norm_gains": norm_gains, "conv_taps": conv_taps, "conv_offset": conv_offset, "gate_offset": gate_offset, "decay_logit": decay_logit, "intake": intake, "gate_blocks": gate_blocks, "outlet": outlet, "expand": expand, "contract": contract}


EPSILON = 1e-06
DECAY_SCALE = 8.0
TOP_PRECISION = lax.Precision.HIGHEST

@jax.custom_vjp
def low(v):
    return lax.optimization_barrier(v.astype(jnp.bfloat16)).astype(jnp.float32)

@jax.custom_vjp
def low_back(v):
    return v

def low_keep(v):
    return (low(v), None)

def low_pass(kept, grad):
    return (grad,)

def back_keep(v):
    return (v, None)

def back_low(kept, grad):
    return (low(grad),)
low.defvjp(low_keep, low_pass)
low_back.defvjp(back_keep, back_low)

def rms_scale(values, weighting):
    inverse = lax.rsqrt(lax.optimization_barrier(jnp.mean(values * values, axis=-1, keepdims=True)) + EPSILON)
    return values * inverse * weighting

def gelu_tanh(values):
    return jax.nn.gelu(values, approximate=True)

def conv_mix(before, current, conv_taps, conv_offset, seg_ext):
    joined = jnp.concatenate([before, current], axis=1)
    sequence_extent = current.shape[1]
    own_seg = seg_ext[:, 3:]
    summed = jnp.zeros(current.shape, jnp.float32) + conv_offset
    for tap_index in range(4):
        window = joined[:, 3 - tap_index:3 - tap_index + sequence_extent]
        matching = (seg_ext[:, 3 - tap_index:3 - tap_index + sequence_extent] == own_seg).astype(jnp.float32)
        summed = summed + conv_taps[tap_index] * window * matching[:, :, None]
    return summed

def lru_terms(pre_rate, pre_inlet, conv_out, decay_logit, gate_offset, starts):
    recur_gate = jax.nn.sigmoid(pre_rate + gate_offset[0])
    input_gate = jax.nn.sigmoid(pre_inlet + gate_offset[1])
    log_keep = -DECAY_SCALE * recur_gate * jax.nn.softplus(-decay_logit)
    carry_coef = jnp.exp(log_keep) * (1.0 - starts)
    norm_scale = jnp.where(starts > 0.5, 1.0, jnp.sqrt(-jnp.expm1(2.0 * log_keep)))
    return (carry_coef, input_gate * conv_out * norm_scale)

def merge_affine_maps(earlier, later):
    return (earlier[0] * later[0], later[0] * earlier[1] + later[1])

def affine_state_sweep(forget_multipliers, sweep_increment_terms):
    return lax.associative_scan(merge_affine_maps, (forget_multipliers, sweep_increment_terms), axis=1)

def forward(block_rows, seg_rows, norm_gains, conv_taps, conv_offset, gate_offset, decay_logit, intake, gate_blocks, outlet, expand, contract):
    group_rows, seq_len, embedding_dimension = block_rows.shape
    unit_count = intake.shape[2]
    head_count = unit_count // HEAD_W
    normed_rows = low(rms_scale(block_rows, norm_gains[0]))
    projected_rows = low_back(jnp.einsum('nfj,jeg->nfeg', normed_rows, intake, precision=TOP_PRECISION))
    gelu_in = projected_rows[:, :, 0]
    x_branch = low(projected_rows[:, :, 1])
    seg_ext = jnp.pad(seg_rows + 1, ((0, 0), (3, 0)))
    before = jnp.zeros((group_rows, 3, unit_count), jnp.float32)
    conv_out = low(conv_mix(before, x_branch, conv_taps, conv_offset, seg_ext))
    heads_in = conv_out.reshape(group_rows, seq_len, head_count, HEAD_W)
    blocks = gate_blocks.reshape(HEAD_W, 2, head_count, HEAD_W)
    gate_pre = low_back(jnp.einsum('slhi,ikhj->slkhj', heads_in, blocks, precision=TOP_PRECISION))
    gate_pre = gate_pre.reshape(group_rows, seq_len, 2, unit_count)
    starts = (seg_ext[:, 3:] != seg_ext[:, 2:-1]).astype(jnp.float32)[:, :, None]
    carry_coef, normed_x = lru_terms(gate_pre[:, :, 0], gate_pre[:, :, 1], conv_out, decay_logit, gate_offset, starts)
    states = affine_state_sweep(carry_coef, normed_x)[1]
    recurrent_block = low(states * gelu_tanh(gelu_in))
    branch_path = low_back(jnp.einsum('ewz,mz->ewm', recurrent_block, outlet, precision=TOP_PRECISION))
    residual = block_rows + branch_path
    second_normed_rows = low(rms_scale(residual, norm_gains[1]))
    expanded_rows = low_back(jnp.einsum('hni,izm->hnzm', second_normed_rows, expand, precision=TOP_PRECISION))
    hidden_rows = low(gelu_tanh(expanded_rows[:, :, 0]) * expanded_rows[:, :, 1])
    feed_output = low_back(jnp.einsum('tzo,no->tzn', hidden_rows, contract, precision=TOP_PRECISION))
    return residual + feed_output

def reference(block_input, segments, token_mask, cotangent, norm_gains, conv_taps, conv_offset, gate_offset, decay_logit, intake, gate_blocks, outlet, expand, contract):
    group_rows = MICRO * ROWS_MB
    group_count = block_input.shape[0] // group_rows
    params = (norm_gains, conv_taps, conv_offset, gate_offset, decay_logit, intake.astype(jnp.float32), gate_blocks.astype(jnp.float32), outlet.astype(jnp.float32), expand.astype(jnp.float32), contract.astype(jnp.float32))

    def one_group(totals, batch):
        block_rows, seg_rows, mask_rows, cot_rows = batch

        def apply_block(rows_float, gains_in, taps_in, offset_in, gating_in, decay_in, intake_in, blocks_in, outlet_in, expand_in, contract_in):
            return forward(rows_float, seg_rows, gains_in, taps_in, offset_in, gating_in, decay_in, intake_in, blocks_in, outlet_in, expand_in, contract_in)
        result, pull = jax.vjp(apply_block, block_rows.astype(jnp.float32), params[0], params[1], params[2], params[3], params[4], params[5], params[6], params[7], params[8], params[9])
        grads = pull(cot_rows.astype(jnp.float32) * mask_rows.astype(jnp.float32)[:, :, None])
        totals = jax.tree.map(jnp.add, totals, tuple(grads[1:]))
        return (totals, (result.astype(jnp.bfloat16), grads[0]))

    def grouped(array):
        return array.reshape((group_count, group_rows) + array.shape[1:])
    zero_grads = jax.tree.map(jnp.zeros_like, params)
    totals, (mixed, input_grad) = lax.scan(one_group, zero_grads, (grouped(block_input), grouped(segments), grouped(token_mask), grouped(cotangent)))
    mixed = mixed.reshape(block_input.shape)
    input_grad = input_grad.reshape(block_input.shape)
    return (mixed, input_grad, totals[0], totals[1], totals[2], totals[3], totals[4], totals[5], totals[6], totals[7], totals[8], totals[9])
```

```python
import jax
import jax.numpy as jnp
from jax import lax
from jax.experimental import pallas as pl
from jax.experimental.pallas import tpu as pltpu
from jax.sharding import PartitionSpec as P

HEAD_W = 256
LANES = 128
CHUNKS = 8

EPSILON = 1e-06
DECAY_SCALE = 8.0
GELU_C = 0.7978845608028654
GELU_A = 0.044715

F32 = jnp.float32
BF16 = jnp.bfloat16

TAP0, OFFSET, RATE_OFF, INLET_OFF, SOFTPLUS, NEG_SIG, PARAM_ROWS = 0, 4, 5, 6, 7, 8, 16


def shifted(x, axis, by):
    length = lax.axis_size(axis)
    pairs = [(i, i + by) for i in range(length) if 0 <= i + by < length]
    return lax.ppermute(x, axis, pairs)


def swap(x, axis):
    length = lax.axis_size(axis)
    return lax.ppermute(x, axis, [(i, (i + 1) % length) for i in range(length)])


def gelu_pair(v):
    t = jnp.tanh(GELU_C * (v + GELU_A * v * v * v))
    value = 0.5 * v * (1.0 + t)
    slope = 0.5 * (1.0 + t) + 0.5 * v * (1.0 - t * t) * GELU_C * (1.0 + 3.0 * GELU_A * v * v)
    return value, slope


def one_minus_exp(x):
    s = 1.0 + x / 7.0
    for n in (6.0, 5.0, 4.0, 3.0, 2.0):
        s = 1.0 + x / n * s
    return jnp.where(x > -0.5, -x * s, 1.0 - jnp.exp(x))


def sigmoid(v):
    return 1.0 / (1.0 + jnp.exp(-v))


def dot(a, b, dims):
    return lax.dot_general(a, b, (dims, ((), ())), preferred_element_type=F32)


def lane_scan(load_a, load_b, store, length, reverse):
    steps = length // CHUNKS
    prod = jnp.ones((CHUNKS, LANES), F32)
    total = jnp.zeros((CHUNKS, LANES), F32)
    for n in range(steps):
        s = steps - 1 - n if reverse else n
        coef = load_a(s)
        total = coef * total + load_b(s)
        prod = coef * prod
        store(s, prod, total)
    return prod, total


def chunk_carries(prod, total, reverse):
    order = range(CHUNKS - 1, -1, -1) if reverse else range(CHUNKS)
    run_p = jnp.ones((1, LANES), F32)
    run_s = jnp.zeros((1, LANES), F32)
    carries = [None] * CHUNKS
    for c in order:
        carries[c] = (run_p, run_s)
        run_s = prod[c : c + 1] * run_s + total[c : c + 1]
        run_p = prod[c : c + 1] * run_p
    return carries


def sweep(a_scr, b_scr, p_scr, s_scr, prod_ref, sum_ref, rows, length, reverse, shift):
    steps = length // CHUNKS
    for b in range(rows):
        for j in range(HEAD_W // LANES):
            av, bv, pv, sv = (a_scr.at[b, j], b_scr.at[b, j], p_scr.at[b, j], s_scr.at[b, j])

            def store(s, prod, total):
                pv[pl.ds(s, CHUNKS, stride=steps), :] = prod
                sv[pl.ds(s, CHUNKS, stride=steps), :] = total

            prod, total = lane_scan(
                lambda s: av[pl.ds(s + shift, CHUNKS, stride=steps), :],
                lambda s: bv[pl.ds(s, CHUNKS, stride=steps), :],
                store,
                length,
                reverse,
            )
            carries = chunk_carries(prod, total, reverse)
            lanes = slice(j * LANES, (j + 1) * LANES)
            for c in range(CHUNKS):
                here = slice(c * steps, (c + 1) * steps)
                p = pv[here, :]
                prod_ref[b, here, lanes] = p * carries[c][0]
                sum_ref[b, here, lanes] = sv[here, :] + p * carries[c][1]


def to_lanes(ref, b, at, value):
    for j in range(HEAD_W // LANES):
        ref[b, j, pl.ds(at, value.shape[0]), :] = value[:, j * LANES : (j + 1) * LANES]


def forward_kernel(
    x_ref, halo_ref, mask_ref, par_ref, w_ref,
    conv_ref, r_ref, i_ref, a_ref, prod_ref, sum_ref,
    ext, a_scr, b_scr, p_scr, s_scr,
):
    rows, length, _ = x_ref.shape
    par = par_ref[...]
    w0, w1 = w_ref[0], w_ref[1]
    for b in range(rows):
        ext[b, pl.ds(0, 8), :] = halo_ref[b]
        ext[b, pl.ds(8, length), :] = x_ref[b].astype(F32)
        conv = ext[b, pl.ds(8, length), :] * par[TAP0 : TAP0 + 1] + par[OFFSET : OFFSET + 1]
        for k in range(1, 4):
            match = mask_ref[b, :, k : k + 1]
            conv = conv + par[TAP0 + k : TAP0 + k + 1] * ext[b, pl.ds(8 - k, length), :] * match
        conv_low = conv.astype(BF16)
        conv_ref[b] = conv_low
        conv = conv_low.astype(F32)
        r = sigmoid(dot(conv_low, w0, ((1,), (0,))) + par[RATE_OFF : RATE_OFF + 1])
        i = sigmoid(dot(conv_low, w1, ((1,), (0,))) + par[INLET_OFF : INLET_OFF + 1])
        r_ref[b] = r
        i_ref[b] = i
        log_keep = -DECAY_SCALE * r * par[SOFTPLUS : SOFTPLUS + 1]
        going = mask_ref[b, :, 0:1]
        a = jnp.exp(log_keep) * going
        a_ref[b] = a
        scale = jnp.where(going > 0.5, jnp.sqrt(one_minus_exp(2.0 * log_keep)), 1.0)
        to_lanes(a_scr, b, 0, a)
        to_lanes(b_scr, b, 0, i * conv * scale)
    sweep(a_scr, b_scr, p_scr, s_scr, prod_ref, sum_ref, rows, length, False, 0)


def head_spec(rows, length):
    return pl.BlockSpec((rows, length, HEAD_W), lambda h: (0, 0, h))


def recurrent_forward(x_branch, halo, masks, params, blocks):
    rows, length, units = x_branch.shape
    full = head_spec(rows, length)
    scan = pltpu.VMEM((rows, HEAD_W // LANES, length, LANES), F32)
    big = jax.ShapeDtypeStruct((rows, length, units), F32)
    return pl.pallas_call(
        forward_kernel,
        grid=(units // HEAD_W,),
        in_specs=[
            full,
            head_spec(rows, 8),
            pl.BlockSpec((rows, length, 8), lambda h: (0, 0, 0)),
            pl.BlockSpec((PARAM_ROWS, HEAD_W), lambda h: (0, h)),
            pl.BlockSpec((2, HEAD_W, HEAD_W), lambda h: (0, 0, h)),
        ],
        out_specs=[full] * 6,
        out_shape=[jax.ShapeDtypeStruct((rows, length, units), BF16)] + [big] * 5,
        scratch_shapes=[pltpu.VMEM((rows, length + 8, HEAD_W), F32), scan, scan, scan, scan],
        compiler_params=pltpu.CompilerParams(vmem_limit_bytes=48 * 1024 * 1024),
        cost_estimate=pl.CostEstimate(
            flops=4 * rows * length * units * HEAD_W,
            bytes_accessed=24 * rows * length * units,
            transcendentals=8 * rows * length * units,
        ),
        name="recurrent_forward",
    )(x_branch, halo, masks, params, blocks)


def adjoint_kernel(
    rg_ref, gelu_ref, a_ref, prod_ref, sum_ref, in_ref,
    gg_ref, tprod_ref, tsum_ref,
    a_scr, b_scr, p_scr, s_scr,
):
    rows, length, _ = rg_ref.shape
    for b in range(rows):
        states = sum_ref[b] + prod_ref[b] * in_ref[b, 0:1]
        value, slope = gelu_pair(gelu_ref[b])
        rg = rg_ref[b]
        gg_ref[b] = (rg * states * slope).astype(BF16)
        to_lanes(a_scr, b, 0, a_ref[b])
        to_lanes(a_scr, b, length, jnp.ones((8, HEAD_W), F32))
        to_lanes(b_scr, b, 0, rg * value)
    sweep(a_scr, b_scr, p_scr, s_scr, tprod_ref, tsum_ref, rows, length, True, 1)


def recurrent_adjoint(rec_grad, gelu_in, coef, prod, total, state_in):
    rows, length, units = rec_grad.shape
    full = head_spec(rows, length)
    scan = pltpu.VMEM((rows, HEAD_W // LANES, length, LANES), F32)
    longer = pltpu.VMEM((rows, HEAD_W // LANES, length + 8, LANES), F32)
    big = jax.ShapeDtypeStruct((rows, length, units), F32)
    return pl.pallas_call(
        adjoint_kernel,
        grid=(units // HEAD_W,),
        in_specs=[full] * 5 + [head_spec(rows, 8)],
        out_specs=[full] * 3,
        out_shape=[jax.ShapeDtypeStruct((rows, length, units), BF16), big, big],
        scratch_shapes=[longer, scan, scan, scan],
        compiler_params=pltpu.CompilerParams(vmem_limit_bytes=48 * 1024 * 1024),
        cost_estimate=pl.CostEstimate(
            flops=30 * rows * length * units,
            bytes_accessed=32 * rows * length * units,
            transcendentals=rows * length * units,
        ),
        name="recurrent_adjoint",
    )(rec_grad, gelu_in, coef, prod, total, state_in)


def backward_kernel(
    tprod_ref, tsum_ref, leave_ref, prod_ref, sum_ref, in_ref, a_ref, r_ref, i_ref, conv_ref,
    x_ref, halo_ref, mask_ref, par_ref, w_ref,
    bx_ref, before_ref, small_ref, blocks_ref,
    ext, st_ext, g_ext,
):
    rows, length, _ = tprod_ref.shape
    par = par_ref[...]
    w0, w1 = w_ref[0], w_ref[1]
    sums = [jnp.zeros((1, HEAD_W), F32) for _ in range(8)]
    blocks = [jnp.zeros((HEAD_W, HEAD_W), F32) for _ in range(2)]

    def add(n, value):
        sums[n] = sums[n] + jnp.sum(value, axis=0, keepdims=True)

    for b in range(rows):
        adjoint = tsum_ref[b] + tprod_ref[b] * leave_ref[b, 0:1]
        st_ext[b, pl.ds(0, 8), :] = in_ref[b]
        st_ext[b, pl.ds(8, length), :] = sum_ref[b] + prod_ref[b] * in_ref[b, 0:1]
        prev = st_ext[b, pl.ds(7, length), :]
        r, i, a = r_ref[b], i_ref[b], a_ref[b]
        conv_low = conv_ref[b]
        conv = conv_low.astype(F32)
        going = mask_ref[b, :, 0:1]
        log_keep = -DECAY_SCALE * r * par[SOFTPLUS : SOFTPLUS + 1]
        scale = jnp.where(going > 0.5, jnp.sqrt(one_minus_exp(2.0 * log_keep)), 1.0)
        log_grad = adjoint * prev * a - adjoint * i * conv * (a * a) / scale
        rate = log_grad * (-DECAY_SCALE * par[SOFTPLUS : SOFTPLUS + 1]) * r * (1.0 - r)
        spread = adjoint * scale
        inlet = spread * conv * i * (1.0 - i)
        add(5, rate)
        add(6, inlet)
        add(7, log_grad * r)
        rate_low = rate.astype(BF16)
        inlet_low = inlet.astype(BF16)
        grad = spread * i + dot(rate_low, w0, ((1,), (1,))) + dot(inlet_low, w1, ((1,), (1,)))
        blocks[0] = blocks[0] + dot(conv_low, rate_low, ((0,), (0,)))
        blocks[1] = blocks[1] + dot(conv_low, inlet_low, ((0,), (0,)))
        ext[b, pl.ds(0, 8), :] = halo_ref[b]
        ext[b, pl.ds(8, length), :] = x_ref[b].astype(F32)
        add(4, grad)
        add(0, grad * ext[b, pl.ds(8, length), :])
        bx = grad * par[TAP0 : TAP0 + 1]
        g_ext[b, pl.ds(0, 8), :] = jnp.zeros((8, HEAD_W), F32)
        g_ext[b, pl.ds(8 + length, 8), :] = jnp.zeros((8, HEAD_W), F32)
        before = jnp.zeros((8, HEAD_W), F32)
        for k in range(1, 4):
            masked = grad * mask_ref[b, :, k : k + 1]
            add(k, masked * ext[b, pl.ds(8 - k, length), :])
            g_ext[b, pl.ds(8, length), :] = masked
            tap = par[TAP0 + k : TAP0 + k + 1]
            bx = bx + tap * g_ext[b, pl.ds(8 + k, length), :]
            before = before + tap * g_ext[b, pl.ds(k, 8), :]
        bx_ref[b] = bx
        before_ref[b] = before
    sums[7] = sums[7] * (DECAY_SCALE * par[NEG_SIG : NEG_SIG + 1])
    for n in range(8):
        small_ref[pl.ds(n, 1), :] = sums[n]
    blocks_ref[0] = blocks[0].astype(blocks_ref.dtype)
    blocks_ref[1] = blocks[1].astype(blocks_ref.dtype)


def recurrent_backward(tprod, tsum, leaving, prod, total, state_in, coef, r, i, conv_low, x_branch, halo, masks, params, blocks):
    rows, length, units = tprod.shape
    full = head_spec(rows, length)
    edge = head_spec(rows, 8)
    return pl.pallas_call(
        backward_kernel,
        grid=(units // HEAD_W,),
        in_specs=[
            full, full, edge, full, full, edge, full, full, full, full, full, edge,
            pl.BlockSpec((rows, length, 8), lambda h: (0, 0, 0)),
            pl.BlockSpec((PARAM_ROWS, HEAD_W), lambda h: (0, h)),
            pl.BlockSpec((2, HEAD_W, HEAD_W), lambda h: (0, 0, h)),
        ],
        out_specs=[
            full,
            edge,
            pl.BlockSpec((8, HEAD_W), lambda h: (0, h)),
            pl.BlockSpec((2, HEAD_W, HEAD_W), lambda h: (0, 0, h)),
        ],
        out_shape=[
            jax.ShapeDtypeStruct((rows, length, units), F32),
            jax.ShapeDtypeStruct((rows, 8, units), F32),
            jax.ShapeDtypeStruct((8, units), F32),
            jax.ShapeDtypeStruct((2, HEAD_W, units), BF16),
        ],
        scratch_shapes=[
            pltpu.VMEM((rows, length + 8, HEAD_W), F32),
            pltpu.VMEM((rows, length + 8, HEAD_W), F32),
            pltpu.VMEM((rows, length + 16, HEAD_W), F32),
        ],
        compiler_params=pltpu.CompilerParams(vmem_limit_bytes=48 * 1024 * 1024),
        cost_estimate=pl.CostEstimate(
            flops=8 * rows * length * units * HEAD_W,
            bytes_accessed=40 * rows * length * units,
            transcendentals=4 * rows * length * units,
        ),
        name="recurrent_backward",
    )(tprod, tsum, leaving, prod, total, state_in, coef, r, i, conv_low, x_branch, halo, masks, params, blocks)


def rms(values):
    return lax.rsqrt(jnp.mean(values * values, axis=-1, keepdims=True) + EPSILON)


def rms_back(values, inverse, gain, grad):
    u = grad * gain
    inner = jnp.mean(values * u, axis=-1, keepdims=True)
    gain_grad = jnp.sum(grad * values * inverse, axis=0)
    return inverse * u - values * (inverse * inverse * inverse) * inner, gain_grad


def exchange_units(x, axis):
    length, me = lax.axis_size(axis), lax.axis_index(axis)
    got = [lax.dynamic_index_in_dim(x, me, 0, keepdims=False)]
    for by in range(1, length):
        piece = lax.dynamic_index_in_dim(x, (me + by) % length, 0, keepdims=False)
        got.append(lax.ppermute(piece, axis, [(s, (s + by) % length) for s in range(length)]))
    stacked = jnp.stack(got)
    order = (me - jnp.arange(length)) % length
    return jnp.take(stacked, order, axis=0)


def shards(
    block_input, segments, token_mask, cotangent, norm_gains, conv_taps, conv_offset, gate_offset,
    decay_logit, intake, gate_blocks, outlet, expand, contract,
):
    rows, length, width = block_input.shape
    depth = intake.shape[0]
    units = intake.shape[2]
    hidden_units = contract.shape[1]
    tokens = rows * length
    ctx, tp = lax.axis_size("ctx"), lax.axis_size("tp")
    mine = lax.axis_index("tp")
    half = tokens // tp
    share = -(-hidden_units // (ctx * 256)) * 256
    padding = ctx * share - hidden_units

    def own(x):
        return lax.dynamic_slice_in_dim(x, mine * half, half, 0)

    def other(x):
        return lax.dynamic_slice_in_dim(x, (1 - mine) * half, half, 0)

    def join(x):
        theirs = swap(x, "tp")
        return jnp.concatenate(
            [jnp.where(mine == 0, x, theirs), jnp.where(mine == 0, theirs, x)], axis=0
        )

    w_intake = lax.all_gather(intake.reshape(depth, 2 * units), ("fsdp", "ctx"), axis=0, tiled=True)
    w_gates = lax.all_gather(gate_blocks, ("fsdp", "ctx"), axis=0, tiled=True)
    w_outlet = lax.all_gather(outlet, ("fsdp", "ctx"), axis=0, tiled=True)

    feed_in = jnp.concatenate([expand, contract[:, None, :]], axis=1)
    feed_in = jnp.pad(feed_in, ((0, 0), (0, 0), (0, padding)))
    feed_in = feed_in.reshape(depth, 3, ctx, share).transpose(2, 0, 1, 3).reshape(ctx, depth, 3 * share)
    feed_in = exchange_units(feed_in, "ctx").reshape(ctx * depth, 3 * share)
    w_feed = lax.all_gather(feed_in, "fsdp", axis=0, tiled=True)
    w_expand, w_contract = w_feed[:, : 2 * share], w_feed[:, 2 * share :]

    mask_rows = token_mask.astype(F32).reshape(tokens, 1)
    out_grad = own(cotangent.reshape(tokens, width)).astype(F32) * own(mask_rows)
    feed_grad = lax.all_gather(out_grad.astype(BF16), ("ctx", "tp"), axis=0, tiled=True)

    seg_next = segments + 1
    seg_before = shifted(seg_next[:, -3:], "ctx", 1)
    seg_ext = jnp.concatenate([seg_before, seg_next], axis=1)
    masks = jnp.stack(
        [(seg_ext[:, 3 - k : 3 - k + length] == seg_next).astype(F32) for k in (1, 1, 2, 3)]
        + [jnp.zeros(segments.shape, F32)] * 4,
        axis=2,
    )
    params = jnp.concatenate(
        [
            conv_taps,
            conv_offset[None],
            gate_offset,
            jax.nn.softplus(-decay_logit)[None],
            jax.nn.sigmoid(-decay_logit)[None],
            jnp.zeros((PARAM_ROWS - 9, units), F32),
        ],
        axis=0,
    )

    x = block_input.reshape(tokens, width).astype(F32)
    inverse_one = rms(x)
    normed = (x * inverse_one * norm_gains[0]).astype(BF16)
    x_branch = dot(normed, w_intake[:, units:], ((1,), (0,))).astype(BF16).reshape(rows, length, units)
    gelu_in = dot(normed, w_intake[:, :units], ((1,), (0,))).reshape(rows, length, units)
    x_before = shifted(x_branch[:, -3:], "ctx", 1)
    halo = jnp.pad(x_before, ((0, 0), (5, 0), (0, 0))).astype(F32)
    blocks = w_gates.transpose(1, 0, 2)
    conv_low, r, i, coef, prod, total = recurrent_forward(x_branch, halo, masks, params, blocks)
    ends = jnp.stack([prod[:, -1], total[:, -1]])
    entering = jnp.zeros((rows, units), F32)
    for by in range(ctx - 1, 0, -1):
        end = shifted(ends, "ctx", by)
        entering = end[1] + end[0] * entering
    state_in = jnp.broadcast_to(entering[:, None], (rows, 8, units))
    states = total + prod * entering[:, None]
    recurrent = (states * jax.nn.gelu(gelu_in, approximate=True)).astype(BF16).reshape(tokens, units)

    sent = swap(dot(other(recurrent), w_outlet, ((1,), (1,))), "tp")
    branch = dot(own(recurrent), w_outlet, ((1,), (1,))) + sent
    residual = own(x) + branch
    inverse_two = rms(residual)
    normed_two = lax.all_gather(
        (residual * inverse_two * norm_gains[1]).astype(BF16), ("ctx", "tp"), axis=0, tiled=True
    )

    expanded = dot(normed_two, w_expand, ((1,), (0,)))
    gate, up = expanded[:, :share], expanded[:, share:]
    value, slope = gelu_pair(gate)
    hidden = (value * up).astype(BF16)
    hidden_grad = dot(feed_grad, w_contract, ((1,), (0,)))
    expand_low = jnp.concatenate(
        [(hidden_grad * up * slope).astype(BF16), (hidden_grad * value).astype(BF16)], axis=1
    )
    normed_two_grad = lax.psum_scatter(
        dot(expand_low, w_expand, ((1,), (1,))).astype(BF16), ("ctx", "tp"), scatter_dimension=0, tiled=True
    ).astype(F32)
    feed_out = lax.psum_scatter(
        dot(hidden, w_contract, ((1,), (1,))).astype(BF16), ("ctx", "tp"), scatter_dimension=0, tiled=True
    ).astype(F32)
    block_output = join((residual + feed_out).astype(BF16)).reshape(rows, length, width)

    feed_weight_grad = jnp.concatenate(
        [
            dot(normed_two, expand_low, ((0,), (0,))).astype(BF16),
            dot(feed_grad, hidden, ((0,), (0,))).astype(BF16),
        ],
        axis=1,
    )
    feed_part = lax.psum_scatter(feed_weight_grad, "fsdp", scatter_dimension=0, tiled=True)
    feed_part = exchange_units(feed_part.reshape(ctx, depth, 3 * share), "ctx")
    feed_part = feed_part.reshape(ctx, depth, 3, share).transpose(1, 2, 0, 3).reshape(depth, 3, ctx * share)
    feed_part = feed_part[:, :, :hidden_units].astype(F32)

    norm_part, gain_two = rms_back(residual, inverse_two, norm_gains[1], normed_two_grad)
    residual_grad = out_grad + norm_part
    branch_grad = join(residual_grad.astype(BF16))
    outlet_grad = dot(branch_grad, recurrent, ((0,), (0,))).astype(BF16)
    rec_grad = dot(branch_grad, w_outlet, ((1,), (0,))).reshape(rows, length, units)
    gelu_grad, tprod, tsum = recurrent_adjoint(rec_grad, gelu_in, coef, prod, total, state_in)
    heads = jnp.stack([coef[:, 0] * tprod[:, 0], coef[:, 0] * tsum[:, 0]])
    leaving = jnp.zeros((rows, units), F32)
    for by in range(ctx - 1, 0, -1):
        head = shifted(heads, "ctx", -by)
        leaving = head[1] + head[0] * leaving
    leaving = jnp.broadcast_to(leaving[:, None], (rows, 8, units))
    branch_x, before, small, blocks_grad = recurrent_backward(
        tprod, tsum, leaving, prod, total, state_in, coef, r, i, conv_low, x_branch, halo, masks, params, blocks
    )
    from_next = shifted(before[:, 5:], "ctx", -1)
    branch_x = branch_x + jnp.pad(from_next, ((0, 0), (length - 3, 0), (0, 0)))
    intake_low = jnp.concatenate([gelu_grad, branch_x.astype(BF16)], axis=2).reshape(tokens, 2 * units)

    sent = swap(dot(other(intake_low), w_intake, ((1,), (1,))), "tp")
    normed_grad = dot(own(intake_low), w_intake, ((1,), (1,))) + sent
    norm_part, gain_one = rms_back(own(x), own(inverse_one), norm_gains[0], normed_grad)
    input_grad = join(residual_grad + norm_part).reshape(rows, length, width)

    intake_grad = dot(normed, intake_low, ((0,), (0,))).astype(BF16)

    def scatter(grad):
        part = lax.psum_scatter(grad, "fsdp", scatter_dimension=0, tiled=True)
        return lax.psum_scatter(part, "ctx", scatter_dimension=0, tiled=True).astype(F32)

    outlet_part = scatter(outlet_grad)
    blocks_part = scatter(blocks_grad.transpose(1, 0, 2).reshape(HEAD_W, 2 * units)).reshape(-1, 2, units)
    intake_part = scatter(intake_grad).reshape(depth, 2, units)

    gains = jnp.stack([gain_one, gain_two])
    gains, small = lax.psum((gains, small), ("fsdp", "ctx"))
    gains = lax.psum(gains, "tp")
    return (
        block_output,
        input_grad,
        gains,
        small[0:4],
        small[4],
        small[5:7],
        small[7],
        intake_part,
        blocks_part,
        outlet_part,
        feed_part[:, :2],
        feed_part[:, 2],
    )


def solution(mesh):
    placed = (
        P("fsdp", "ctx", None),
        P("fsdp", "ctx"),
        P("fsdp", "ctx"),
        P("fsdp", "ctx", None),
        P(),
        P(None, "tp"),
        P("tp"),
        P(None, "tp"),
        P("tp"),
        P(("fsdp", "ctx"), None, "tp"),
        P(("fsdp", "ctx"), None, "tp"),
        P(("fsdp", "ctx"), "tp"),
        P(("fsdp", "ctx"), None, "tp"),
        P(("fsdp", "ctx"), "tp"),
    )
    return jax.shard_map(
        shards,
        mesh=mesh,
        in_specs=placed,
        out_specs=(
            P("fsdp", "ctx", None),
            P("fsdp", "ctx", None),
            P(),
            P(None, "tp"),
            P("tp"),
            P(None, "tp"),
            P("tp"),
            P(("fsdp", "ctx"), None, "tp"),
            P(("fsdp", "ctx"), None, "tp"),
            P(("fsdp", "ctx"), "tp"),
            P(("fsdp", "ctx"), None, "tp"),
            P(("fsdp", "ctx"), "tp"),
        ),
        check_vma=False,
    )
```

```python
import jax
import jax.numpy as jnp
from jax import lax
from jax.experimental import pallas as pl
from jax.experimental.pallas import tpu as pltpu
from jax.sharding import PartitionSpec as P

HEAD_W = 256
LANES = 128
CHUNKS = 8

EPSILON = 1e-06
DECAY_SCALE = 8.0
GELU_C = 0.7978845608028654
GELU_A = 0.044715

F32 = jnp.float32
BF16 = jnp.bfloat16

TAP0, OFFSET, RATE_OFF, INLET_OFF, SOFTPLUS, NEG_SIG, PARAM_ROWS = 0, 4, 5, 6, 7, 8, 16


def shifted(x, axis, by):
    length = lax.axis_size(axis)
    pairs = [(i, i + by) for i in range(length) if 0 <= i + by < length]
    return lax.ppermute(x, axis, pairs)


def swap(x, axis):
    length = lax.axis_size(axis)
    return lax.ppermute(x, axis, [(i, (i + 1) % length) for i in range(length)])


def gelu_pair(v):
    t = jnp.tanh(GELU_C * (v + GELU_A * v * v * v))
    value = 0.5 * v * (1.0 + t)
    slope = 0.5 * (1.0 + t) + 0.5 * v * (1.0 - t * t) * GELU_C * (1.0 + 3.0 * GELU_A * v * v)
    return value, slope


def one_minus_exp(x):
    s = 1.0 + x / 7.0
    for n in (6.0, 5.0, 4.0, 3.0, 2.0):
        s = 1.0 + x / n * s
    return jnp.where(x > -0.5, -x * s, 1.0 - jnp.exp(x))


def sigmoid(v):
    return 1.0 / (1.0 + jnp.exp(-v))


def dot(a, b, dims):
    return lax.dot_general(a, b, (dims, ((), ())), preferred_element_type=F32)


def lane_scan(load_a, load_b, store, length, reverse):
    steps = length // CHUNKS
    prod = jnp.ones((CHUNKS, LANES), F32)
    total = jnp.zeros((CHUNKS, LANES), F32)
    for n in range(steps):
        s = steps - 1 - n if reverse else n
        coef = load_a(s)
        total = coef * total + load_b(s)
        prod = coef * prod
        store(s, prod, total)
    return prod, total


def chunk_carries(prod, total, reverse):
    order = range(CHUNKS - 1, -1, -1) if reverse else range(CHUNKS)
    run_p = jnp.ones((1, LANES), F32)
    run_s = jnp.zeros((1, LANES), F32)
    carries = [None] * CHUNKS
    for c in order:
        carries[c] = (run_p, run_s)
        run_s = prod[c : c + 1] * run_s + total[c : c + 1]
        run_p = prod[c : c + 1] * run_p
    return carries


def sweep(a_scr, b_scr, p_scr, s_scr, prod_ref, sum_ref, rows, length, reverse, shift):
    steps = length // CHUNKS
    for b in range(rows):
        for j in range(HEAD_W // LANES):
            av, bv, pv, sv = (a_scr.at[b, j], b_scr.at[b, j], p_scr.at[b, j], s_scr.at[b, j])

            def store(s, prod, total):
                pv[pl.ds(s, CHUNKS, stride=steps), :] = prod
                sv[pl.ds(s, CHUNKS, stride=steps), :] = total

            prod, total = lane_scan(
                lambda s: av[pl.ds(s + shift, CHUNKS, stride=steps), :],
                lambda s: bv[pl.ds(s, CHUNKS, stride=steps), :],
                store,
                length,
                reverse,
            )
            carries = chunk_carries(prod, total, reverse)
            lanes = slice(j * LANES, (j + 1) * LANES)
            for c in range(CHUNKS):
                here = slice(c * steps, (c + 1) * steps)
                p = pv[here, :]
                prod_ref[b, here, lanes] = p * carries[c][0]
                sum_ref[b, here, lanes] = sv[here, :] + p * carries[c][1]


def to_lanes(ref, b, at, value):
    for j in range(HEAD_W // LANES):
        ref[b, j, pl.ds(at, value.shape[0]), :] = value[:, j * LANES : (j + 1) * LANES]


def forward_kernel(
    x_ref, halo_ref, mask_ref, par_ref, w_ref,
    conv_ref, r_ref, i_ref, a_ref, prod_ref, sum_ref,
    ext, a_scr, b_scr, p_scr, s_scr,
):
    rows, length, _ = x_ref.shape
    par = par_ref[...]
    w0, w1 = w_ref[0], w_ref[1]
    for b in range(rows):
        ext[b, pl.ds(0, 8), :] = halo_ref[b]
        ext[b, pl.ds(8, length), :] = x_ref[b].astype(F32)
        conv = ext[b, pl.ds(8, length), :] * par[TAP0 : TAP0 + 1] + par[OFFSET : OFFSET + 1]
        for k in range(1, 4):
            match = mask_ref[b, :, k : k + 1]
            conv = conv + par[TAP0 + k : TAP0 + k + 1] * ext[b, pl.ds(8 - k, length), :] * match
        conv_low = conv.astype(BF16)
        conv_ref[b] = conv_low
        conv = conv_low.astype(F32)
        r = sigmoid(dot(conv_low, w0, ((1,), (0,))) + par[RATE_OFF : RATE_OFF + 1])
        i = sigmoid(dot(conv_low, w1, ((1,), (0,))) + par[INLET_OFF : INLET_OFF + 1])
        r_ref[b] = r
        i_ref[b] = i
        log_keep = -DECAY_SCALE * r * par[SOFTPLUS : SOFTPLUS + 1]
        going = mask_ref[b, :, 0:1]
        a = jnp.exp(log_keep) * going
        a_ref[b] = a
        scale = jnp.where(going > 0.5, jnp.sqrt(one_minus_exp(2.0 * log_keep)), 1.0)
        to_lanes(a_scr, b, 0, a)
        to_lanes(b_scr, b, 0, i * conv * scale)
    sweep(a_scr, b_scr, p_scr, s_scr, prod_ref, sum_ref, rows, length, False, 0)


def head_spec(rows, length):
    return pl.BlockSpec((rows, length, HEAD_W), lambda h: (0, 0, h))


def recurrent_forward(x_branch, halo, masks, params, blocks):
    rows, length, units = x_branch.shape
    full = head_spec(rows, length)
    scan = pltpu.VMEM((rows, HEAD_W // LANES, length, LANES), F32)
    big = jax.ShapeDtypeStruct((rows, length, units), F32)
    return pl.pallas_call(
        forward_kernel,
        grid=(units // HEAD_W,),
        in_specs=[
            full,
            head_spec(rows, 8),
            pl.BlockSpec((rows, length, 8), lambda h: (0, 0, 0)),
            pl.BlockSpec((PARAM_ROWS, HEAD_W), lambda h: (0, h)),
            pl.BlockSpec((2, HEAD_W, HEAD_W), lambda h: (0, 0, h)),
        ],
        out_specs=[full] * 6,
        out_shape=[jax.ShapeDtypeStruct((rows, length, units), BF16)] + [big] * 5,
        scratch_shapes=[pltpu.VMEM((rows, length + 8, HEAD_W), F32), scan, scan, scan, scan],
        compiler_params=pltpu.CompilerParams(vmem_limit_bytes=48 * 1024 * 1024),
        cost_estimate=pl.CostEstimate(
            flops=4 * rows * length * units * HEAD_W,
            bytes_accessed=24 * rows * length * units,
            transcendentals=8 * rows * length * units,
        ),
        name="recurrent_forward",
    )(x_branch, halo, masks, params, blocks)


def adjoint_kernel(
    rg_ref, gelu_ref, a_ref, prod_ref, sum_ref, in_ref,
    gg_ref, tprod_ref, tsum_ref,
    a_scr, b_scr, p_scr, s_scr,
):
    rows, length, _ = rg_ref.shape
    for b in range(rows):
        states = sum_ref[b] + prod_ref[b] * in_ref[b, 0:1]
        value, slope = gelu_pair(gelu_ref[b])
        rg = rg_ref[b]
        gg_ref[b] = (rg * states * slope).astype(BF16)
        to_lanes(a_scr, b, 0, a_ref[b])
        to_lanes(a_scr, b, length, jnp.ones((8, HEAD_W), F32))
        to_lanes(b_scr, b, 0, rg * value)
    sweep(a_scr, b_scr, p_scr, s_scr, tprod_ref, tsum_ref, rows, length, True, 1)


def recurrent_adjoint(rec_grad, gelu_in, coef, prod, total, state_in):
    rows, length, units = rec_grad.shape
    full = head_spec(rows, length)
    scan = pltpu.VMEM((rows, HEAD_W // LANES, length, LANES), F32)
    longer = pltpu.VMEM((rows, HEAD_W // LANES, length + 8, LANES), F32)
    big = jax.ShapeDtypeStruct((rows, length, units), F32)
    return pl.pallas_call(
        adjoint_kernel,
        grid=(units // HEAD_W,),
        in_specs=[full] * 5 + [head_spec(rows, 8)],
        out_specs=[full] * 3,
        out_shape=[jax.ShapeDtypeStruct((rows, length, units), BF16), big, big],
        scratch_shapes=[longer, scan, scan, scan],
        compiler_params=pltpu.CompilerParams(vmem_limit_bytes=48 * 1024 * 1024),
        cost_estimate=pl.CostEstimate(
            flops=30 * rows * length * units,
            bytes_accessed=32 * rows * length * units,
            transcendentals=rows * length * units,
        ),
        name="recurrent_adjoint",
    )(rec_grad, gelu_in, coef, prod, total, state_in)


def backward_kernel(
    tprod_ref, tsum_ref, leave_ref, prod_ref, sum_ref, in_ref, a_ref, r_ref, i_ref, conv_ref,
    x_ref, halo_ref, mask_ref, par_ref, w_ref,
    bx_ref, before_ref, small_ref, blocks_ref,
    ext, st_ext, g_ext,
):
    rows, length, _ = tprod_ref.shape
    par = par_ref[...]
    w0, w1 = w_ref[0], w_ref[1]
    sums = [jnp.zeros((1, HEAD_W), F32) for _ in range(8)]
    blocks = [jnp.zeros((HEAD_W, HEAD_W), F32) for _ in range(2)]

    def add(n, value):
        sums[n] = sums[n] + jnp.sum(value, axis=0, keepdims=True)

    for b in range(rows):
        adjoint = tsum_ref[b] + tprod_ref[b] * leave_ref[b, 0:1]
        st_ext[b, pl.ds(0, 8), :] = in_ref[b]
        st_ext[b, pl.ds(8, length), :] = sum_ref[b] + prod_ref[b] * in_ref[b, 0:1]
        prev = st_ext[b, pl.ds(7, length), :]
        r, i, a = r_ref[b], i_ref[b], a_ref[b]
        conv_low = conv_ref[b]
        conv = conv_low.astype(F32)
        going = mask_ref[b, :, 0:1]
        log_keep = -DECAY_SCALE * r * par[SOFTPLUS : SOFTPLUS + 1]
        scale = jnp.where(going > 0.5, jnp.sqrt(one_minus_exp(2.0 * log_keep)), 1.0)
        log_grad = adjoint * prev * a - adjoint * i * conv * (a * a) / scale
        rate = log_grad * (-DECAY_SCALE * par[SOFTPLUS : SOFTPLUS + 1]) * r * (1.0 - r)
        spread = adjoint * scale
        inlet = spread * conv * i * (1.0 - i)
        add(5, rate)
        add(6, inlet)
        add(7, log_grad * r)
        rate_low = rate.astype(BF16)
        inlet_low = inlet.astype(BF16)
        grad = spread * i + dot(rate_low, w0, ((1,), (1,))) + dot(inlet_low, w1, ((1,), (1,)))
        blocks[0] = blocks[0] + dot(conv_low, rate_low, ((0,), (0,)))
        blocks[1] = blocks[1] + dot(conv_low, inlet_low, ((0,), (0,)))
        ext[b, pl.ds(0, 8), :] = halo_ref[b]
        ext[b, pl.ds(8, length), :] = x_ref[b].astype(F32)
        add(4, grad)
        add(0, grad * ext[b, pl.ds(8, length), :])
        bx = grad * par[TAP0 : TAP0 + 1]
        g_ext[b, pl.ds(0, 8), :] = jnp.zeros((8, HEAD_W), F32)
        g_ext[b, pl.ds(8 + length, 8), :] = jnp.zeros((8, HEAD_W), F32)
        before = jnp.zeros((8, HEAD_W), F32)
        for k in range(1, 4):
            masked = grad * mask_ref[b, :, k : k + 1]
            add(k, masked * ext[b, pl.ds(8 - k, length), :])
            g_ext[b, pl.ds(8, length), :] = masked
            tap = par[TAP0 + k : TAP0 + k + 1]
            bx = bx + tap * g_ext[b, pl.ds(8 + k, length), :]
            before = before + tap * g_ext[b, pl.ds(k, 8), :]
        bx_ref[b] = bx
        before_ref[b] = before
    sums[7] = sums[7] * (DECAY_SCALE * par[NEG_SIG : NEG_SIG + 1])
    for n in range(8):
        small_ref[pl.ds(n, 1), :] = sums[n]
    blocks_ref[0] = blocks[0].astype(blocks_ref.dtype)
    blocks_ref[1] = blocks[1].astype(blocks_ref.dtype)


def recurrent_backward(tprod, tsum, leaving, prod, total, state_in, coef, r, i, conv_low, x_branch, halo, masks, params, blocks):
    rows, length, units = tprod.shape
    full = head_spec(rows, length)
    edge = head_spec(rows, 8)
    return pl.pallas_call(
        backward_kernel,
        grid=(units // HEAD_W,),
        in_specs=[
            full, full, edge, full, full, edge, full, full, full, full, full, edge,
            pl.BlockSpec((rows, length, 8), lambda h: (0, 0, 0)),
            pl.BlockSpec((PARAM_ROWS, HEAD_W), lambda h: (0, h)),
            pl.BlockSpec((2, HEAD_W, HEAD_W), lambda h: (0, 0, h)),
        ],
        out_specs=[
            full,
            edge,
            pl.BlockSpec((8, HEAD_W), lambda h: (0, h)),
            pl.BlockSpec((2, HEAD_W, HEAD_W), lambda h: (0, 0, h)),
        ],
        out_shape=[
            jax.ShapeDtypeStruct((rows, length, units), F32),
            jax.ShapeDtypeStruct((rows, 8, units), F32),
            jax.ShapeDtypeStruct((8, units), F32),
            jax.ShapeDtypeStruct((2, HEAD_W, units), BF16),
        ],
        scratch_shapes=[
            pltpu.VMEM((rows, length + 8, HEAD_W), F32),
            pltpu.VMEM((rows, length + 8, HEAD_W), F32),
            pltpu.VMEM((rows, length + 16, HEAD_W), F32),
        ],
        compiler_params=pltpu.CompilerParams(vmem_limit_bytes=48 * 1024 * 1024),
        cost_estimate=pl.CostEstimate(
            flops=8 * rows * length * units * HEAD_W,
            bytes_accessed=40 * rows * length * units,
            transcendentals=4 * rows * length * units,
        ),
        name="recurrent_backward",
    )(tprod, tsum, leaving, prod, total, state_in, coef, r, i, conv_low, x_branch, halo, masks, params, blocks)


TILE = 256


def tokens_spec(columns, tiles, first):
    return pl.BlockSpec((TILE, columns), lambda m: ((m + first) % tiles, 0))


def held(rows, columns):
    return pl.BlockSpec((rows, columns), lambda m: (0, 0), pipeline_mode=pl.Buffered(1))


def half_specs(columns, tiles):
    mid = tiles // 2
    return [
        pl.BlockSpec((TILE, columns), lambda m: (jnp.maximum(m - mid, 0), 0)),
        pl.BlockSpec((TILE, columns), lambda m: (jnp.minimum(m, mid - 1), 0)),
    ]


def store_half(first_ref, second_ref, tiles, value):
    m = pl.program_id(0)

    @pl.when(m < tiles // 2)
    def _():
        second_ref[...] = value

    @pl.when(m >= tiles // 2)
    def _():
        first_ref[...] = value


def feed_params():
    return pltpu.CompilerParams(vmem_limit_bytes=56 * 1024 * 1024)


def cost(flops, size):
    return pl.CostEstimate(flops=flops, bytes_accessed=size, transcendentals=0)


def forward_tile(x_ref, w_ref, hidden_ref, by_gate_ref, by_up_ref):
    share = hidden_ref.shape[1]
    x = x_ref[...]
    value, slope = gelu_pair(dot(x, w_ref[:, :share], ((1,), (0,))))
    up = dot(x, w_ref[:, share:], ((1,), (0,)))
    hidden_ref[...] = (value * up).astype(BF16)
    by_gate_ref[...] = up * slope
    by_up_ref[...] = value


def feed_forward(x, w_expand):
    count, width = x.shape
    share = w_expand.shape[1] // 2
    tiles = count // TILE
    tile = tokens_spec(share, tiles, 0)
    return pl.pallas_call(
        forward_tile,
        grid=(tiles,),
        in_specs=[tokens_spec(width, tiles, 0), held(width, 2 * share)],
        out_specs=[tile] * 3,
        out_shape=[
            jax.ShapeDtypeStruct((count, share), BF16),
            jax.ShapeDtypeStruct((count, share), F32),
            jax.ShapeDtypeStruct((count, share), F32),
        ],
        compiler_params=feed_params(),
        cost_estimate=cost(4 * count * width * share, 10 * count * share + 2 * count * width),
        name="feed_forward",
    )(x, w_expand)


def feed_backward(feed_grad, by_gate, by_up, w_down, w_expand):
    count, width = feed_grad.shape
    share = w_down.shape[1]
    tiles = count // TILE
    mid = tiles // 2

    def body(fg_ref, gate_ref, up_ref, wd_ref, we_ref, low_ref, first_ref, second_ref):
        grad = dot(fg_ref[...], wd_ref[...], ((1,), (0,)))
        gate = (grad * gate_ref[...]).astype(BF16)
        up = (grad * up_ref[...]).astype(BF16)
        low_ref[:, :share] = gate
        low_ref[:, share:] = up
        terms = dot(gate, we_ref[:, :share], ((1,), (1,))) + dot(up, we_ref[:, share:], ((1,), (1,)))
        store_half(first_ref, second_ref, tiles, terms.astype(BF16))

    tile = tokens_spec(share, tiles, mid)
    return pl.pallas_call(
        body,
        grid=(tiles,),
        in_specs=[tokens_spec(width, tiles, mid), tile, tile, held(width, share), held(width, 2 * share)],
        out_specs=[tokens_spec(2 * share, tiles, mid)] + half_specs(width, tiles),
        out_shape=[
            jax.ShapeDtypeStruct((count, 2 * share), BF16),
            jax.ShapeDtypeStruct((count // 2, width), BF16),
            jax.ShapeDtypeStruct((count // 2, width), BF16),
        ],
        compiler_params=feed_params(),
        cost_estimate=cost(6 * count * width * share, 12 * count * share + 4 * count * width),
        name="feed_backward",
    )(feed_grad, by_gate, by_up, w_down, w_expand)


def feed_down(hidden, w_down):
    count, share = hidden.shape
    width = w_down.shape[0]
    tiles = count // TILE

    def body(h_ref, w_ref, first_ref, second_ref):
        store_half(first_ref, second_ref, tiles, dot(h_ref[...], w_ref[...], ((1,), (1,))).astype(BF16))

    return pl.pallas_call(
        body,
        grid=(tiles,),
        in_specs=[tokens_spec(share, tiles, tiles // 2), held(width, share)],
        out_specs=half_specs(width, tiles),
        out_shape=[jax.ShapeDtypeStruct((count // 2, width), BF16)] * 2,
        compiler_params=feed_params(),
        cost_estimate=cost(2 * count * width * share, 2 * count * share + 2 * count * width),
        name="feed_down",
    )(hidden, w_down)


def weight_grad(x, grad):
    count, width = x.shape
    columns = grad.shape[1]
    deep, wide = 512, min(columns, 1024)

    def body(x_ref, g_ref, out_ref):
        out_ref[...] = dot(x_ref[...], g_ref[...], ((0,), (0,))).astype(BF16)

    return pl.pallas_call(
        body,
        grid=(columns // wide, width // deep),
        in_specs=[
            pl.BlockSpec((count, deep), lambda n, m: (0, m)),
            pl.BlockSpec((count, wide), lambda n, m: (0, n)),
        ],
        out_specs=pl.BlockSpec((deep, wide), lambda n, m: (m, n)),
        out_shape=jax.ShapeDtypeStruct((width, columns), BF16),
        compiler_params=feed_params(),
        cost_estimate=cost(2 * count * width * columns, 2 * (count * width + count * columns + width * columns)),
        name="weight_grad",
    )(x, grad)


def cross(x, axis, r):
    return lax.ppermute(x, axis, [(i, i ^ r) for i in range(lax.axis_size(axis))])


def total_over(x, axis):
    r = 1
    while r < lax.axis_size(axis):
        x = x + cross(x, axis, r)
        r *= 2
    return x


def after(x, done):
    return lax.optimization_barrier((x, done))


SQUARE = 4


def token_axes():
    return ("fsdp", "ctx") if lax.axis_size("fsdp") == SQUARE else ("ctx", "fsdp")


def place(blocks, axis):
    me = lax.axis_index(axis)
    whole = jnp.zeros((len(blocks),) + blocks[0].shape, blocks[0].dtype)
    for r, block in enumerate(blocks):
        whole = lax.dynamic_update_index_in_dim(whole, block, me ^ r, 0)
    return whole


def near(x, axis):
    mid = x.shape[0] // 2
    one, two = cross(x, axis, 1), cross(x, axis, 2)
    three = jnp.concatenate([cross(one[:mid], axis, 2), cross(two[mid:], axis, 1)], axis=0)
    return [x, one, two, three]


def near_sum(block, axis):
    low = lambda v: v.astype(BF16)
    wide = lambda v: v.astype(F32)
    a1, a3 = cross(low(block(1, 0)), axis, 1), cross(low(block(3, 0)), axis, 1)
    b2, b3 = cross(low(block(2, 1)), axis, 2), cross(low(block(3, 1)), axis, 2)
    a2 = cross(low(wide(block(2, 0)) + wide(a3)), axis, 2)
    b1 = cross(low(wide(block(1, 1)) + wide(b3)), axis, 1)
    left = wide(block(0, 0)) + wide(a1) + wide(a2)
    right = wide(block(0, 1)) + wide(b2) + wide(b1)
    return jnp.concatenate([left, right], axis=1)


def gather_rows(x):
    if lax.axis_size("fsdp") != SQUARE:
        return lax.all_gather(x, "fsdp", axis=0, tiled=True)
    return place(near(x, "fsdp"), "fsdp").reshape(SQUARE * x.shape[0], x.shape[1])


def scatter_rows(x):
    if lax.axis_size("fsdp") != SQUARE:
        return lax.psum_scatter(x, "fsdp", scatter_dimension=0, tiled=True).astype(F32)
    me, rows, cols = lax.axis_index("fsdp"), x.shape[0] // SQUARE, x.shape[1] // 2
    return near_sum(lambda r, h: lax.dynamic_slice(x, ((me ^ r) * rows, h * cols), (rows, cols)), "fsdp")


def gather_tokens(x):
    blocks = near(x, token_axes()[0])
    return jnp.concatenate(blocks + [swap(block, "tp") for block in blocks], axis=0)


def scatter_tokens(first, second):
    theirs = swap(second, "tp")
    mine = (first.astype(F32) + theirs.astype(F32)).astype(BF16)
    rows, cols = mine.shape[0] // SQUARE, mine.shape[1] // 2
    return near_sum(lambda r, h: mine[r * rows : (r + 1) * rows, h * cols : (h + 1) * cols], token_axes()[0])


def trade(pieces):
    axis = token_axes()[0]
    me = lax.axis_index(axis)
    return place([pieces(me)] + [cross(pieces(me ^ r), axis, r) for r in range(1, SQUARE)], axis)


def gather_feed(local):
    _, along = token_axes()
    whole = lax.all_gather(local, along, axis=1 if along == "ctx" else 0, tiled=True)
    return whole.reshape(-1, local.shape[2])


def scatter_feed(grad):
    _, along = token_axes()
    if along == "ctx":
        grad = grad.reshape(SQUARE, -1, grad.shape[1])
        return lax.psum_scatter(grad, along, scatter_dimension=1, tiled=True)
    part = lax.psum_scatter(grad, along, scatter_dimension=0, tiled=True)
    return part.reshape(SQUARE, -1, grad.shape[1])


def rms(values):
    return lax.rsqrt(jnp.mean(values * values, axis=-1, keepdims=True) + EPSILON)


def rms_back(values, inverse, gain, grad):
    u = grad * gain
    inner = jnp.mean(values * u, axis=-1, keepdims=True)
    gain_grad = jnp.sum(grad * values * inverse, axis=0)
    return inverse * u - values * (inverse * inverse * inverse) * inner, gain_grad


def shards(
    block_input, segments, token_mask, cotangent, norm_gains, conv_taps, conv_offset, gate_offset,
    decay_logit, intake, gate_blocks, outlet, expand, contract,
):
    rows, length, width = block_input.shape
    depth = intake.shape[0]
    units = intake.shape[2]
    gate_rows = gate_blocks.shape[0]
    hidden_units = contract.shape[1]
    tokens = rows * length
    ctx, tp = lax.axis_size("ctx"), lax.axis_size("tp")
    mine = lax.axis_index("tp")
    half = tokens // tp
    share = -(-hidden_units // (SQUARE * 256)) * 256
    padding = SQUARE * share - hidden_units

    def own(x):
        return lax.dynamic_slice_in_dim(x, mine * half, half, 0)

    def other(x):
        return lax.dynamic_slice_in_dim(x, (1 - mine) * half, half, 0)

    def join(x):
        theirs = swap(x, "tp")
        return jnp.concatenate(
            [jnp.where(mine == 0, x, theirs), jnp.where(mine == 0, theirs, x)], axis=0
        )

    packed = jnp.concatenate(
        [intake[:, 1], intake[:, 0], outlet, gate_blocks.reshape(2 * gate_rows, units)], axis=0
    )
    packed = lax.all_gather(packed, "ctx", axis=0)

    def part(n, count):
        return packed[:, n * depth : n * depth + count].reshape(ctx * count, units)

    def cut(w):
        w = jnp.pad(w, ((0, 0), (0, padding)))
        return lambda p: lax.dynamic_slice_in_dim(w, p * share, share, 1)

    down, gate_in, up_in = cut(contract), cut(expand[:, 0]), cut(expand[:, 1])
    w_expand = trade(lambda p: jnp.concatenate([gate_in(p), up_in(p)], axis=1))
    w_expand = gather_feed(w_expand)
    local_down = trade(down)

    mask_rows = token_mask.astype(F32).reshape(tokens, 1)
    out_grad = own(cotangent.reshape(tokens, width)).astype(F32) * own(mask_rows)
    feed_grad = gather_tokens(out_grad.astype(BF16))

    local_branch, local_down, feed_grad = lax.optimization_barrier((part(0, depth), local_down, feed_grad))
    w_down = gather_feed(local_down)
    w_branch = gather_rows(local_branch)
    local_gates, w_branch = after(part(3, 2 * gate_rows), w_branch)
    w_gates = gather_rows(local_gates)
    local_gelu, w_gates = after(part(1, depth), w_gates)
    blocks = w_gates.reshape(HEAD_W, 2, units).transpose(1, 0, 2)
    w_gelu = gather_rows(local_gelu)
    local_outlet, w_gelu = after(part(2, depth), w_gelu)
    w_outlet = gather_rows(local_outlet)

    seg_next = segments + 1
    seg_before = shifted(seg_next[:, -3:], "ctx", 1)
    seg_ext = jnp.concatenate([seg_before, seg_next], axis=1)
    masks = jnp.stack(
        [(seg_ext[:, 3 - k : 3 - k + length] == seg_next).astype(F32) for k in (1, 1, 2, 3)]
        + [jnp.zeros(segments.shape, F32)] * 4,
        axis=2,
    )
    params = jnp.concatenate(
        [
            conv_taps,
            conv_offset[None],
            gate_offset,
            jax.nn.softplus(-decay_logit)[None],
            jax.nn.sigmoid(-decay_logit)[None],
            jnp.zeros((PARAM_ROWS - 9, units), F32),
        ],
        axis=0,
    )

    x = block_input.reshape(tokens, width).astype(F32)
    inverse_one = rms(x)
    normed = (x * inverse_one * norm_gains[0]).astype(BF16)
    x_branch = dot(normed, w_branch, ((1,), (0,))).astype(BF16).reshape(rows, length, units)
    gelu_in = dot(normed, w_gelu, ((1,), (0,))).reshape(rows, length, units)
    x_before = shifted(x_branch[:, -3:], "ctx", 1)
    halo = jnp.pad(x_before, ((0, 0), (5, 0), (0, 0))).astype(F32)
    conv_low, r, i, coef, prod, total = recurrent_forward(x_branch, halo, masks, params, blocks)
    ends = jnp.stack([prod[:, -1], total[:, -1]])
    entering = jnp.zeros((rows, units), F32)
    for by in range(ctx - 1, 0, -1):
        end = shifted(ends, "ctx", by)
        entering = end[1] + end[0] * entering
    state_in = jnp.broadcast_to(entering[:, None], (rows, 8, units))
    states = total + prod * entering[:, None]
    recurrent = (states * jax.nn.gelu(gelu_in, approximate=True)).astype(BF16).reshape(tokens, units)

    sent = swap(dot(other(recurrent), w_outlet, ((1,), (1,))), "tp")
    branch = dot(own(recurrent), w_outlet, ((1,), (1,))) + sent
    residual = own(x) + branch
    inverse_two = rms(residual)
    normed_two = gather_tokens((residual * inverse_two * norm_gains[1]).astype(BF16))

    def to_owners(part):
        return trade(lambda p: lax.dynamic_index_in_dim(part, p, 0, keepdims=False))

    hidden, by_gate, by_up = feed_forward(normed_two, w_expand)
    down_part = scatter_feed(weight_grad(feed_grad, hidden))
    low, n2g_own, n2g_other = feed_backward(feed_grad, by_gate, by_up, w_down, w_expand)
    normed_two_grad = scatter_tokens(n2g_own, n2g_other)
    expand_all = weight_grad(normed_two, low)
    feed_own, feed_other = feed_down(hidden, w_down)
    normed_two_grad, expand_all, feed_own, feed_other = lax.optimization_barrier(
        (normed_two_grad, expand_all, feed_own, feed_other)
    )
    expand_part = scatter_feed(expand_all)
    feed_out = scatter_tokens(feed_own, feed_other)
    block_output = join((residual + feed_out).astype(BF16)).reshape(rows, length, width)

    norm_part, gain_two = rms_back(residual, inverse_two, norm_gains[1], normed_two_grad)
    residual_grad = out_grad + norm_part
    branch_grad = join(residual_grad.astype(BF16))

    outlet_grad = dot(branch_grad, recurrent, ((0,), (0,))).astype(BF16)
    rec_grad = dot(branch_grad, w_outlet, ((1,), (0,))).reshape(rows, length, units)
    gelu_grad, tprod, tsum = recurrent_adjoint(rec_grad, gelu_in, coef, prod, total, state_in)
    heads = jnp.stack([coef[:, 0] * tprod[:, 0], coef[:, 0] * tsum[:, 0]])
    leaving = jnp.zeros((rows, units), F32)
    for by in range(ctx - 1, 0, -1):
        head = shifted(heads, "ctx", -by)
        leaving = head[1] + head[0] * leaving
    leaving = jnp.broadcast_to(leaving[:, None], (rows, 8, units))
    branch_x, before, small, blocks_grad = recurrent_backward(
        tprod, tsum, leaving, prod, total, state_in, coef, r, i, conv_low, x_branch, halo, masks, params, blocks
    )
    from_next = shifted(before[:, 5:], "ctx", -1)
    branch_x = branch_x + jnp.pad(from_next, ((0, 0), (length - 3, 0), (0, 0)))
    gelu_low = gelu_grad.reshape(tokens, units)
    branch_low = branch_x.astype(BF16).reshape(tokens, units)

    def input_terms(pick):
        return dot(pick(branch_low), w_branch, ((1,), (1,))) + dot(pick(gelu_low), w_gelu, ((1,), (1,)))

    gelu_part = scatter_rows(dot(normed, gelu_low, ((0,), (0,))).astype(BF16)).astype(BF16)
    outlet_part = scatter_rows(outlet_grad).astype(BF16)
    branch_part = scatter_rows(dot(normed, branch_low, ((0,), (0,))).astype(BF16)).astype(BF16)
    blocks_part = scatter_rows(blocks_grad.transpose(1, 0, 2).reshape(2 * HEAD_W, units)).astype(BF16)

    def scatter_ctx(parts):
        parts = jnp.concatenate([p.reshape(ctx, -1, units) for p in parts], axis=1)
        return lax.psum_scatter(parts, "ctx", scatter_dimension=0, tiled=False).astype(F32)

    gelu_part, expand_part = after(gelu_part, expand_part)
    early = scatter_ctx([gelu_part, outlet_part])
    branch_part, early = after(branch_part, early)
    late = scatter_ctx([branch_part, blocks_part])

    down_part = to_owners(down_part)
    expand_part = to_owners(expand_part)

    def columns(part, n):
        return jnp.concatenate([part[p, :, n * share : (n + 1) * share] for p in range(SQUARE)], axis=1)[
            :, :hidden_units
        ].astype(F32)

    contract_grad = columns(down_part, 0)
    expand_grad = jnp.stack([columns(expand_part, 0), columns(expand_part, 1)], axis=1)

    sent = swap(input_terms(other), "tp")
    normed_grad = input_terms(own) + sent
    norm_part, gain_one = rms_back(own(x), own(inverse_one), norm_gains[0], normed_grad)
    input_grad = join(residual_grad + norm_part).reshape(rows, length, width)

    gains = jnp.concatenate([gain_one, gain_two]).reshape(-1, units)
    small = total_over(total_over(jnp.concatenate([small, gains], axis=0), "fsdp"), "ctx")
    gains = total_over(small[8:], "tp").reshape(2, width)
    return (
        block_output,
        input_grad,
        gains,
        small[0:4],
        small[4],
        small[5:7],
        small[7],
        jnp.stack([early[:depth], late[:depth]], axis=1),
        late[depth:].reshape(gate_rows, 2, units),
        early[depth:],
        expand_grad,
        contract_grad,
    )


def solution(mesh):
    placed = (
        P("fsdp", "ctx", None),
        P("fsdp", "ctx"),
        P("fsdp", "ctx"),
        P("fsdp", "ctx", None),
        P(),
        P(None, "tp"),
        P("tp"),
        P(None, "tp"),
        P("tp"),
        P(("fsdp", "ctx"), None, "tp"),
        P(("fsdp", "ctx"), None, "tp"),
        P(("fsdp", "ctx"), "tp"),
        P(("fsdp", "ctx"), None, "tp"),
        P(("fsdp", "ctx"), "tp"),
    )
    return jax.shard_map(
        shards,
        mesh=mesh,
        in_specs=placed,
        out_specs=(
            P("fsdp", "ctx", None),
            P("fsdp", "ctx", None),
            P(),
            P(None, "tp"),
            P("tp"),
            P(None, "tp"),
            P("tp"),
            P(("fsdp", "ctx"), None, "tp"),
            P(("fsdp", "ctx"), None, "tp"),
            P(("fsdp", "ctx"), "tp"),
            P(("fsdp", "ctx"), None, "tp"),
            P(("fsdp", "ctx"), "tp"),
        ),
        check_vma=False,
    )
```

```python
import jax
import jax.numpy as jnp
from jax import lax
from jax.experimental import pallas as pl
from jax.experimental.pallas import tpu as pltpu
from jax.sharding import PartitionSpec as P

HEAD_W = 256
LANES = 128
CHUNKS = 8

EPSILON = 1e-06
DECAY_SCALE = 8.0
GELU_C = 0.7978845608028654
GELU_A = 0.044715

F32 = jnp.float32
BF16 = jnp.bfloat16

TAP0, OFFSET, RATE_OFF, INLET_OFF, SOFTPLUS, NEG_SIG, PARAM_ROWS = 0, 4, 5, 6, 7, 8, 16


def shifted(x, axis, by):
    length = lax.axis_size(axis)
    pairs = [(i, i + by) for i in range(length) if 0 <= i + by < length]
    return lax.ppermute(x, axis, pairs)


def swap(x, axis):
    length = lax.axis_size(axis)
    return lax.ppermute(x, axis, [(i, (i + 1) % length) for i in range(length)])


def gelu_pair(v):
    t = jnp.tanh(GELU_C * (v + GELU_A * v * v * v))
    value = 0.5 * v * (1.0 + t)
    slope = 0.5 * (1.0 + t) + 0.5 * v * (1.0 - t * t) * GELU_C * (1.0 + 3.0 * GELU_A * v * v)
    return value, slope


def one_minus_exp(x):
    s = 1.0 + x / 7.0
    for n in (6.0, 5.0, 4.0, 3.0, 2.0):
        s = 1.0 + x / n * s
    return jnp.where(x > -0.5, -x * s, 1.0 - jnp.exp(x))


def sigmoid(v):
    return 1.0 / (1.0 + jnp.exp(-v))


def dot(a, b, dims):
    return lax.dot_general(a, b, (dims, ((), ())), preferred_element_type=F32)


def lane_scan(load_a, load_b, store, length, reverse):
    steps = length // CHUNKS
    prod = jnp.ones((CHUNKS, LANES), F32)
    total = jnp.zeros((CHUNKS, LANES), F32)
    for n in range(steps):
        s = steps - 1 - n if reverse else n
        coef = load_a(s)
        total = coef * total + load_b(s)
        prod = coef * prod
        store(s, prod, total)
    return prod, total


def chunk_carries(prod, total, reverse):
    order = range(CHUNKS - 1, -1, -1) if reverse else range(CHUNKS)
    run_p = jnp.ones((1, LANES), F32)
    run_s = jnp.zeros((1, LANES), F32)
    carries = [None] * CHUNKS
    for c in order:
        carries[c] = (run_p, run_s)
        run_s = prod[c : c + 1] * run_s + total[c : c + 1]
        run_p = prod[c : c + 1] * run_p
    return carries


def sweep(a_scr, b_scr, p_scr, s_scr, prod_ref, sum_ref, rows, length, reverse, shift):
    steps = length // CHUNKS
    for b in range(rows):
        for j in range(HEAD_W // LANES):
            av, bv, pv, sv = (a_scr.at[b, j], b_scr.at[b, j], p_scr.at[b, j], s_scr.at[b, j])

            def store(s, prod, total):
                pv[pl.ds(s, CHUNKS, stride=steps), :] = prod
                sv[pl.ds(s, CHUNKS, stride=steps), :] = total

            prod, total = lane_scan(
                lambda s: av[pl.ds(s + shift, CHUNKS, stride=steps), :],
                lambda s: bv[pl.ds(s, CHUNKS, stride=steps), :],
                store,
                length,
                reverse,
            )
            carries = chunk_carries(prod, total, reverse)
            lanes = slice(j * LANES, (j + 1) * LANES)
            for c in range(CHUNKS):
                here = slice(c * steps, (c + 1) * steps)
                p = pv[here, :]
                prod_ref[b, here, lanes] = p * carries[c][0]
                sum_ref[b, here, lanes] = sv[here, :] + p * carries[c][1]


def to_lanes(ref, b, at, value):
    for j in range(HEAD_W // LANES):
        ref[b, j, pl.ds(at, value.shape[0]), :] = value[:, j * LANES : (j + 1) * LANES]


def forward_kernel(
    x_ref, halo_ref, mask_ref, par_ref, w_ref,
    conv_ref, r_ref, i_ref, a_ref, prod_ref, sum_ref,
    ext, a_scr, b_scr, p_scr, s_scr,
):
    rows, length, _ = x_ref.shape
    par = par_ref[...]
    w0, w1 = w_ref[0], w_ref[1]
    for b in range(rows):
        ext[b, pl.ds(0, 8), :] = halo_ref[b]
        ext[b, pl.ds(8, length), :] = x_ref[b].astype(F32)
        conv = ext[b, pl.ds(8, length), :] * par[TAP0 : TAP0 + 1] + par[OFFSET : OFFSET + 1]
        for k in range(1, 4):
            match = mask_ref[b, :, k : k + 1]
            conv = conv + par[TAP0 + k : TAP0 + k + 1] * ext[b, pl.ds(8 - k, length), :] * match
        conv_low = conv.astype(BF16)
        conv_ref[b] = conv_low
        conv = conv_low.astype(F32)
        r = sigmoid(dot(conv_low, w0, ((1,), (0,))) + par[RATE_OFF : RATE_OFF + 1])
        i = sigmoid(dot(conv_low, w1, ((1,), (0,))) + par[INLET_OFF : INLET_OFF + 1])
        r_ref[b] = r
        i_ref[b] = i
        log_keep = -DECAY_SCALE * r * par[SOFTPLUS : SOFTPLUS + 1]
        going = mask_ref[b, :, 0:1]
        a = jnp.exp(log_keep) * going
        a_ref[b] = a
        scale = jnp.where(going > 0.5, jnp.sqrt(one_minus_exp(2.0 * log_keep)), 1.0)
        to_lanes(a_scr, b, 0, a)
        to_lanes(b_scr, b, 0, i * conv * scale)
    sweep(a_scr, b_scr, p_scr, s_scr, prod_ref, sum_ref, rows, length, False, 0)


def head_spec(rows, length):
    return pl.BlockSpec((rows, length, HEAD_W), lambda h: (0, 0, h))


def recurrent_forward(x_branch, halo, masks, params, blocks):
    rows, length, units = x_branch.shape
    full = head_spec(rows, length)
    scan = pltpu.VMEM((rows, HEAD_W // LANES, length, LANES), F32)
    big = jax.ShapeDtypeStruct((rows, length, units), F32)
    return pl.pallas_call(
        forward_kernel,
        grid=(units // HEAD_W,),
        in_specs=[
            full,
            head_spec(rows, 8),
            pl.BlockSpec((rows, length, 8), lambda h: (0, 0, 0)),
            pl.BlockSpec((PARAM_ROWS, HEAD_W), lambda h: (0, h)),
            pl.BlockSpec((2, HEAD_W, HEAD_W), lambda h: (0, 0, h)),
        ],
        out_specs=[full] * 6,
        out_shape=[jax.ShapeDtypeStruct((rows, length, units), BF16)] + [big] * 5,
        scratch_shapes=[pltpu.VMEM((rows, length + 8, HEAD_W), F32), scan, scan, scan, scan],
        compiler_params=pltpu.CompilerParams(vmem_limit_bytes=48 * 1024 * 1024),
        cost_estimate=cost(),
        name="recurrent_forward",
    )(x_branch, halo, masks, params, blocks)


def adjoint_kernel(
    rg_ref, gelu_ref, a_ref, prod_ref, sum_ref, in_ref,
    gg_ref, tprod_ref, tsum_ref,
    a_scr, b_scr, p_scr, s_scr,
):
    rows, length, _ = rg_ref.shape
    for b in range(rows):
        states = sum_ref[b] + prod_ref[b] * in_ref[b, 0:1]
        value, slope = gelu_pair(gelu_ref[b])
        rg = rg_ref[b]
        gg_ref[b] = (rg * states * slope).astype(BF16)
        to_lanes(a_scr, b, 0, a_ref[b])
        to_lanes(a_scr, b, length, jnp.ones((8, HEAD_W), F32))
        to_lanes(b_scr, b, 0, rg * value)
    sweep(a_scr, b_scr, p_scr, s_scr, tprod_ref, tsum_ref, rows, length, True, 1)


def recurrent_adjoint(rec_grad, gelu_in, coef, prod, total, state_in):
    rows, length, units = rec_grad.shape
    full = head_spec(rows, length)
    scan = pltpu.VMEM((rows, HEAD_W // LANES, length, LANES), F32)
    longer = pltpu.VMEM((rows, HEAD_W // LANES, length + 8, LANES), F32)
    big = jax.ShapeDtypeStruct((rows, length, units), F32)
    return pl.pallas_call(
        adjoint_kernel,
        grid=(units // HEAD_W,),
        in_specs=[full] * 5 + [head_spec(rows, 8)],
        out_specs=[full] * 3,
        out_shape=[jax.ShapeDtypeStruct((rows, length, units), BF16), big, big],
        scratch_shapes=[longer, scan, scan, scan],
        compiler_params=pltpu.CompilerParams(vmem_limit_bytes=48 * 1024 * 1024),
        cost_estimate=cost(),
        name="recurrent_adjoint",
    )(rec_grad, gelu_in, coef, prod, total, state_in)


def backward_kernel(
    tprod_ref, tsum_ref, leave_ref, prod_ref, sum_ref, in_ref, a_ref, r_ref, i_ref, conv_ref,
    x_ref, halo_ref, mask_ref, par_ref, w_ref,
    bx_ref, before_ref, small_ref, blocks_ref,
    ext, st_ext, g_ext,
):
    rows, length, _ = tprod_ref.shape
    par = par_ref[...]
    w0, w1 = w_ref[0], w_ref[1]
    sums = [jnp.zeros((1, HEAD_W), F32) for _ in range(8)]
    blocks = [jnp.zeros((HEAD_W, HEAD_W), F32) for _ in range(2)]

    def add(n, value):
        sums[n] = sums[n] + jnp.sum(value, axis=0, keepdims=True)

    for b in range(rows):
        adjoint = tsum_ref[b] + tprod_ref[b] * leave_ref[b, 0:1]
        st_ext[b, pl.ds(0, 8), :] = in_ref[b]
        st_ext[b, pl.ds(8, length), :] = sum_ref[b] + prod_ref[b] * in_ref[b, 0:1]
        prev = st_ext[b, pl.ds(7, length), :]
        r, i, a = r_ref[b], i_ref[b], a_ref[b]
        conv_low = conv_ref[b]
        conv = conv_low.astype(F32)
        going = mask_ref[b, :, 0:1]
        log_keep = -DECAY_SCALE * r * par[SOFTPLUS : SOFTPLUS + 1]
        scale = jnp.where(going > 0.5, jnp.sqrt(one_minus_exp(2.0 * log_keep)), 1.0)
        log_grad = adjoint * prev * a - adjoint * i * conv * (a * a) / scale
        rate = log_grad * (-DECAY_SCALE * par[SOFTPLUS : SOFTPLUS + 1]) * r * (1.0 - r)
        spread = adjoint * scale
        inlet = spread * conv * i * (1.0 - i)
        add(5, rate)
        add(6, inlet)
        add(7, log_grad * r)
        rate_low = rate.astype(BF16)
        inlet_low = inlet.astype(BF16)
        grad = spread * i + dot(rate_low, w0, ((1,), (1,))) + dot(inlet_low, w1, ((1,), (1,)))
        blocks[0] = blocks[0] + dot(conv_low, rate_low, ((0,), (0,)))
        blocks[1] = blocks[1] + dot(conv_low, inlet_low, ((0,), (0,)))
        ext[b, pl.ds(0, 8), :] = halo_ref[b]
        ext[b, pl.ds(8, length), :] = x_ref[b].astype(F32)
        add(4, grad)
        add(0, grad * ext[b, pl.ds(8, length), :])
        bx = grad * par[TAP0 : TAP0 + 1]
        g_ext[b, pl.ds(0, 8), :] = jnp.zeros((8, HEAD_W), F32)
        g_ext[b, pl.ds(8 + length, 8), :] = jnp.zeros((8, HEAD_W), F32)
        before = jnp.zeros((8, HEAD_W), F32)
        for k in range(1, 4):
            masked = grad * mask_ref[b, :, k : k + 1]
            add(k, masked * ext[b, pl.ds(8 - k, length), :])
            g_ext[b, pl.ds(8, length), :] = masked
            tap = par[TAP0 + k : TAP0 + k + 1]
            bx = bx + tap * g_ext[b, pl.ds(8 + k, length), :]
            before = before + tap * g_ext[b, pl.ds(k, 8), :]
        bx_ref[b] = bx
        before_ref[b] = before
    sums[7] = sums[7] * (DECAY_SCALE * par[NEG_SIG : NEG_SIG + 1])
    for n in range(8):
        small_ref[pl.ds(n, 1), :] = sums[n]
    blocks_ref[0] = blocks[0].astype(blocks_ref.dtype)
    blocks_ref[1] = blocks[1].astype(blocks_ref.dtype)


def recurrent_backward(tprod, tsum, leaving, prod, total, state_in, coef, r, i, conv_low, x_branch, halo, masks, params, blocks):
    rows, length, units = tprod.shape
    full = head_spec(rows, length)
    edge = head_spec(rows, 8)
    return pl.pallas_call(
        backward_kernel,
        grid=(units // HEAD_W,),
        in_specs=[
            full, full, edge, full, full, edge, full, full, full, full, full, edge,
            pl.BlockSpec((rows, length, 8), lambda h: (0, 0, 0)),
            pl.BlockSpec((PARAM_ROWS, HEAD_W), lambda h: (0, h)),
            pl.BlockSpec((2, HEAD_W, HEAD_W), lambda h: (0, 0, h)),
        ],
        out_specs=[
            full,
            edge,
            pl.BlockSpec((8, HEAD_W), lambda h: (0, h)),
            pl.BlockSpec((2, HEAD_W, HEAD_W), lambda h: (0, 0, h)),
        ],
        out_shape=[
            jax.ShapeDtypeStruct((rows, length, units), F32),
            jax.ShapeDtypeStruct((rows, 8, units), F32),
            jax.ShapeDtypeStruct((8, units), F32),
            jax.ShapeDtypeStruct((2, HEAD_W, units), BF16),
        ],
        scratch_shapes=[
            pltpu.VMEM((rows, length + 8, HEAD_W), F32),
            pltpu.VMEM((rows, length + 8, HEAD_W), F32),
            pltpu.VMEM((rows, length + 16, HEAD_W), F32),
        ],
        compiler_params=pltpu.CompilerParams(vmem_limit_bytes=48 * 1024 * 1024),
        cost_estimate=cost(),
        name="recurrent_backward",
    )(tprod, tsum, leaving, prod, total, state_in, coef, r, i, conv_low, x_branch, halo, masks, params, blocks)


TILE = 256


def tokens_spec(columns, tiles, first):
    return pl.BlockSpec((TILE, columns), lambda m: ((m + first) % tiles, 0))


def held(rows, columns, at=0):
    return pl.BlockSpec((rows, columns), lambda m: (0, at), pipeline_mode=pl.Buffered(1))


def half_specs(columns, tiles):
    mid = tiles // 2
    return [
        pl.BlockSpec((TILE, columns), lambda m: (jnp.maximum(m - mid, 0), 0)),
        pl.BlockSpec((TILE, columns), lambda m: (jnp.minimum(m, mid - 1), 0)),
    ]


def store_half(first_ref, second_ref, tiles, value):
    m = pl.program_id(0)

    @pl.when(m < tiles // 2)
    def _():
        second_ref[...] = value

    @pl.when(m >= tiles // 2)
    def _():
        first_ref[...] = value


def feed_params():
    return pltpu.CompilerParams(vmem_limit_bytes=56 * 1024 * 1024)


def cost():
    return pl.CostEstimate(flops=1, bytes_accessed=1, transcendentals=0)


def feed_forward(pieces, w_feed):
    width = pieces[0].shape[1]
    share = w_feed.shape[1] // 3
    part = TILE // 2
    halves = []
    for n, piece in enumerate(pieces):
        halves += [(n, at) for at in range(0, piece.shape[0], part)]
    tiles = len(halves) // 2
    count = tiles * TILE

    def body(*refs):
        xs, (w_ref, all_ref, hidden_ref, by_gate_ref, by_up_ref, held_x, sems) = refs[: len(pieces)], refs[len(pieces) :]
        m = pl.program_id(0)

        def fetch(tile, slot):
            for at in range(tiles):

                @pl.when(tile == at)
                def _():
                    for h in range(2):
                        n, row = halves[2 * at + h]
                        pltpu.make_async_copy(
                            xs[n].at[pl.ds(row, part)], held_x.at[slot, pl.ds(h * part, part)], sems.at[slot, h]
                        ).start()

        @pl.when(m == 0)
        def _():
            fetch(0, 0)

        @pl.when(m + 1 < tiles)
        def _():
            fetch(m + 1, (m + 1) % 2)

        slot = m % 2
        for h in range(2):
            pltpu.make_async_copy(
                xs[0].at[pl.ds(0, part)], held_x.at[slot, pl.ds(h * part, part)], sems.at[slot, h]
            ).wait()
        x = held_x[slot]
        all_ref[...] = x
        value, slope = gelu_pair(dot(x, w_ref[:, :share], ((1,), (0,))))
        up = dot(x, w_ref[:, share:], ((1,), (0,)))
        hidden_ref[...] = (value * up).astype(BF16)
        by_gate_ref[...] = up * slope
        by_up_ref[...] = value

    tile = tokens_spec(share, tiles, 0)
    return pl.pallas_call(
        body,
        grid=(tiles,),
        in_specs=[pl.BlockSpec(memory_space=pl.ANY)] * len(pieces) + [held(width, 2 * share)],
        out_specs=[tokens_spec(width, tiles, 0)] + [tile] * 3,
        out_shape=[
            jax.ShapeDtypeStruct((count, width), BF16),
            jax.ShapeDtypeStruct((count, share), BF16),
            jax.ShapeDtypeStruct((count, share), F32),
            jax.ShapeDtypeStruct((count, share), F32),
        ],
        scratch_shapes=[pltpu.VMEM((2, TILE, width), BF16), pltpu.SemaphoreType.DMA((2, 2))],
        compiler_params=feed_params(),
        cost_estimate=cost(),
        name="feed_forward",
    )(*pieces, w_feed)


def feed_backward(feed_grad, by_gate, by_up, w_feed):
    count, width = feed_grad.shape
    share = w_feed.shape[1] // 3
    tiles = count // TILE
    mid = tiles // 2

    def body(fg_ref, gate_ref, up_ref, wd_ref, we_ref, low_ref, first_ref, second_ref):
        grad = dot(fg_ref[...], wd_ref[...], ((1,), (0,)))
        gate = (grad * gate_ref[...]).astype(BF16)
        up = (grad * up_ref[...]).astype(BF16)
        low_ref[:, :share] = gate
        low_ref[:, share:] = up
        terms = dot(gate, we_ref[:, :share], ((1,), (1,))) + dot(up, we_ref[:, share:], ((1,), (1,)))
        store_half(first_ref, second_ref, tiles, terms.astype(BF16))

    tile = tokens_spec(share, tiles, mid)
    return pl.pallas_call(
        body,
        grid=(tiles,),
        in_specs=[tokens_spec(width, tiles, mid), tile, tile, held(width, share, 2), held(width, 2 * share)],
        out_specs=[tokens_spec(2 * share, tiles, mid)] + half_specs(width, tiles),
        out_shape=[
            jax.ShapeDtypeStruct((count, 2 * share), BF16),
            jax.ShapeDtypeStruct((count // 2, width), BF16),
            jax.ShapeDtypeStruct((count // 2, width), BF16),
        ],
        compiler_params=feed_params(),
        cost_estimate=cost(),
        name="feed_backward",
    )(feed_grad, by_gate, by_up, w_feed, w_feed)


def feed_down(hidden, w_feed):
    count, share = hidden.shape
    width = w_feed.shape[0]
    tiles = count // TILE

    def body(h_ref, w_ref, first_ref, second_ref):
        store_half(first_ref, second_ref, tiles, dot(h_ref[...], w_ref[...], ((1,), (1,))).astype(BF16))

    return pl.pallas_call(
        body,
        grid=(tiles,),
        in_specs=[tokens_spec(share, tiles, tiles // 2), held(width, share, 2)],
        out_specs=half_specs(width, tiles),
        out_shape=[jax.ShapeDtypeStruct((count // 2, width), BF16)] * 2,
        compiler_params=feed_params(),
        cost_estimate=cost(),
        name="feed_down",
    )(hidden, w_feed)


def weight_grad(x, grad, into=None, at=0, blocks=1):
    count, width = x.shape
    columns = grad.shape[1]
    deep, wide = 512 if count > 1024 else width // 2, columns // blocks

    def body(x_ref, g_ref, *rest):
        rest[-1][...] = dot(x_ref[...], g_ref[...], ((0,), (0,))).astype(BF16)

    return pl.pallas_call(
        body,
        grid=(width // deep,),
        in_specs=[
            pl.BlockSpec((count, deep), lambda m: (0, m)),
            pl.BlockSpec((count, wide), lambda m: (0, at), pipeline_mode=pl.Buffered(1)),
        ]
        + ([] if into is None else [pl.BlockSpec(memory_space=pl.ANY)]),
        out_specs=pl.BlockSpec((deep, wide), lambda m: (m, at)),
        out_shape=jax.ShapeDtypeStruct((width, columns), BF16),
        input_output_aliases={} if into is None else {2: 0},
        compiler_params=feed_params(),
        cost_estimate=cost(),
        name="weight_grad",
    )(x, grad, *([] if into is None else [into]))


ORDER = (1, 3, 2, 0)


def weight_grad_parts(x, grad, places, extra=None):
    count, width = x.shape
    columns = grad.shape[1]
    rows, cols = width // SQUARE, columns // 2
    more = 0 if extra is None else extra.shape[0] // SQUARE
    each = rows + more

    def body(places_ref, x_ref, g_ref, *rest):
        left_ref, right_ref, two_ref, one_ref, own_left, own_right = rest[-6:]
        targets = [
            ((left_ref, 0), (one_ref, 0)),
            ((left_ref, each), (right_ref, 0)),
            ((two_ref, 0), (right_ref, each)),
            ((own_left, 0), (own_right, 0)),
        ]
        value = dot(x_ref[...], g_ref[...], ((0,), (0,))).astype(BF16)
        for n in range(SQUARE):

            @pl.when(pl.program_id(0) == n)
            def _():
                for h, (ref, at) in enumerate(targets[n]):
                    ref[pl.ds(at, rows), :] = value[:, h * cols : (h + 1) * cols]
                    if more:
                        ref[pl.ds(at + rows, more), :] = rest[0][:, h * cols : (h + 1) * cols]

    sizes = [2 * each, 2 * each] + [each] * 4
    return pl.pallas_call(
        body,
        grid_spec=pltpu.PrefetchScalarGridSpec(
            num_scalar_prefetch=1,
            grid=(SQUARE,),
            in_specs=[
                pl.BlockSpec((count, rows), lambda n, places_ref: (0, places_ref[n])),
                pl.BlockSpec((count, columns), lambda n, places_ref: (0, 0)),
            ]
            + ([pl.BlockSpec((more, columns), lambda n, places_ref: (places_ref[n], 0))] if more else []),
            out_specs=[pl.BlockSpec((size, cols), lambda n, places_ref: (0, 0)) for size in sizes],
        ),
        out_shape=[jax.ShapeDtypeStruct((size, cols), BF16) for size in sizes],
        compiler_params=feed_params(),
        cost_estimate=cost(),
        name="weight_grad_parts",
    )(places, x, grad, *([extra] if more else []))


def cross(x, axis, r):
    return lax.ppermute(x, axis, [(i, i ^ r) for i in range(lax.axis_size(axis))])


def total_over(x, axis):
    r = 1
    while r < lax.axis_size(axis):
        x = x + cross(x, axis, r)
        r *= 2
    return x


def after(x, done):
    return lax.optimization_barrier((x, done))


SQUARE = 4


def token_axes():
    return ("fsdp", "ctx") if lax.axis_size("fsdp") == SQUARE else ("ctx", "fsdp")


def together(*values):
    return lax.optimization_barrier(values)


def place(blocks, axis):
    me = lax.axis_index(axis)
    first = blocks[0]
    whole = jnp.zeros((len(blocks),) + first.shape, first.dtype)
    for r, block in enumerate(blocks):
        at = 0
        for piece in block if isinstance(block, list) else [block]:
            whole = lax.dynamic_update_slice(whole, piece[None], (me ^ r, at) + (0,) * (piece.ndim - 1))
            at += piece.shape[0]
    return whole


def near_blocks(x, axis):
    return list(together(cross(x, axis, 1), cross(x, axis, 2)))


def far_block(got, axis):
    mid = got[0].shape[0] // 2
    halves = together(got[0][:mid], got[1][mid:])
    return [cross(halves[0], axis, 2), cross(halves[1], axis, 1)]


def near(x, axis):
    got = near_blocks(x, axis)
    return [x] + got + [far_block(got, axis)]


def low(v):
    return v.astype(BF16)


def wide(v):
    return v.astype(F32)


def near_send(parts, axis):
    return together(cross(parts[0], axis, 1), cross(parts[1], axis, 2))


def near_middle(parts, got):
    rows = got[0].shape[0] // 2
    return together(low(wide(parts[2]) + wide(got[0][rows:])), low(wide(parts[3]) + wide(got[1][:rows])))


def near_second(sums, axis):
    return together(cross(sums[0], axis, 2), cross(sums[1], axis, 1))


def near_last(parts, got, more):
    rows = got[0].shape[0] // 2
    left = wide(parts[4]) + wide(got[0][:rows]) + wide(more[0])
    right = wide(parts[5]) + wide(got[1][rows:]) + wide(more[1])
    return jnp.concatenate([left, right], axis=1)


def gather_in_turn(arrays):
    if lax.axis_size("fsdp") != SQUARE:
        return [lax.all_gather(x, "fsdp", axis=0) for x in arrays]
    results = []
    for x in arrays:
        if results:
            x, results[-1] = together(x, results[-1])
        results.append(near(x, "fsdp"))
    return results


def rows_of(blocks, start, stop):
    if lax.axis_size("fsdp") != SQUARE:
        return blocks[:, :, start:stop].reshape(-1, blocks.shape[-1])
    cut = lambda v: v[:, start:stop]
    whole = place([[cut(v) for v in block] if isinstance(block, list) else cut(block) for block in blocks], "fsdp")
    return whole.reshape(-1, whole.shape[-1])


def token_pieces(x):
    axis = token_axes()[0]
    theirs = swap(x, "tp")
    got = near_blocks(x, axis)
    far = far_block(got, axis)
    got_theirs = [swap(v, "tp") for v in got]
    far_theirs = [swap(v, "tp") for v in far]
    return [got[0], *far, got[1], x, got_theirs[0], *far_theirs, got_theirs[1], theirs]


def token_parts(first, theirs):
    rows, cols = first.shape[0] // SQUARE, first.shape[1] // 2

    def part(start, stop, half):
        here = (slice(start * rows, stop * rows), slice(half * cols, (half + 1) * cols))
        return low(wide(first[here]) + wide(theirs[here]))

    return together(part(0, 2, 0), part(1, 3, 1), part(2, 3, 0), part(0, 1, 1), part(3, 4, 0), part(3, 4, 1))


def trade(pieces):
    axis = token_axes()[0]
    me = lax.axis_index(axis)
    return place([pieces(me)] + [cross(pieces(me ^ r), axis, r) for r in range(1, SQUARE)], axis)


def gather_feed(local):
    _, along = token_axes()
    whole = lax.all_gather(local, along, axis=1 if along == "ctx" else 0, tiled=True)
    return whole.reshape(-1, local.shape[2])


def scatter_feed(grad):
    _, along = token_axes()
    if along == "ctx":
        grad = grad.reshape(SQUARE, -1, grad.shape[1])
        return lax.psum_scatter(grad, along, scatter_dimension=1, tiled=True)
    part = lax.psum_scatter(grad, along, scatter_dimension=0, tiled=True)
    return part.reshape(SQUARE, -1, grad.shape[1])


def rms(values):
    return lax.rsqrt(jnp.mean(values * values, axis=-1, keepdims=True) + EPSILON)


def rms_back(values, inverse, gain, grad):
    u = grad * gain
    inner = jnp.mean(values * u, axis=-1, keepdims=True)
    gain_grad = jnp.sum(grad * values * inverse, axis=0)
    return inverse * u - values * (inverse * inverse * inverse) * inner, gain_grad


def shards(
    block_input, segments, token_mask, cotangent, norm_gains, conv_taps, conv_offset, gate_offset,
    decay_logit, intake, gate_blocks, outlet, expand, contract,
):
    rows, length, width = block_input.shape
    depth = intake.shape[0]
    units = intake.shape[2]
    gate_rows = gate_blocks.shape[0]
    hidden_units = contract.shape[1]
    tokens = rows * length
    ctx, tp = lax.axis_size("ctx"), lax.axis_size("tp")
    mine = lax.axis_index("tp")
    half = tokens // tp
    share = -(-hidden_units // (SQUARE * 256)) * 256
    padding = SQUARE * share - hidden_units

    def own(x):
        return lax.dynamic_slice_in_dim(x, mine * half, half, 0)

    def other(x):
        return lax.dynamic_slice_in_dim(x, (1 - mine) * half, half, 0)

    def join(x):
        theirs = swap(x, "tp")
        return jnp.concatenate(
            [jnp.where(mine == 0, x, theirs), jnp.where(mine == 0, theirs, x)], axis=0
        )

    first = jnp.concatenate([intake[:, 1], gate_blocks.reshape(2 * gate_rows, units)], axis=0)
    first = lax.all_gather(first, "ctx", axis=0)
    second = lax.all_gather(jnp.concatenate([intake[:, 0], outlet], axis=0), "ctx", axis=0)

    def cut(w):
        w = jnp.pad(w, ((0, 0), (0, padding)))
        return lambda p: lax.dynamic_slice_in_dim(w, p * share, share, 1)

    down, gate_in, up_in = cut(contract), cut(expand[:, 0]), cut(expand[:, 1])
    w_feed = gather_feed(trade(lambda p: jnp.concatenate([gate_in(p), up_in(p), down(p)], axis=1)))

    mask_rows = token_mask.astype(F32).reshape(tokens, 1)
    out_grad = own(cotangent.reshape(tokens, width)).astype(F32) * own(mask_rows)
    local_feed_grad = out_grad.astype(BF16)

    got_first, got_gelu, got_outlet = gather_in_turn([first, second[:, :depth], second[:, depth:]])
    w_branch = rows_of(got_first, 0, depth)
    blocks = rows_of(got_first, depth, first.shape[1]).reshape(HEAD_W, 2, units).transpose(1, 0, 2)
    w_gelu = rows_of(got_gelu, 0, depth)
    w_outlet = rows_of(got_outlet, 0, depth)

    seg_next = segments + 1
    seg_before = shifted(seg_next[:, -3:], "ctx", 1)
    seg_ext = jnp.concatenate([seg_before, seg_next], axis=1)
    masks = jnp.stack(
        [(seg_ext[:, 3 - k : 3 - k + length] == seg_next).astype(F32) for k in (1, 1, 2, 3)]
        + [jnp.zeros(segments.shape, F32)] * 4,
        axis=2,
    )
    params = jnp.concatenate(
        [
            conv_taps,
            conv_offset[None],
            gate_offset,
            jax.nn.softplus(-decay_logit)[None],
            jax.nn.sigmoid(-decay_logit)[None],
            jnp.zeros((PARAM_ROWS - 9, units), F32),
        ],
        axis=0,
    )

    x = block_input.reshape(tokens, width).astype(F32)
    inverse_one = rms(x)
    normed = (x * inverse_one * norm_gains[0]).astype(BF16)
    x_branch = dot(normed, w_branch, ((1,), (0,))).astype(BF16).reshape(rows, length, units)
    gelu_in = dot(normed, w_gelu, ((1,), (0,))).reshape(rows, length, units)
    x_before = shifted(x_branch[:, -3:], "ctx", 1)
    halo = jnp.pad(x_before, ((0, 0), (5, 0), (0, 0))).astype(F32)
    conv_low, r, i, coef, prod, total = recurrent_forward(x_branch, halo, masks, params, blocks)
    ends = jnp.stack([prod[:, -1], total[:, -1]])
    entering = jnp.zeros((rows, units), F32)
    for by in range(ctx - 1, 0, -1):
        end = shifted(ends, "ctx", by)
        entering = end[1] + end[0] * entering
    state_in = jnp.broadcast_to(entering[:, None], (rows, 8, units))
    states = total + prod * entering[:, None]
    recurrent = (states * jax.nn.gelu(gelu_in, approximate=True)).astype(BF16).reshape(tokens, units)

    sent = swap(dot(other(recurrent), w_outlet, ((1,), (1,))), "tp")
    branch = dot(own(recurrent), w_outlet, ((1,), (1,))) + sent
    residual = own(x) + branch
    inverse_two = rms(residual)
    normed_two = token_pieces((residual * inverse_two * norm_gains[1]).astype(BF16))

    def to_owners(part):
        return trade(lambda p: lax.dynamic_index_in_dim(part, p, 0, keepdims=False))

    local_feed_grad, normed_two = together(local_feed_grad, normed_two)
    feed_grad = jnp.concatenate(token_pieces(local_feed_grad), axis=0)
    normed_two, hidden, by_gate, by_up = feed_forward(normed_two, w_feed)
    down_grad = weight_grad(feed_grad, hidden)
    by_gate, down_grad = after(by_gate, down_grad)
    down_part = scatter_feed(down_grad)
    expand_low, n2g_own, n2g_other = feed_backward(feed_grad, by_gate, by_up, w_feed)

    group = token_axes()[0]
    theirs = swap(n2g_other, "tp")
    parts, expand_low = after(token_parts(n2g_own, theirs), expand_low)
    got = near_send(parts, group)
    expand_all = weight_grad(normed_two, expand_low)
    got, expand_all = after(got, expand_all)
    sums, hidden = after(near_middle(parts, got), hidden)
    more = near_second(sums, group)
    feed_own, feed_other = feed_down(hidden, w_feed)
    more, (feed_own, feed_other) = after(more, (feed_own, feed_other))
    normed_two_grad = near_last(parts, got, more)
    expand_part = scatter_feed(expand_all)
    feed_theirs = swap(feed_other, "tp")

    norm_part, gain_two = rms_back(residual, inverse_two, norm_gains[1], normed_two_grad)
    residual_grad = out_grad + norm_part
    branch_grad = join(residual_grad.astype(BF16))

    square = lax.axis_size("fsdp") == SQUARE
    places = lax.axis_index("fsdp").astype(jnp.int32) ^ jnp.array(ORDER, jnp.int32)
    rec_grad = dot(branch_grad, w_outlet, ((1,), (0,))).reshape(rows, length, units)
    feed_parts, rec_grad = after(token_parts(feed_own, feed_theirs), rec_grad)
    feed_got = near_send(feed_parts, group)
    gelu_grad, tprod, tsum = recurrent_adjoint(rec_grad, gelu_in, coef, prod, total, state_in)
    heads = jnp.stack([coef[:, 0] * tprod[:, 0], coef[:, 0] * tsum[:, 0]])
    leaving = jnp.zeros((rows, units), F32)
    for by in range(ctx - 1, 0, -1):
        head = shifted(heads, "ctx", -by)
        leaving = head[1] + head[0] * leaving
    leaving = jnp.broadcast_to(leaving[:, None], (rows, 8, units))
    gelu_low = gelu_grad.reshape(tokens, units)
    branch_grad, gelu_low = after(branch_grad, gelu_low)
    if square:
        outlet_parts = weight_grad_parts(branch_grad, recurrent, places)
    else:
        outlet_parts = weight_grad(branch_grad, recurrent)
    outlet_parts, tprod, feed_got = together(outlet_parts, tprod, feed_got)
    feed_sums = near_middle(feed_parts, feed_got)
    feed_sums, tprod = after(feed_sums, tprod)
    feed_more = near_second(feed_sums, group)
    if square:
        outlet_got = near_send(outlet_parts, "fsdp")
    branch_x, before, small, blocks_grad = recurrent_backward(
        tprod, tsum, leaving, prod, total, state_in, coef, r, i, conv_low, x_branch, halo, masks, params, blocks
    )
    gelu_low, small = after(gelu_low, small)
    if square:
        gelu_parts = weight_grad_parts(normed, gelu_low, places)
    else:
        gelu_parts = weight_grad(normed, gelu_low)
    from_next = shifted(before[:, 5:], "ctx", -1)
    branch_x = branch_x + jnp.pad(from_next, ((0, 0), (length - 3, 0), (0, 0)))
    branch_low, gelu_parts = together(branch_x.astype(BF16).reshape(tokens, units), gelu_parts)
    blocks_rows = blocks_grad.transpose(1, 0, 2).reshape(2 * HEAD_W, units)
    if square:
        branch_parts = weight_grad_parts(normed, branch_low, places, blocks_rows)
        outlet_got, branch_parts, feed_more = together(outlet_got, branch_parts, feed_more)
        outlet_sums, gelu_parts = after(near_middle(outlet_parts, outlet_got), gelu_parts)
        outlet_more, gelu_got = near_second(outlet_sums, "fsdp"), near_send(gelu_parts, "fsdp")
    else:
        branch_parts = weight_grad(normed, branch_low)

    def input_terms(pick):
        return dot(pick(branch_low), w_branch, ((1,), (1,))) + dot(pick(gelu_low), w_gelu, ((1,), (1,)))

    theirs = input_terms(other)
    normed_grad = input_terms(own) + swap(theirs, "tp")
    norm_part, gain_one = rms_back(own(x), own(inverse_one), norm_gains[0], normed_grad)
    input_own = residual_grad + norm_part
    if square:
        gelu_got, outlet_more, input_own = together(gelu_got, outlet_more, input_own)
        early = [low(near_last(outlet_parts, outlet_got, outlet_more))]
        gelu_sums, branch_parts = together(near_middle(gelu_parts, gelu_got), branch_parts)
        gelu_more, branch_got = near_second(gelu_sums, "fsdp"), near_send(branch_parts, "fsdp")
        early.append(low(near_last(gelu_parts, gelu_got, gelu_more)))
    else:
        early = [lax.psum_scatter(v, "fsdp", scatter_dimension=0, tiled=True) for v in (outlet_parts, gelu_parts)]
    early = jnp.concatenate([v.reshape(ctx, depth, units) for v in early], axis=2)
    early, expand_part = after(early, expand_part)
    if square:
        branch_got, early = together(branch_got, early)
        late = low(near_last(branch_parts, branch_got, near_second(near_middle(branch_parts, branch_got), "fsdp")))
        late = [late[: ctx * depth], late[ctx * depth :]]
    else:
        late = [lax.psum_scatter(v, "fsdp", scatter_dimension=0, tiled=True) for v in (branch_parts, blocks_rows)]
    late = jnp.concatenate([v.reshape(ctx, -1, units) for v in late], axis=1)

    early = lax.psum_scatter(early, "ctx", scatter_dimension=0, tiled=False)
    late, early = after(late, early)
    late = wide(lax.psum_scatter(late, "ctx", scatter_dimension=0, tiled=False))

    down_part = to_owners(down_part)
    expand_part = to_owners(expand_part)
    feed_out = near_last(feed_parts, feed_got, feed_more)
    block_output = join(low(residual + feed_out)).reshape(rows, length, width)
    input_grad = join(input_own).reshape(rows, length, width)

    def columns(part, n):
        return jnp.concatenate([part[p, :, n * share : (n + 1) * share] for p in range(SQUARE)], axis=1)[
            :, :hidden_units
        ].astype(F32)

    contract_grad = columns(down_part, 0)
    expand_grad = jnp.stack([columns(expand_part, 0), columns(expand_part, 1)], axis=1)

    gains = jnp.concatenate([gain_one, gain_two]).reshape(-1, units)
    small = total_over(total_over(jnp.concatenate([small, gains], axis=0), "fsdp"), "ctx")
    gains = total_over(small[8:], "tp").reshape(2, width)
    return (
        block_output,
        input_grad,
        gains,
        small[0:4],
        small[4],
        small[5:7],
        small[7],
        jnp.stack([wide(early[:, units:]), late[:depth]], axis=1),
        late[depth:].reshape(gate_rows, 2, units),
        wide(early[:, :units]),
        expand_grad,
        contract_grad,
    )


def solution(mesh):
    placed = (
        P("fsdp", "ctx", None),
        P("fsdp", "ctx"),
        P("fsdp", "ctx"),
        P("fsdp", "ctx", None),
        P(),
        P(None, "tp"),
        P("tp"),
        P(None, "tp"),
        P("tp"),
        P(("fsdp", "ctx"), None, "tp"),
        P(("fsdp", "ctx"), None, "tp"),
        P(("fsdp", "ctx"), "tp"),
        P(("fsdp", "ctx"), None, "tp"),
        P(("fsdp", "ctx"), "tp"),
    )
    return jax.shard_map(
        shards,
        mesh=mesh,
        in_specs=placed,
        out_specs=(
            P("fsdp", "ctx", None),
            P("fsdp", "ctx", None),
            P(),
            P(None, "tp"),
            P("tp"),
            P(None, "tp"),
            P("tp"),
            P(("fsdp", "ctx"), None, "tp"),
            P(("fsdp", "ctx"), None, "tp"),
            P(("fsdp", "ctx"), "tp"),
            P(("fsdp", "ctx"), None, "tp"),
            P(("fsdp", "ctx"), "tp"),
        ),
        check_vma=False,
    )
```

```python
import jax
import jax.numpy as jnp
from jax import lax
from jax.experimental import pallas as pl
from jax.experimental.pallas import tpu as pltpu
from jax.sharding import PartitionSpec as P

HEAD_W = 256
LANES = 128
CHUNKS = 8

EPSILON = 1e-06
DECAY_SCALE = 8.0
GELU_C = 0.7978845608028654
GELU_A = 0.044715

F32 = jnp.float32
BF16 = jnp.bfloat16

TAP0, OFFSET, RATE_OFF, INLET_OFF, SOFTPLUS, NEG_SIG, PARAM_ROWS = 0, 4, 5, 6, 7, 8, 16


def shifted(x, axis, by):
    length = lax.axis_size(axis)
    pairs = [(i, i + by) for i in range(length) if 0 <= i + by < length]
    return lax.ppermute(x, axis, pairs)


def swap(x, axis):
    length = lax.axis_size(axis)
    return lax.ppermute(x, axis, [(i, (i + 1) % length) for i in range(length)])


def gelu_pair(v):
    t = jnp.tanh(GELU_C * (v + GELU_A * v * v * v))
    value = 0.5 * v * (1.0 + t)
    slope = 0.5 * (1.0 + t) + 0.5 * v * (1.0 - t * t) * GELU_C * (1.0 + 3.0 * GELU_A * v * v)
    return value, slope


def one_minus_exp(x):
    s = 1.0 + x / 7.0
    for n in (6.0, 5.0, 4.0, 3.0, 2.0):
        s = 1.0 + x / n * s
    return jnp.where(x > -0.5, -x * s, 1.0 - jnp.exp(x))


def sigmoid(v):
    return 1.0 / (1.0 + jnp.exp(-v))


def dot(a, b, dims):
    return lax.dot_general(a, b, (dims, ((), ())), preferred_element_type=F32)


def lane_scan(load_a, load_b, store, length, reverse):
    steps = length // CHUNKS
    prod = jnp.ones((CHUNKS, LANES), F32)
    total = jnp.zeros((CHUNKS, LANES), F32)
    for n in range(steps):
        s = steps - 1 - n if reverse else n
        coef = load_a(s)
        total = coef * total + load_b(s)
        prod = coef * prod
        store(s, prod, total)
    return prod, total


def chunk_carries(prod, total, reverse):
    order = range(CHUNKS - 1, -1, -1) if reverse else range(CHUNKS)
    run_p = jnp.ones((1, LANES), F32)
    run_s = jnp.zeros((1, LANES), F32)
    carries = [None] * CHUNKS
    for c in order:
        carries[c] = (run_p, run_s)
        run_s = prod[c : c + 1] * run_s + total[c : c + 1]
        run_p = prod[c : c + 1] * run_p
    return carries


def sweep(a_scr, b_scr, p_scr, s_scr, prod_ref, sum_ref, rows, length, reverse, shift):
    steps = length // CHUNKS
    for b in range(rows):
        for j in range(HEAD_W // LANES):
            av, bv, pv, sv = (a_scr.at[b, j], b_scr.at[b, j], p_scr.at[b, j], s_scr.at[b, j])

            def store(s, prod, total):
                pv[pl.ds(s, CHUNKS, stride=steps), :] = prod
                sv[pl.ds(s, CHUNKS, stride=steps), :] = total

            prod, total = lane_scan(
                lambda s: av[pl.ds(s + shift, CHUNKS, stride=steps), :],
                lambda s: bv[pl.ds(s, CHUNKS, stride=steps), :],
                store,
                length,
                reverse,
            )
            carries = chunk_carries(prod, total, reverse)
            lanes = slice(j * LANES, (j + 1) * LANES)
            for c in range(CHUNKS):
                here = slice(c * steps, (c + 1) * steps)
                p = pv[here, :]
                prod_ref[b, here, lanes] = p * carries[c][0]
                sum_ref[b, here, lanes] = sv[here, :] + p * carries[c][1]


def to_lanes(ref, b, at, value):
    for j in range(HEAD_W // LANES):
        ref[b, j, pl.ds(at, value.shape[0]), :] = value[:, j * LANES : (j + 1) * LANES]


def forward_kernel(
    x_ref, halo_ref, mask_ref, par_ref, w_ref,
    conv_ref, r_ref, i_ref, a_ref, prod_ref, sum_ref,
    ext, a_scr, b_scr, p_scr, s_scr,
):
    rows, length, _ = x_ref.shape
    par = par_ref[...]
    w0, w1 = w_ref[0], w_ref[1]
    for b in range(rows):
        ext[b, pl.ds(0, 8), :] = halo_ref[b]
        ext[b, pl.ds(8, length), :] = x_ref[b].astype(F32)
        conv = ext[b, pl.ds(8, length), :] * par[TAP0 : TAP0 + 1] + par[OFFSET : OFFSET + 1]
        for k in range(1, 4):
            match = mask_ref[b, :, k : k + 1]
            conv = conv + par[TAP0 + k : TAP0 + k + 1] * ext[b, pl.ds(8 - k, length), :] * match
        conv_low = conv.astype(BF16)
        conv_ref[b] = conv_low
        conv = conv_low.astype(F32)
        r = sigmoid(dot(conv_low, w0, ((1,), (0,))) + par[RATE_OFF : RATE_OFF + 1])
        i = sigmoid(dot(conv_low, w1, ((1,), (0,))) + par[INLET_OFF : INLET_OFF + 1])
        r_ref[b] = r
        i_ref[b] = i
        log_keep = -DECAY_SCALE * r * par[SOFTPLUS : SOFTPLUS + 1]
        going = mask_ref[b, :, 0:1]
        a = jnp.exp(log_keep) * going
        a_ref[b] = a
        scale = jnp.where(going > 0.5, jnp.sqrt(one_minus_exp(2.0 * log_keep)), 1.0)
        to_lanes(a_scr, b, 0, a)
        to_lanes(b_scr, b, 0, i * conv * scale)
    sweep(a_scr, b_scr, p_scr, s_scr, prod_ref, sum_ref, rows, length, False, 0)


def head_spec(rows, length):
    return pl.BlockSpec((rows, length, HEAD_W), lambda h: (0, 0, h))


def recurrent_forward(x_branch, halo, masks, params, blocks):
    rows, length, units = x_branch.shape
    full = head_spec(rows, length)
    scan = pltpu.VMEM((rows, HEAD_W // LANES, length, LANES), F32)
    big = jax.ShapeDtypeStruct((rows, length, units), F32)
    return pl.pallas_call(
        forward_kernel,
        grid=(units // HEAD_W,),
        in_specs=[
            full,
            head_spec(rows, 8),
            pl.BlockSpec((rows, length, 8), lambda h: (0, 0, 0)),
            pl.BlockSpec((PARAM_ROWS, HEAD_W), lambda h: (0, h)),
            pl.BlockSpec((2, HEAD_W, HEAD_W), lambda h: (0, 0, h)),
        ],
        out_specs=[full] * 6,
        out_shape=[jax.ShapeDtypeStruct((rows, length, units), BF16)] + [big] * 5,
        scratch_shapes=[pltpu.VMEM((rows, length + 8, HEAD_W), F32), scan, scan, scan, scan],
        compiler_params=pltpu.CompilerParams(vmem_limit_bytes=48 * 1024 * 1024),
        cost_estimate=cost(),
        name="recurrent_forward",
    )(x_branch, halo, masks, params, blocks)


def adjoint_kernel(
    rg_ref, gelu_ref, a_ref, prod_ref, sum_ref, in_ref,
    gg_ref, tprod_ref, tsum_ref,
    a_scr, b_scr, p_scr, s_scr,
):
    rows, length, _ = rg_ref.shape
    for b in range(rows):
        states = sum_ref[b] + prod_ref[b] * in_ref[b, 0:1]
        value, slope = gelu_pair(gelu_ref[b])
        rg = rg_ref[b]
        gg_ref[b] = (rg * states * slope).astype(BF16)
        to_lanes(a_scr, b, 0, a_ref[b])
        to_lanes(a_scr, b, length, jnp.ones((8, HEAD_W), F32))
        to_lanes(b_scr, b, 0, rg * value)
    sweep(a_scr, b_scr, p_scr, s_scr, tprod_ref, tsum_ref, rows, length, True, 1)


def recurrent_adjoint(rec_grad, gelu_in, coef, prod, total, state_in):
    rows, length, units = rec_grad.shape
    full = head_spec(rows, length)
    scan = pltpu.VMEM((rows, HEAD_W // LANES, length, LANES), F32)
    longer = pltpu.VMEM((rows, HEAD_W // LANES, length + 8, LANES), F32)
    big = jax.ShapeDtypeStruct((rows, length, units), F32)
    return pl.pallas_call(
        adjoint_kernel,
        grid=(units // HEAD_W,),
        in_specs=[full] * 5 + [head_spec(rows, 8)],
        out_specs=[full] * 3,
        out_shape=[jax.ShapeDtypeStruct((rows, length, units), BF16), big, big],
        scratch_shapes=[longer, scan, scan, scan],
        compiler_params=pltpu.CompilerParams(vmem_limit_bytes=48 * 1024 * 1024),
        cost_estimate=cost(),
        name="recurrent_adjoint",
    )(rec_grad, gelu_in, coef, prod, total, state_in)


def backward_kernel(
    tprod_ref, tsum_ref, leave_ref, prod_ref, sum_ref, in_ref, a_ref, r_ref, i_ref, conv_ref,
    x_ref, halo_ref, mask_ref, par_ref, w_ref,
    bx_ref, before_ref, small_ref, blocks_ref,
    ext, st_ext, g_ext,
):
    rows, length, _ = tprod_ref.shape
    par = par_ref[...]
    w0, w1 = w_ref[0], w_ref[1]
    sums = [jnp.zeros((1, HEAD_W), F32) for _ in range(8)]
    blocks = [jnp.zeros((HEAD_W, HEAD_W), F32) for _ in range(2)]

    def add(n, value):
        sums[n] = sums[n] + jnp.sum(value, axis=0, keepdims=True)

    for b in range(rows):
        adjoint = tsum_ref[b] + tprod_ref[b] * leave_ref[b, 0:1]
        st_ext[b, pl.ds(0, 8), :] = in_ref[b]
        st_ext[b, pl.ds(8, length), :] = sum_ref[b] + prod_ref[b] * in_ref[b, 0:1]
        prev = st_ext[b, pl.ds(7, length), :]
        r, i, a = r_ref[b], i_ref[b], a_ref[b]
        conv_low = conv_ref[b]
        conv = conv_low.astype(F32)
        going = mask_ref[b, :, 0:1]
        log_keep = -DECAY_SCALE * r * par[SOFTPLUS : SOFTPLUS + 1]
        scale = jnp.where(going > 0.5, jnp.sqrt(one_minus_exp(2.0 * log_keep)), 1.0)
        log_grad = adjoint * prev * a - adjoint * i * conv * (a * a) / scale
        rate = log_grad * (-DECAY_SCALE * par[SOFTPLUS : SOFTPLUS + 1]) * r * (1.0 - r)
        spread = adjoint * scale
        inlet = spread * conv * i * (1.0 - i)
        add(5, rate)
        add(6, inlet)
        add(7, log_grad * r)
        rate_low = rate.astype(BF16)
        inlet_low = inlet.astype(BF16)
        grad = spread * i + dot(rate_low, w0, ((1,), (1,))) + dot(inlet_low, w1, ((1,), (1,)))
        blocks[0] = blocks[0] + dot(conv_low, rate_low, ((0,), (0,)))
        blocks[1] = blocks[1] + dot(conv_low, inlet_low, ((0,), (0,)))
        ext[b, pl.ds(0, 8), :] = halo_ref[b]
        ext[b, pl.ds(8, length), :] = x_ref[b].astype(F32)
        add(4, grad)
        add(0, grad * ext[b, pl.ds(8, length), :])
        bx = grad * par[TAP0 : TAP0 + 1]
        g_ext[b, pl.ds(0, 8), :] = jnp.zeros((8, HEAD_W), F32)
        g_ext[b, pl.ds(8 + length, 8), :] = jnp.zeros((8, HEAD_W), F32)
        before = jnp.zeros((8, HEAD_W), F32)
        for k in range(1, 4):
            masked = grad * mask_ref[b, :, k : k + 1]
            add(k, masked * ext[b, pl.ds(8 - k, length), :])
            g_ext[b, pl.ds(8, length), :] = masked
            tap = par[TAP0 + k : TAP0 + k + 1]
            bx = bx + tap * g_ext[b, pl.ds(8 + k, length), :]
            before = before + tap * g_ext[b, pl.ds(k, 8), :]
        bx_ref[b] = bx
        before_ref[b] = before
    sums[7] = sums[7] * (DECAY_SCALE * par[NEG_SIG : NEG_SIG + 1])
    for n in range(8):
        small_ref[pl.ds(n, 1), :] = sums[n]
    blocks_ref[0] = blocks[0].astype(blocks_ref.dtype)
    blocks_ref[1] = blocks[1].astype(blocks_ref.dtype)


def recurrent_backward(tprod, tsum, leaving, prod, total, state_in, coef, r, i, conv_low, x_branch, halo, masks, params, blocks):
    rows, length, units = tprod.shape
    full = head_spec(rows, length)
    edge = head_spec(rows, 8)
    return pl.pallas_call(
        backward_kernel,
        grid=(units // HEAD_W,),
        in_specs=[
            full, full, edge, full, full, edge, full, full, full, full, full, edge,
            pl.BlockSpec((rows, length, 8), lambda h: (0, 0, 0)),
            pl.BlockSpec((PARAM_ROWS, HEAD_W), lambda h: (0, h)),
            pl.BlockSpec((2, HEAD_W, HEAD_W), lambda h: (0, 0, h)),
        ],
        out_specs=[
            full,
            edge,
            pl.BlockSpec((8, HEAD_W), lambda h: (0, h)),
            pl.BlockSpec((2, HEAD_W, HEAD_W), lambda h: (0, 0, h)),
        ],
        out_shape=[
            jax.ShapeDtypeStruct((rows, length, units), F32),
            jax.ShapeDtypeStruct((rows, 8, units), F32),
            jax.ShapeDtypeStruct((8, units), F32),
            jax.ShapeDtypeStruct((2, HEAD_W, units), BF16),
        ],
        scratch_shapes=[
            pltpu.VMEM((rows, length + 8, HEAD_W), F32),
            pltpu.VMEM((rows, length + 8, HEAD_W), F32),
            pltpu.VMEM((rows, length + 16, HEAD_W), F32),
        ],
        compiler_params=pltpu.CompilerParams(vmem_limit_bytes=48 * 1024 * 1024),
        cost_estimate=cost(),
        name="recurrent_backward",
    )(tprod, tsum, leaving, prod, total, state_in, coef, r, i, conv_low, x_branch, halo, masks, params, blocks)


TILE = 256


def tokens_spec(columns, tiles, first):
    return pl.BlockSpec((TILE, columns), lambda m: ((m + first) % tiles, 0))


def held(rows, columns, at=0):
    return pl.BlockSpec((rows, columns), lambda m: (0, at), pipeline_mode=pl.Buffered(1))


def half_specs(columns, tiles):
    mid = tiles // 2
    return [
        pl.BlockSpec((TILE, columns), lambda m: (jnp.maximum(m - mid, 0), 0)),
        pl.BlockSpec((TILE, columns), lambda m: (jnp.minimum(m, mid - 1), 0)),
    ]


def store_half(first_ref, second_ref, tiles, value):
    m = pl.program_id(0)

    @pl.when(m < tiles // 2)
    def _():
        second_ref[...] = value

    @pl.when(m >= tiles // 2)
    def _():
        first_ref[...] = value


def feed_params():
    return pltpu.CompilerParams(vmem_limit_bytes=56 * 1024 * 1024)


def cost():
    return pl.CostEstimate(flops=1, bytes_accessed=1, transcendentals=0)


def feed_forward(pieces, w_feed):
    width = pieces[0].shape[1]
    share = w_feed.shape[1] // 3
    part = TILE // 2
    halves = []
    for n, piece in enumerate(pieces):
        halves += [(n, at) for at in range(0, piece.shape[0], part)]
    tiles = len(halves) // 2
    count = tiles * TILE

    def body(*refs):
        xs, (w_ref, all_ref, hidden_ref, by_gate_ref, by_up_ref, held_x, sems) = refs[: len(pieces)], refs[len(pieces) :]
        m = pl.program_id(0)

        def fetch(tile, slot):
            for at in range(tiles):

                @pl.when(tile == at)
                def _():
                    for h in range(2):
                        n, row = halves[2 * at + h]
                        pltpu.make_async_copy(
                            xs[n].at[pl.ds(row, part)], held_x.at[slot, pl.ds(h * part, part)], sems.at[slot, h]
                        ).start()

        @pl.when(m == 0)
        def _():
            fetch(0, 0)

        @pl.when(m + 1 < tiles)
        def _():
            fetch(m + 1, (m + 1) % 2)

        slot = m % 2
        for h in range(2):
            pltpu.make_async_copy(
                xs[0].at[pl.ds(0, part)], held_x.at[slot, pl.ds(h * part, part)], sems.at[slot, h]
            ).wait()
        x = held_x[slot]
        all_ref[...] = x
        value, slope = gelu_pair(dot(x, w_ref[:, :share], ((1,), (0,))))
        up = dot(x, w_ref[:, share:], ((1,), (0,)))
        hidden_ref[...] = (value * up).astype(BF16)
        by_gate_ref[...] = up * slope
        by_up_ref[...] = value

    tile = tokens_spec(share, tiles, 0)
    return pl.pallas_call(
        body,
        grid=(tiles,),
        in_specs=[pl.BlockSpec(memory_space=pl.ANY)] * len(pieces) + [held(width, 2 * share)],
        out_specs=[tokens_spec(width, tiles, 0)] + [tile] * 3,
        out_shape=[
            jax.ShapeDtypeStruct((count, width), BF16),
            jax.ShapeDtypeStruct((count, share), BF16),
            jax.ShapeDtypeStruct((count, share), F32),
            jax.ShapeDtypeStruct((count, share), F32),
        ],
        scratch_shapes=[pltpu.VMEM((2, TILE, width), BF16), pltpu.SemaphoreType.DMA((2, 2))],
        compiler_params=feed_params(),
        cost_estimate=cost(),
        name="feed_forward",
    )(*pieces, w_feed)


def feed_backward(feed_grad, by_gate, by_up, w_feed):
    count, width = feed_grad.shape
    share = w_feed.shape[1] // 3
    tiles = count // TILE
    mid = tiles // 2

    def body(fg_ref, gate_ref, up_ref, wd_ref, we_ref, low_ref, first_ref, second_ref):
        grad = dot(fg_ref[...], wd_ref[...], ((1,), (0,)))
        gate = (grad * gate_ref[...]).astype(BF16)
        up = (grad * up_ref[...]).astype(BF16)
        low_ref[:, :share] = gate
        low_ref[:, share:] = up
        terms = dot(gate, we_ref[:, :share], ((1,), (1,))) + dot(up, we_ref[:, share:], ((1,), (1,)))
        store_half(first_ref, second_ref, tiles, terms.astype(BF16))

    tile = tokens_spec(share, tiles, mid)
    return pl.pallas_call(
        body,
        grid=(tiles,),
        in_specs=[tokens_spec(width, tiles, mid), tile, tile, held(width, share, 2), held(width, 2 * share)],
        out_specs=[tokens_spec(2 * share, tiles, mid)] + half_specs(width, tiles),
        out_shape=[
            jax.ShapeDtypeStruct((count, 2 * share), BF16),
            jax.ShapeDtypeStruct((count // 2, width), BF16),
            jax.ShapeDtypeStruct((count // 2, width), BF16),
        ],
        compiler_params=feed_params(),
        cost_estimate=cost(),
        name="feed_backward",
    )(feed_grad, by_gate, by_up, w_feed, w_feed)


def feed_down(hidden, w_feed):
    count, share = hidden.shape
    width = w_feed.shape[0]
    tiles = count // TILE

    def body(h_ref, w_ref, first_ref, second_ref):
        store_half(first_ref, second_ref, tiles, dot(h_ref[...], w_ref[...], ((1,), (1,))).astype(BF16))

    return pl.pallas_call(
        body,
        grid=(tiles,),
        in_specs=[tokens_spec(share, tiles, tiles // 2), held(width, share, 2)],
        out_specs=half_specs(width, tiles),
        out_shape=[jax.ShapeDtypeStruct((count // 2, width), BF16)] * 2,
        compiler_params=feed_params(),
        cost_estimate=cost(),
        name="feed_down",
    )(hidden, w_feed)


def weight_grad(x, grad, into=None, at=0, blocks=1):
    count, width = x.shape
    columns = grad.shape[1]
    deep, wide = 512 if count > 1024 else width // 2, columns // blocks

    def body(x_ref, g_ref, *rest):
        rest[-1][...] = dot(x_ref[...], g_ref[...], ((0,), (0,))).astype(BF16)

    return pl.pallas_call(
        body,
        grid=(width // deep,),
        in_specs=[
            pl.BlockSpec((count, deep), lambda m: (0, m)),
            pl.BlockSpec((count, wide), lambda m: (0, at), pipeline_mode=pl.Buffered(1)),
        ]
        + ([] if into is None else [pl.BlockSpec(memory_space=pl.ANY)]),
        out_specs=pl.BlockSpec((deep, wide), lambda m: (m, at)),
        out_shape=jax.ShapeDtypeStruct((width, columns), BF16),
        input_output_aliases={} if into is None else {2: 0},
        compiler_params=feed_params(),
        cost_estimate=cost(),
        name="weight_grad",
    )(x, grad, *([] if into is None else [into]))


def unit_terms(pairs, order):
    count = pairs[0][0].shape[0] // 2
    units, width = pairs[0][0].shape[1], pairs[0][1].shape[0]
    refs = 2 * len(pairs)

    def body(order_ref, *rest):
        total = dot(rest[0][...], rest[1][...], ((1,), (1,)))
        for n in range(2, refs, 2):
            total = total + dot(rest[n][...], rest[n + 1][...], ((1,), (1,)))
        for n in range(2):

            @pl.when(pl.program_id(0) == n)
            def _():
                rest[refs + n][...] = total

    rows = pl.BlockSpec((count, units), lambda n, order_ref: (order_ref[n], 0))
    weights = pl.BlockSpec((width, units), lambda n, order_ref: (0, 0), pipeline_mode=pl.Buffered(1))
    return pl.pallas_call(
        body,
        grid_spec=pltpu.PrefetchScalarGridSpec(
            num_scalar_prefetch=1,
            grid=(2,),
            in_specs=[rows, weights] * len(pairs),
            out_specs=[pl.BlockSpec((count, width), lambda n, order_ref: (0, 0))] * 2,
        ),
        out_shape=[jax.ShapeDtypeStruct((count, width), F32)] * 2,
        compiler_params=feed_params(),
        cost_estimate=cost(),
        name="unit_terms",
    )(order, *[v for pair in pairs for v in pair])


ORDER = (1, 3, 2, 0)


def weight_grad_parts(x, grad, places, extra=None):
    count, width = x.shape
    columns = grad.shape[1]
    rows, cols = width // SQUARE, columns // 2
    more = 0 if extra is None else extra.shape[0] // SQUARE
    each = rows + more

    def body(places_ref, x_ref, g_ref, *rest):
        left_ref, right_ref, two_ref, one_ref, own_left, own_right = rest[-6:]
        targets = [
            ((left_ref, 0), (one_ref, 0)),
            ((left_ref, each), (right_ref, 0)),
            ((two_ref, 0), (right_ref, each)),
            ((own_left, 0), (own_right, 0)),
        ]
        value = dot(x_ref[...], g_ref[...], ((0,), (0,))).astype(BF16)
        for n in range(SQUARE):

            @pl.when(pl.program_id(0) == n)
            def _():
                for h, (ref, at) in enumerate(targets[n]):
                    ref[pl.ds(at, rows), :] = value[:, h * cols : (h + 1) * cols]
                    if more:
                        ref[pl.ds(at + rows, more), :] = rest[0][:, h * cols : (h + 1) * cols]

    sizes = [2 * each, 2 * each] + [each] * 4
    return pl.pallas_call(
        body,
        grid_spec=pltpu.PrefetchScalarGridSpec(
            num_scalar_prefetch=1,
            grid=(SQUARE,),
            in_specs=[
                pl.BlockSpec((count, rows), lambda n, places_ref: (0, places_ref[n])),
                pl.BlockSpec((count, columns), lambda n, places_ref: (0, 0)),
            ]
            + ([pl.BlockSpec((more, columns), lambda n, places_ref: (places_ref[n], 0))] if more else []),
            out_specs=[pl.BlockSpec((size, cols), lambda n, places_ref: (0, 0)) for size in sizes],
        ),
        out_shape=[jax.ShapeDtypeStruct((size, cols), BF16) for size in sizes],
        compiler_params=feed_params(),
        cost_estimate=cost(),
        name="weight_grad_parts",
    )(places, x, grad, *([extra] if more else []))


def carried(own, axis, step):
    near_map = shifted(own, axis, step)
    both = jnp.stack([near_map[0] * own[0], own[0] * near_map[1] + own[1]])
    result, reach = near_map, 2
    while reach < lax.axis_size(axis):
        far = shifted(both, axis, step * reach)
        result = jnp.stack([result[0] * far[0], result[0] * far[1] + result[1]])
        both = jnp.stack([both[0] * far[0], both[0] * far[1] + both[1]])
        reach *= 2
    return result[1]


def cross(x, axis, r):
    return lax.ppermute(x, axis, [(i, i ^ r) for i in range(lax.axis_size(axis))])


def total_over(x, axis):
    r = 1
    while r < lax.axis_size(axis):
        x = x + cross(x, axis, r)
        r *= 2
    return x


def after(x, done):
    return lax.optimization_barrier((x, done))


SQUARE = 4


def token_axes():
    return ("fsdp", "ctx") if lax.axis_size("fsdp") == SQUARE else ("ctx", "fsdp")


def together(*values):
    return lax.optimization_barrier(values)


def place(blocks, axis):
    me = lax.axis_index(axis)
    first = blocks[0]
    whole = jnp.zeros((len(blocks),) + first.shape, first.dtype)
    for r, block in enumerate(blocks):
        at = 0
        for piece in block if isinstance(block, list) else [block]:
            whole = lax.dynamic_update_slice(whole, piece[None], (me ^ r, at) + (0,) * (piece.ndim - 1))
            at += piece.shape[0]
    return whole


def near_blocks(x, axis):
    return list(together(cross(x, axis, 1), cross(x, axis, 2)))


def far_block(got, axis):
    mid = got[0].shape[0] // 2
    halves = together(got[0][:mid], got[1][mid:])
    return [cross(halves[0], axis, 2), cross(halves[1], axis, 1)]


def near(x, axis):
    got = near_blocks(x, axis)
    return [x] + got + [far_block(got, axis)]


def low(v):
    return v.astype(BF16)


def wide(v):
    return v.astype(F32)


def near_send(parts, axis):
    return together(cross(parts[0], axis, 1), cross(parts[1], axis, 2))


def near_middle(parts, got):
    rows = got[0].shape[0] // 2
    return together(low(wide(parts[2]) + wide(got[0][rows:])), low(wide(parts[3]) + wide(got[1][:rows])))


def near_second(sums, axis):
    return together(cross(sums[0], axis, 2), cross(sums[1], axis, 1))


def near_last(parts, got, more):
    rows = got[0].shape[0] // 2
    left = wide(parts[4]) + wide(got[0][:rows]) + wide(more[0])
    right = wide(parts[5]) + wide(got[1][rows:]) + wide(more[1])
    return jnp.concatenate([left, right], axis=1)


def gather_in_turn(arrays, ready):
    if lax.axis_size("fsdp") != SQUARE:
        return [lax.all_gather(x, "fsdp", axis=0) for x in arrays], ready
    results = []
    for x in arrays:
        if results:
            x, results[-1] = together(x, results[-1])
        got = near_blocks(x, "fsdp")
        if not results:
            got, ready = together(got, ready)
        results.append([x] + got + [far_block(got, "fsdp")])
    return results, ready


def rows_of(blocks, start, stop):
    if lax.axis_size("fsdp") != SQUARE:
        return blocks[:, :, start:stop].reshape(-1, blocks.shape[-1])
    cut = lambda v: v[:, start:stop]
    whole = place([[cut(v) for v in block] if isinstance(block, list) else cut(block) for block in blocks], "fsdp")
    return whole.reshape(-1, whole.shape[-1])


def token_pieces(x):
    axis = token_axes()[0]
    theirs = swap(x, "tp")
    got = near_blocks(x, axis)
    far = far_block(got, axis)
    got_theirs = [swap(v, "tp") for v in got]
    far_theirs = [swap(v, "tp") for v in far]
    return [got[0], *far, got[1], x, got_theirs[0], *far_theirs, got_theirs[1], theirs]


def token_parts(first, theirs):
    rows, cols = first.shape[0] // SQUARE, first.shape[1] // 2

    def part(start, stop, half):
        here = (slice(start * rows, stop * rows), slice(half * cols, (half + 1) * cols))
        return low(wide(first[here]) + wide(theirs[here]))

    return [part(0, 2, 0), part(1, 3, 1)], [part(2, 3, 0), part(0, 1, 1), part(3, 4, 0), part(3, 4, 1)]


def trade(pieces):
    axis = token_axes()[0]
    me = lax.axis_index(axis)
    return place([pieces(me)] + [cross(pieces(me ^ r), axis, r) for r in range(1, SQUARE)], axis)


def gather_feed(local):
    _, along = token_axes()
    whole = lax.all_gather(local, along, axis=1 if along == "ctx" else 0, tiled=True)
    return whole.reshape(-1, local.shape[2])


def scatter_feed(grad):
    _, along = token_axes()
    if along == "ctx":
        grad = grad.reshape(SQUARE, -1, grad.shape[1])
        return lax.psum_scatter(grad, along, scatter_dimension=1, tiled=True)
    part = lax.psum_scatter(grad, along, scatter_dimension=0, tiled=True)
    return part.reshape(SQUARE, -1, grad.shape[1])


def rms(values):
    return lax.rsqrt(jnp.mean(values * values, axis=-1, keepdims=True) + EPSILON)


def rms_back(values, inverse, gain, grad):
    u = grad * gain
    inner = jnp.mean(values * u, axis=-1, keepdims=True)
    gain_grad = jnp.sum(grad * values * inverse, axis=0)
    return inverse * u - values * (inverse * inverse * inverse) * inner, gain_grad


def shards(
    block_input, segments, token_mask, cotangent, norm_gains, conv_taps, conv_offset, gate_offset,
    decay_logit, intake, gate_blocks, outlet, expand, contract,
):
    rows, length, width = block_input.shape
    depth = intake.shape[0]
    units = intake.shape[2]
    gate_rows = gate_blocks.shape[0]
    hidden_units = contract.shape[1]
    tokens = rows * length
    ctx, tp = lax.axis_size("ctx"), lax.axis_size("tp")
    mine = lax.axis_index("tp")
    half = tokens // tp
    share = -(-hidden_units // (SQUARE * 256)) * 256
    padding = SQUARE * share - hidden_units

    def own(x):
        return lax.dynamic_slice_in_dim(x, mine * half, half, 0)

    def other(x):
        return lax.dynamic_slice_in_dim(x, (1 - mine) * half, half, 0)

    def join(x):
        theirs = swap(x, "tp")
        return jnp.concatenate(
            [jnp.where(mine == 0, x, theirs), jnp.where(mine == 0, theirs, x)], axis=0
        )

    first = jnp.concatenate([intake[:, 1], gate_blocks.reshape(2 * gate_rows, units)], axis=0)
    first = lax.all_gather(first, "ctx", axis=0)
    second = lax.all_gather(jnp.concatenate([intake[:, 0], outlet], axis=0), "ctx", axis=0)

    def cut(w):
        w = jnp.pad(w, ((0, 0), (0, padding)))
        return lambda p: lax.dynamic_slice_in_dim(w, p * share, share, 1)

    down, gate_in, up_in = cut(contract), cut(expand[:, 0]), cut(expand[:, 1])
    local_feed = trade(lambda p: jnp.concatenate([gate_in(p), up_in(p), down(p)], axis=1))

    mask_rows = token_mask.astype(F32).reshape(tokens, 1)
    out_grad = own(cotangent.reshape(tokens, width)).astype(F32) * own(mask_rows)
    local_feed_grad = out_grad.astype(BF16)

    (got_first, got_gelu, got_outlet), local_feed = gather_in_turn(
        [first, second[:, :depth], second[:, depth:]], local_feed
    )
    w_feed = gather_feed(local_feed)
    w_branch = rows_of(got_first, 0, depth)
    blocks = rows_of(got_first, depth, first.shape[1]).reshape(HEAD_W, 2, units).transpose(1, 0, 2)
    w_gelu = rows_of(got_gelu, 0, depth)
    w_outlet = rows_of(got_outlet, 0, depth)

    seg_next = segments + 1
    seg_before = shifted(seg_next[:, -3:], "ctx", 1)
    seg_ext = jnp.concatenate([seg_before, seg_next], axis=1)
    masks = jnp.stack(
        [(seg_ext[:, 3 - k : 3 - k + length] == seg_next).astype(F32) for k in (1, 1, 2, 3)]
        + [jnp.zeros(segments.shape, F32)] * 4,
        axis=2,
    )
    params = jnp.concatenate(
        [
            conv_taps,
            conv_offset[None],
            gate_offset,
            jax.nn.softplus(-decay_logit)[None],
            jax.nn.sigmoid(-decay_logit)[None],
            jnp.zeros((PARAM_ROWS - 9, units), F32),
        ],
        axis=0,
    )

    x = block_input.reshape(tokens, width).astype(F32)
    inverse_one = rms(x)
    normed = (x * inverse_one * norm_gains[0]).astype(BF16)
    x_branch = dot(normed, w_branch, ((1,), (0,))).astype(BF16).reshape(rows, length, units)
    gelu_in = dot(normed, w_gelu, ((1,), (0,))).reshape(rows, length, units)
    x_before = shifted(x_branch[:, -3:], "ctx", 1)
    halo = jnp.pad(x_before, ((0, 0), (5, 0), (0, 0))).astype(F32)
    conv_low, r, i, coef, prod, total = recurrent_forward(x_branch, halo, masks, params, blocks)
    ends = jnp.stack([prod[:, -1], total[:, -1]])
    entering = carried(ends, "ctx", 1)
    state_in = jnp.broadcast_to(entering[:, None], (rows, 8, units))
    states = total + prod * entering[:, None]
    recurrent = (states * jax.nn.gelu(gelu_in, approximate=True)).astype(BF16).reshape(tokens, units)

    sent = swap(dot(other(recurrent), w_outlet, ((1,), (1,))), "tp")
    branch = dot(own(recurrent), w_outlet, ((1,), (1,))) + sent
    residual = own(x) + branch
    inverse_two = rms(residual)
    normed_two = token_pieces((residual * inverse_two * norm_gains[1]).astype(BF16))

    def to_owners(part):
        return trade(lambda p: lax.dynamic_index_in_dim(part, p, 0, keepdims=False))

    local_feed_grad, normed_two = together(local_feed_grad, normed_two)
    feed_grad = jnp.concatenate(token_pieces(local_feed_grad), axis=0)
    normed_two, hidden, by_gate, by_up = feed_forward(normed_two, w_feed)
    down_grad = weight_grad(feed_grad, hidden)
    by_gate, down_grad = after(by_gate, down_grad)
    down_part = scatter_feed(down_grad)
    expand_low, n2g_own, n2g_other = feed_backward(feed_grad, by_gate, by_up, w_feed)

    group = token_axes()[0]
    theirs = swap(n2g_other, "tp")
    parts, kept = token_parts(n2g_own, theirs)
    parts, expand_low = after(parts, expand_low)
    got = near_send(parts, group)
    parts = parts + kept
    expand_all = weight_grad(normed_two, expand_low)
    got, expand_all = after(got, expand_all)
    sums, hidden = after(near_middle(parts, got), hidden)
    more = near_second(sums, group)
    feed_own, feed_other = feed_down(hidden, w_feed)
    more, (feed_own, feed_other) = after(more, (feed_own, feed_other))
    normed_two_grad = near_last(parts, got, more)
    expand_all, down_part = after(expand_all, down_part)
    expand_part = scatter_feed(expand_all)
    feed_theirs = swap(feed_other, "tp")

    norm_part, gain_two = rms_back(residual, inverse_two, norm_gains[1], normed_two_grad)
    residual_grad = out_grad + norm_part
    branch_grad = join(residual_grad.astype(BF16))

    square = lax.axis_size("fsdp") == SQUARE
    places = lax.axis_index("fsdp").astype(jnp.int32) ^ jnp.array(ORDER, jnp.int32)
    feed_parts, feed_kept = token_parts(feed_own, feed_theirs)
    feed_parts, branch_grad = after(feed_parts, branch_grad)
    feed_got = near_send(feed_parts, group)
    feed_parts = feed_parts + feed_kept
    if square:
        outlet_parts = weight_grad_parts(branch_grad, recurrent, places)
    else:
        outlet_parts = weight_grad(branch_grad, recurrent)
    outlet_parts, branch_grad = after(outlet_parts, branch_grad)
    outlet_got = near_send(outlet_parts, "fsdp") if square else outlet_parts
    rec_grad = dot(branch_grad, w_outlet, ((1,), (0,))).reshape(rows, length, units)
    gelu_grad, tprod, tsum = recurrent_adjoint(rec_grad, gelu_in, coef, prod, total, state_in)
    gelu_low = gelu_grad.reshape(tokens, units)
    if square:
        gelu_parts = weight_grad_parts(normed, gelu_low, places)
    else:
        gelu_parts = weight_grad(normed, gelu_low)
    feed_got, outlet_got, gelu_parts, tprod, tsum = together(feed_got, outlet_got, gelu_parts, tprod, tsum)
    feed_sums = near_middle(feed_parts, feed_got)
    if square:
        outlet_sums, gelu_parts, tprod = together(near_middle(outlet_parts, outlet_got), gelu_parts, tprod)
        outlet_more, gelu_got = near_second(outlet_sums, "fsdp"), near_send(gelu_parts, "fsdp")
    heads = jnp.stack([coef[:, 0] * tprod[:, 0], coef[:, 0] * tsum[:, 0]])
    leaving = carried(heads, "ctx", -1)
    leaving = jnp.broadcast_to(leaving[:, None], (rows, 8, units))
    branch_x, before, small, blocks_grad = recurrent_backward(
        tprod, tsum, leaving, prod, total, state_in, coef, r, i, conv_low, x_branch, halo, masks, params, blocks
    )
    from_next = shifted(before[:, 5:], "ctx", -1)
    branch_x = branch_x + jnp.pad(from_next, ((0, 0), (length - 3, 0), (0, 0)))
    branch_low = branch_x.astype(BF16).reshape(tokens, units)
    blocks_rows = blocks_grad.transpose(1, 0, 2).reshape(2 * HEAD_W, units)
    if square:
        branch_parts = weight_grad_parts(normed, branch_low, places, blocks_rows)
        gelu_got, outlet_more, branch_parts, branch_low = together(gelu_got, outlet_more, branch_parts, branch_low)
        gelu_sums, branch_parts, branch_low = together(near_middle(gelu_parts, gelu_got), branch_parts, branch_low)
        gelu_more, branch_got = near_second(gelu_sums, "fsdp"), near_send(branch_parts, "fsdp")
        outlet_part = low(near_last(outlet_parts, outlet_got, outlet_more))
    else:
        branch_parts = weight_grad(normed, branch_low)
        outlet_part, gelu_part = [
            lax.psum_scatter(v, "fsdp", scatter_dimension=0, tiled=True) for v in (outlet_got, gelu_parts)
        ]
        branch_got = branch_parts
    theirs, ours = unit_terms(
        [(branch_low, w_branch), (gelu_low, w_gelu)], jnp.stack([1 - mine, mine]).astype(jnp.int32)
    )
    def scatter_ctx(v):
        return lax.psum_scatter(v, "ctx", scatter_dimension=0, tiled=False)

    outlet_part, expand_part = after(outlet_part, expand_part)
    outlet_part = scatter_ctx(outlet_part.reshape(ctx, depth, units))
    if square:
        gelu_more, branch_got, theirs, ours, outlet_part = together(gelu_more, branch_got, theirs, ours, outlet_part)
        gelu_part = low(near_last(gelu_parts, gelu_got, gelu_more))
        late_sums, gelu_part = after(near_middle(branch_parts, branch_got), gelu_part)
        late_more = near_second(late_sums, "fsdp")
    else:
        gelu_part, outlet_part = after(gelu_part, outlet_part)
    gelu_part = scatter_ctx(gelu_part.reshape(ctx, depth, units))
    if square:
        late = low(near_last(branch_parts, branch_got, late_more))
        late = [late[: ctx * depth], late[ctx * depth :]]
    else:
        late = [lax.psum_scatter(v, "fsdp", scatter_dimension=0, tiled=True) for v in (branch_got, blocks_rows)]
    late = jnp.concatenate([v.reshape(ctx, -1, units) for v in late], axis=1)
    normed_grad = ours + swap(theirs, "tp")
    norm_part, gain_one = rms_back(own(x), own(inverse_one), norm_gains[0], normed_grad)
    input_own = residual_grad + norm_part
    late, gelu_part, expand_part, down_part, input_own, gain_one, feed_sums = together(
        late, gelu_part, expand_part, down_part, input_own, gain_one, feed_sums
    )
    late = wide(scatter_ctx(late))
    input_grad = join(input_own).reshape(rows, length, width)
    feed_out = near_last(feed_parts, feed_got, near_second(feed_sums, group))
    block_output = join(low(residual + feed_out)).reshape(rows, length, width)

    down_part = to_owners(down_part)
    expand_part = to_owners(expand_part)

    def columns(part, n):
        return jnp.concatenate([part[p, :, n * share : (n + 1) * share] for p in range(SQUARE)], axis=1)[
            :, :hidden_units
        ].astype(F32)

    contract_grad = columns(down_part, 0)
    expand_grad = jnp.stack([columns(expand_part, 0), columns(expand_part, 1)], axis=1)

    gains = jnp.concatenate([gain_one, gain_two]).reshape(-1, units)
    small = total_over(total_over(jnp.concatenate([small, gains], axis=0), "fsdp"), "ctx")
    gains = total_over(small[8:], "tp").reshape(2, width)
    return (
        block_output,
        input_grad,
        gains,
        small[0:4],
        small[4],
        small[5:7],
        small[7],
        jnp.stack([wide(gelu_part), late[:depth]], axis=1),
        late[depth:].reshape(gate_rows, 2, units),
        wide(outlet_part),
        expand_grad,
        contract_grad,
    )


def solution(mesh):
    placed = (
        P("fsdp", "ctx", None),
        P("fsdp", "ctx"),
        P("fsdp", "ctx"),
        P("fsdp", "ctx", None),
        P(),
        P(None, "tp"),
        P("tp"),
        P(None, "tp"),
        P("tp"),
        P(("fsdp", "ctx"), None, "tp"),
        P(("fsdp", "ctx"), None, "tp"),
        P(("fsdp", "ctx"), "tp"),
        P(("fsdp", "ctx"), None, "tp"),
        P(("fsdp", "ctx"), "tp"),
    )
    return jax.shard_map(
        shards,
        mesh=mesh,
        in_specs=placed,
        out_specs=(
            P("fsdp", "ctx", None),
            P("fsdp", "ctx", None),
            P(),
            P(None, "tp"),
            P("tp"),
            P(None, "tp"),
            P("tp"),
            P(("fsdp", "ctx"), None, "tp"),
            P(("fsdp", "ctx"), None, "tp"),
            P(("fsdp", "ctx"), "tp"),
            P(("fsdp", "ctx"), None, "tp"),
            P(("fsdp", "ctx"), "tp"),
        ),
        check_vma=False,
    )
```

```python
import jax
import jax.numpy as jnp
from jax import lax
from jax.experimental import pallas as pl
from jax.experimental.pallas import tpu as pltpu
from jax.sharding import PartitionSpec as P

HEAD_W = 256
LANES = 128
CHUNKS = 8

EPSILON = 1e-06
DECAY_SCALE = 8.0
GELU_C = 0.7978845608028654
GELU_A = 0.044715

F32 = jnp.float32
BF16 = jnp.bfloat16

TAP0, OFFSET, RATE_OFF, INLET_OFF, SOFTPLUS, NEG_SIG, PARAM_ROWS = 0, 4, 5, 6, 7, 8, 16


def shifted(x, axis, by):
    length = lax.axis_size(axis)
    pairs = [(i, i + by) for i in range(length) if 0 <= i + by < length]
    return lax.ppermute(x, axis, pairs)


def swap(x, axis):
    length = lax.axis_size(axis)
    return lax.ppermute(x, axis, [(i, (i + 1) % length) for i in range(length)])


def gelu_pair(v):
    t = jnp.tanh(GELU_C * (v + GELU_A * v * v * v))
    value = 0.5 * v * (1.0 + t)
    slope = 0.5 * (1.0 + t) + 0.5 * v * (1.0 - t * t) * GELU_C * (1.0 + 3.0 * GELU_A * v * v)
    return value, slope


def one_minus_exp(x):
    s = 1.0 + x / 7.0
    for n in (6.0, 5.0, 4.0, 3.0, 2.0):
        s = 1.0 + x / n * s
    return jnp.where(x > -0.5, -x * s, 1.0 - jnp.exp(x))


def sigmoid(v):
    return 1.0 / (1.0 + jnp.exp(-v))


def dot(a, b, dims):
    return lax.dot_general(a, b, (dims, ((), ())), preferred_element_type=F32)


def lane_scan(load_a, load_b, store, length, reverse):
    steps = length // CHUNKS
    prod = jnp.ones((CHUNKS, LANES), F32)
    total = jnp.zeros((CHUNKS, LANES), F32)
    for n in range(steps):
        s = steps - 1 - n if reverse else n
        coef = load_a(s)
        total = coef * total + load_b(s)
        prod = coef * prod
        store(s, prod, total)
    return prod, total


def chunk_carries(prod, total, reverse):
    order = range(CHUNKS - 1, -1, -1) if reverse else range(CHUNKS)
    run_p = jnp.ones((1, LANES), F32)
    run_s = jnp.zeros((1, LANES), F32)
    carries = [None] * CHUNKS
    for c in order:
        carries[c] = (run_p, run_s)
        run_s = prod[c : c + 1] * run_s + total[c : c + 1]
        run_p = prod[c : c + 1] * run_p
    return carries


def sweep(a_scr, b_scr, p_scr, s_scr, prod_ref, sum_ref, rows, length, reverse, shift):
    steps = length // CHUNKS
    for b in range(rows):
        for j in range(HEAD_W // LANES):
            av, bv, pv, sv = (a_scr.at[b, j], b_scr.at[b, j], p_scr.at[b, j], s_scr.at[b, j])

            def store(s, prod, total):
                pv[pl.ds(s, CHUNKS, stride=steps), :] = prod
                sv[pl.ds(s, CHUNKS, stride=steps), :] = total

            prod, total = lane_scan(
                lambda s: av[pl.ds(s + shift, CHUNKS, stride=steps), :],
                lambda s: bv[pl.ds(s, CHUNKS, stride=steps), :],
                store,
                length,
                reverse,
            )
            carries = chunk_carries(prod, total, reverse)
            lanes = slice(j * LANES, (j + 1) * LANES)
            for c in range(CHUNKS):
                here = slice(c * steps, (c + 1) * steps)
                p = pv[here, :]
                prod_ref[b, here, lanes] = p * carries[c][0]
                sum_ref[b, here, lanes] = sv[here, :] + p * carries[c][1]


def to_lanes(ref, b, at, value):
    for j in range(HEAD_W // LANES):
        ref[b, j, pl.ds(at, value.shape[0]), :] = value[:, j * LANES : (j + 1) * LANES]


def forward_kernel(
    x_ref, halo_ref, mask_ref, par_ref, w_ref,
    conv_ref, r_ref, i_ref, a_ref, prod_ref, sum_ref,
    ext, a_scr, b_scr, p_scr, s_scr,
):
    rows, length, _ = x_ref.shape
    par = par_ref[...]
    w0, w1 = w_ref[0], w_ref[1]
    for b in range(rows):
        ext[b, pl.ds(0, 8), :] = halo_ref[b]
        ext[b, pl.ds(8, length), :] = x_ref[b].astype(F32)
        conv = ext[b, pl.ds(8, length), :] * par[TAP0 : TAP0 + 1] + par[OFFSET : OFFSET + 1]
        for k in range(1, 4):
            match = mask_ref[b, :, k : k + 1]
            conv = conv + par[TAP0 + k : TAP0 + k + 1] * ext[b, pl.ds(8 - k, length), :] * match
        conv_low = conv.astype(BF16)
        conv_ref[b] = conv_low
        conv = conv_low.astype(F32)
        r = sigmoid(dot(conv_low, w0, ((1,), (0,))) + par[RATE_OFF : RATE_OFF + 1])
        i = sigmoid(dot(conv_low, w1, ((1,), (0,))) + par[INLET_OFF : INLET_OFF + 1])
        r_ref[b] = r
        i_ref[b] = i
        log_keep = -DECAY_SCALE * r * par[SOFTPLUS : SOFTPLUS + 1]
        going = mask_ref[b, :, 0:1]
        a = jnp.exp(log_keep) * going
        a_ref[b] = a
        scale = jnp.where(going > 0.5, jnp.sqrt(one_minus_exp(2.0 * log_keep)), 1.0)
        to_lanes(a_scr, b, 0, a)
        to_lanes(b_scr, b, 0, i * conv * scale)
    sweep(a_scr, b_scr, p_scr, s_scr, prod_ref, sum_ref, rows, length, False, 0)


def head_spec(rows, length):
    return pl.BlockSpec((rows, length, HEAD_W), lambda h: (0, 0, h))


def recurrent_forward(x_branch, halo, masks, params, blocks):
    rows, length, units = x_branch.shape
    full = head_spec(rows, length)
    scan = pltpu.VMEM((rows, HEAD_W // LANES, length, LANES), F32)
    big = jax.ShapeDtypeStruct((rows, length, units), F32)
    return pl.pallas_call(
        forward_kernel,
        grid=(units // HEAD_W,),
        in_specs=[
            full,
            head_spec(rows, 8),
            pl.BlockSpec((rows, length, 8), lambda h: (0, 0, 0)),
            pl.BlockSpec((PARAM_ROWS, HEAD_W), lambda h: (0, h)),
            pl.BlockSpec((2, HEAD_W, HEAD_W), lambda h: (0, 0, h)),
        ],
        out_specs=[full] * 6,
        out_shape=[jax.ShapeDtypeStruct((rows, length, units), BF16)] + [big] * 5,
        scratch_shapes=[pltpu.VMEM((rows, length + 8, HEAD_W), F32), scan, scan, scan, scan],
        compiler_params=pltpu.CompilerParams(vmem_limit_bytes=48 * 1024 * 1024),
        cost_estimate=cost(),
        name="recurrent_forward",
    )(x_branch, halo, masks, params, blocks)


def adjoint_kernel(
    rg_ref, gelu_ref, a_ref, prod_ref, sum_ref, in_ref,
    gg_ref, tprod_ref, tsum_ref,
    a_scr, b_scr, p_scr, s_scr,
):
    rows, length, _ = rg_ref.shape
    for b in range(rows):
        states = sum_ref[b] + prod_ref[b] * in_ref[b, 0:1]
        value, slope = gelu_pair(gelu_ref[b])
        rg = rg_ref[b]
        gg_ref[b] = (rg * states * slope).astype(BF16)
        to_lanes(a_scr, b, 0, a_ref[b])
        to_lanes(a_scr, b, length, jnp.ones((8, HEAD_W), F32))
        to_lanes(b_scr, b, 0, rg * value)
    sweep(a_scr, b_scr, p_scr, s_scr, tprod_ref, tsum_ref, rows, length, True, 1)


def recurrent_adjoint(rec_grad, gelu_in, coef, prod, total, state_in):
    rows, length, units = rec_grad.shape
    full = head_spec(rows, length)
    scan = pltpu.VMEM((rows, HEAD_W // LANES, length, LANES), F32)
    longer = pltpu.VMEM((rows, HEAD_W // LANES, length + 8, LANES), F32)
    big = jax.ShapeDtypeStruct((rows, length, units), F32)
    return pl.pallas_call(
        adjoint_kernel,
        grid=(units // HEAD_W,),
        in_specs=[full] * 5 + [head_spec(rows, 8)],
        out_specs=[full] * 3,
        out_shape=[jax.ShapeDtypeStruct((rows, length, units), BF16), big, big],
        scratch_shapes=[longer, scan, scan, scan],
        compiler_params=pltpu.CompilerParams(vmem_limit_bytes=48 * 1024 * 1024),
        cost_estimate=cost(),
        name="recurrent_adjoint",
    )(rec_grad, gelu_in, coef, prod, total, state_in)


def backward_kernel(
    tprod_ref, tsum_ref, leave_ref, prod_ref, sum_ref, in_ref, a_ref, r_ref, i_ref, conv_ref,
    x_ref, halo_ref, mask_ref, par_ref, w_ref,
    bx_ref, before_ref, small_ref, blocks_ref,
    ext, st_ext, g_ext,
):
    rows, length, _ = tprod_ref.shape
    par = par_ref[...]
    w0, w1 = w_ref[0], w_ref[1]
    sums = [jnp.zeros((1, HEAD_W), F32) for _ in range(8)]
    blocks = [jnp.zeros((HEAD_W, HEAD_W), F32) for _ in range(2)]

    def add(n, value):
        sums[n] = sums[n] + jnp.sum(value, axis=0, keepdims=True)

    for b in range(rows):
        adjoint = tsum_ref[b] + tprod_ref[b] * leave_ref[b, 0:1]
        st_ext[b, pl.ds(0, 8), :] = in_ref[b]
        st_ext[b, pl.ds(8, length), :] = sum_ref[b] + prod_ref[b] * in_ref[b, 0:1]
        prev = st_ext[b, pl.ds(7, length), :]
        r, i, a = r_ref[b], i_ref[b], a_ref[b]
        conv_low = conv_ref[b]
        conv = conv_low.astype(F32)
        going = mask_ref[b, :, 0:1]
        log_keep = -DECAY_SCALE * r * par[SOFTPLUS : SOFTPLUS + 1]
        scale = jnp.where(going > 0.5, jnp.sqrt(one_minus_exp(2.0 * log_keep)), 1.0)
        log_grad = adjoint * prev * a - adjoint * i * conv * (a * a) / scale
        rate = log_grad * (-DECAY_SCALE * par[SOFTPLUS : SOFTPLUS + 1]) * r * (1.0 - r)
        spread = adjoint * scale
        inlet = spread * conv * i * (1.0 - i)
        add(5, rate)
        add(6, inlet)
        add(7, log_grad * r)
        rate_low = rate.astype(BF16)
        inlet_low = inlet.astype(BF16)
        grad = spread * i + dot(rate_low, w0, ((1,), (1,))) + dot(inlet_low, w1, ((1,), (1,)))
        blocks[0] = blocks[0] + dot(conv_low, rate_low, ((0,), (0,)))
        blocks[1] = blocks[1] + dot(conv_low, inlet_low, ((0,), (0,)))
        ext[b, pl.ds(0, 8), :] = halo_ref[b]
        ext[b, pl.ds(8, length), :] = x_ref[b].astype(F32)
        add(4, grad)
        add(0, grad * ext[b, pl.ds(8, length), :])
        bx = grad * par[TAP0 : TAP0 + 1]
        g_ext[b, pl.ds(0, 8), :] = jnp.zeros((8, HEAD_W), F32)
        g_ext[b, pl.ds(8 + length, 8), :] = jnp.zeros((8, HEAD_W), F32)
        before = jnp.zeros((8, HEAD_W), F32)
        for k in range(1, 4):
            masked = grad * mask_ref[b, :, k : k + 1]
            add(k, masked * ext[b, pl.ds(8 - k, length), :])
            g_ext[b, pl.ds(8, length), :] = masked
            tap = par[TAP0 + k : TAP0 + k + 1]
            bx = bx + tap * g_ext[b, pl.ds(8 + k, length), :]
            before = before + tap * g_ext[b, pl.ds(k, 8), :]
        bx_ref[b] = bx
        before_ref[b] = before
    sums[7] = sums[7] * (DECAY_SCALE * par[NEG_SIG : NEG_SIG + 1])
    for n in range(8):
        small_ref[pl.ds(n, 1), :] = sums[n]
    blocks_ref[0] = blocks[0].astype(blocks_ref.dtype)
    blocks_ref[1] = blocks[1].astype(blocks_ref.dtype)


def recurrent_backward(tprod, tsum, leaving, prod, total, state_in, coef, r, i, conv_low, x_branch, halo, masks, params, blocks):
    rows, length, units = tprod.shape
    full = head_spec(rows, length)
    edge = head_spec(rows, 8)
    return pl.pallas_call(
        backward_kernel,
        grid=(units // HEAD_W,),
        in_specs=[
            full, full, edge, full, full, edge, full, full, full, full, full, edge,
            pl.BlockSpec((rows, length, 8), lambda h: (0, 0, 0)),
            pl.BlockSpec((PARAM_ROWS, HEAD_W), lambda h: (0, h)),
            pl.BlockSpec((2, HEAD_W, HEAD_W), lambda h: (0, 0, h)),
        ],
        out_specs=[
            full,
            edge,
            pl.BlockSpec((8, HEAD_W), lambda h: (0, h)),
            pl.BlockSpec((2, HEAD_W, HEAD_W), lambda h: (0, 0, h)),
        ],
        out_shape=[
            jax.ShapeDtypeStruct((rows, length, units), F32),
            jax.ShapeDtypeStruct((rows, 8, units), F32),
            jax.ShapeDtypeStruct((8, units), F32),
            jax.ShapeDtypeStruct((2, HEAD_W, units), BF16),
        ],
        scratch_shapes=[
            pltpu.VMEM((rows, length + 8, HEAD_W), F32),
            pltpu.VMEM((rows, length + 8, HEAD_W), F32),
            pltpu.VMEM((rows, length + 16, HEAD_W), F32),
        ],
        compiler_params=pltpu.CompilerParams(vmem_limit_bytes=48 * 1024 * 1024),
        cost_estimate=cost(),
        name="recurrent_backward",
    )(tprod, tsum, leaving, prod, total, state_in, coef, r, i, conv_low, x_branch, halo, masks, params, blocks)


TILE = 256


def tokens_spec(columns, tiles, first):
    return pl.BlockSpec((TILE, columns), lambda m: ((m + first) % tiles, 0))


def held(rows, columns, at=0):
    return pl.BlockSpec((rows, columns), lambda m: (0, at), pipeline_mode=pl.Buffered(1))


def half_specs(columns, tiles):
    mid = tiles // 2
    return [
        pl.BlockSpec((TILE, columns), lambda m: (jnp.maximum(m - mid, 0), 0)),
        pl.BlockSpec((TILE, columns), lambda m: (jnp.minimum(m, mid - 1), 0)),
    ]


def store_half(first_ref, second_ref, tiles, value):
    m = pl.program_id(0)

    @pl.when(m < tiles // 2)
    def _():
        second_ref[...] = value

    @pl.when(m >= tiles // 2)
    def _():
        first_ref[...] = value


def feed_params():
    return pltpu.CompilerParams(vmem_limit_bytes=56 * 1024 * 1024)


def cost():
    return pl.CostEstimate(flops=1, bytes_accessed=1, transcendentals=0)


def feed_forward(pieces, w_feed):
    width = pieces[0].shape[1]
    share = w_feed.shape[1] // 3
    part = TILE // 2
    halves = []
    for n, piece in enumerate(pieces):
        halves += [(n, at) for at in range(0, piece.shape[0], part)]
    tiles = len(halves) // 2
    count = tiles * TILE

    def body(*refs):
        xs, (w_ref, all_ref, hidden_ref, by_gate_ref, by_up_ref, held_x, sems) = refs[: len(pieces)], refs[len(pieces) :]
        m = pl.program_id(0)

        def fetch(tile, slot):
            for at in range(tiles):

                @pl.when(tile == at)
                def _():
                    for h in range(2):
                        n, row = halves[2 * at + h]
                        pltpu.make_async_copy(
                            xs[n].at[pl.ds(row, part)], held_x.at[slot, pl.ds(h * part, part)], sems.at[slot, h]
                        ).start()

        @pl.when(m == 0)
        def _():
            fetch(0, 0)

        @pl.when(m + 1 < tiles)
        def _():
            fetch(m + 1, (m + 1) % 2)

        slot = m % 2
        for h in range(2):
            pltpu.make_async_copy(
                xs[0].at[pl.ds(0, part)], held_x.at[slot, pl.ds(h * part, part)], sems.at[slot, h]
            ).wait()
        x = held_x[slot]
        all_ref[...] = x
        value, slope = gelu_pair(dot(x, w_ref[:, :share], ((1,), (0,))))
        up = dot(x, w_ref[:, share:], ((1,), (0,)))
        hidden_ref[...] = (value * up).astype(BF16)
        by_gate_ref[...] = up * slope
        by_up_ref[...] = value

    tile = tokens_spec(share, tiles, 0)
    return pl.pallas_call(
        body,
        grid=(tiles,),
        in_specs=[pl.BlockSpec(memory_space=pl.ANY)] * len(pieces) + [held(width, 2 * share)],
        out_specs=[tokens_spec(width, tiles, 0)] + [tile] * 3,
        out_shape=[
            jax.ShapeDtypeStruct((count, width), BF16),
            jax.ShapeDtypeStruct((count, share), BF16),
            jax.ShapeDtypeStruct((count, share), F32),
            jax.ShapeDtypeStruct((count, share), F32),
        ],
        scratch_shapes=[pltpu.VMEM((2, TILE, width), BF16), pltpu.SemaphoreType.DMA((2, 2))],
        compiler_params=feed_params(),
        cost_estimate=cost(),
        name="feed_forward",
    )(*pieces, w_feed)


def feed_backward(feed_grad, by_gate, by_up, w_feed):
    count, width = feed_grad.shape
    share = w_feed.shape[1] // 3
    tiles = count // TILE
    mid = tiles // 2

    def body(fg_ref, gate_ref, up_ref, wd_ref, we_ref, low_ref, first_ref, second_ref):
        grad = dot(fg_ref[...], wd_ref[...], ((1,), (0,)))
        gate = (grad * gate_ref[...]).astype(BF16)
        up = (grad * up_ref[...]).astype(BF16)
        low_ref[:, :share] = gate
        low_ref[:, share:] = up
        terms = dot(gate, we_ref[:, :share], ((1,), (1,))) + dot(up, we_ref[:, share:], ((1,), (1,)))
        store_half(first_ref, second_ref, tiles, terms.astype(BF16))

    tile = tokens_spec(share, tiles, mid)
    return pl.pallas_call(
        body,
        grid=(tiles,),
        in_specs=[tokens_spec(width, tiles, mid), tile, tile, held(width, share, 2), held(width, 2 * share)],
        out_specs=[tokens_spec(2 * share, tiles, mid)] + half_specs(width, tiles),
        out_shape=[
            jax.ShapeDtypeStruct((count, 2 * share), BF16),
            jax.ShapeDtypeStruct((count // 2, width), BF16),
            jax.ShapeDtypeStruct((count // 2, width), BF16),
        ],
        compiler_params=feed_params(),
        cost_estimate=cost(),
        name="feed_backward",
    )(feed_grad, by_gate, by_up, w_feed, w_feed)


def feed_down(hidden, w_feed):
    count, share = hidden.shape
    width = w_feed.shape[0]
    tiles = count // TILE

    def body(h_ref, w_ref, first_ref, second_ref):
        store_half(first_ref, second_ref, tiles, dot(h_ref[...], w_ref[...], ((1,), (1,))).astype(BF16))

    return pl.pallas_call(
        body,
        grid=(tiles,),
        in_specs=[tokens_spec(share, tiles, tiles // 2), held(width, share, 2)],
        out_specs=half_specs(width, tiles),
        out_shape=[jax.ShapeDtypeStruct((count // 2, width), BF16)] * 2,
        compiler_params=feed_params(),
        cost_estimate=cost(),
        name="feed_down",
    )(hidden, w_feed)


def weight_grad(x, grad, into=None, at=0, blocks=1):
    count, width = x.shape
    columns = grad.shape[1]
    deep, wide = 512 if count > 1024 else width // 2, columns // blocks

    def body(x_ref, g_ref, *rest):
        rest[-1][...] = dot(x_ref[...], g_ref[...], ((0,), (0,))).astype(BF16)

    return pl.pallas_call(
        body,
        grid=(width // deep,),
        in_specs=[
            pl.BlockSpec((count, deep), lambda m: (0, m)),
            pl.BlockSpec((count, wide), lambda m: (0, at), pipeline_mode=pl.Buffered(1)),
        ]
        + ([] if into is None else [pl.BlockSpec(memory_space=pl.ANY)]),
        out_specs=pl.BlockSpec((deep, wide), lambda m: (m, at)),
        out_shape=jax.ShapeDtypeStruct((width, columns), BF16),
        input_output_aliases={} if into is None else {2: 0},
        compiler_params=feed_params(),
        cost_estimate=cost(),
        name="weight_grad",
    )(x, grad, *([] if into is None else [into]))


def unit_terms(pairs, order):
    count = pairs[0][0].shape[0] // 2
    units, width = pairs[0][0].shape[1], pairs[0][1].shape[0]
    refs = 2 * len(pairs)

    def body(order_ref, *rest):
        total = dot(rest[0][...], rest[1][...], ((1,), (1,)))
        for n in range(2, refs, 2):
            total = total + dot(rest[n][...], rest[n + 1][...], ((1,), (1,)))
        for n in range(2):

            @pl.when(pl.program_id(0) == n)
            def _():
                rest[refs + n][...] = total

    rows = pl.BlockSpec((count, units), lambda n, order_ref: (order_ref[n], 0))
    weights = pl.BlockSpec((width, units), lambda n, order_ref: (0, 0), pipeline_mode=pl.Buffered(1))
    return pl.pallas_call(
        body,
        grid_spec=pltpu.PrefetchScalarGridSpec(
            num_scalar_prefetch=1,
            grid=(2,),
            in_specs=[rows, weights] * len(pairs),
            out_specs=[pl.BlockSpec((count, width), lambda n, order_ref: (0, 0))] * 2,
        ),
        out_shape=[jax.ShapeDtypeStruct((count, width), F32)] * 2,
        compiler_params=feed_params(),
        cost_estimate=cost(),
        name="unit_terms",
    )(order, *[v for pair in pairs for v in pair])


ORDER = (1, 3, 2, 0)


def weight_grad_parts(x, grad, places, extra=None):
    count, width = x.shape
    columns = grad.shape[1]
    rows, cols = width // SQUARE, columns // 2
    more = 0 if extra is None else extra.shape[0] // SQUARE
    each = rows + more

    def body(places_ref, x_ref, g_ref, *rest):
        left_ref, right_ref, two_ref, one_ref, own_left, own_right = rest[-6:]
        targets = [
            ((left_ref, 0), (one_ref, 0)),
            ((left_ref, each), (right_ref, 0)),
            ((two_ref, 0), (right_ref, each)),
            ((own_left, 0), (own_right, 0)),
        ]
        value = dot(x_ref[...], g_ref[...], ((0,), (0,))).astype(BF16)
        for n in range(SQUARE):

            @pl.when(pl.program_id(0) == n)
            def _():
                for h, (ref, at) in enumerate(targets[n]):
                    ref[pl.ds(at, rows), :] = value[:, h * cols : (h + 1) * cols]
                    if more:
                        ref[pl.ds(at + rows, more), :] = rest[0][:, h * cols : (h + 1) * cols]

    sizes = [2 * each, 2 * each] + [each] * 4
    return pl.pallas_call(
        body,
        grid_spec=pltpu.PrefetchScalarGridSpec(
            num_scalar_prefetch=1,
            grid=(SQUARE,),
            in_specs=[
                pl.BlockSpec((count, rows), lambda n, places_ref: (0, places_ref[n])),
                pl.BlockSpec((count, columns), lambda n, places_ref: (0, 0)),
            ]
            + ([pl.BlockSpec((more, columns), lambda n, places_ref: (places_ref[n], 0))] if more else []),
            out_specs=[pl.BlockSpec((size, cols), lambda n, places_ref: (0, 0)) for size in sizes],
        ),
        out_shape=[jax.ShapeDtypeStruct((size, cols), BF16) for size in sizes],
        compiler_params=feed_params(),
        cost_estimate=cost(),
        name="weight_grad_parts",
    )(places, x, grad, *([extra] if more else []))


def carried(own, axis, step):
    near_map = shifted(own, axis, step)
    both = jnp.stack([near_map[0] * own[0], own[0] * near_map[1] + own[1]])
    result, reach = near_map, 2
    while reach < lax.axis_size(axis):
        far = shifted(both, axis, step * reach)
        result = jnp.stack([result[0] * far[0], result[0] * far[1] + result[1]])
        both = jnp.stack([both[0] * far[0], both[0] * far[1] + both[1]])
        reach *= 2
    return result[1]


def cross(x, axis, r):
    return lax.ppermute(x, axis, [(i, i ^ r) for i in range(lax.axis_size(axis))])


def total_over(x, axis):
    r = 1
    while r < lax.axis_size(axis):
        x = x + cross(x, axis, r)
        r *= 2
    return x


def after(x, done):
    return lax.optimization_barrier((x, done))


SQUARE = 4


def token_axes():
    return ("fsdp", "ctx") if lax.axis_size("fsdp") == SQUARE else ("ctx", "fsdp")


def together(*values):
    return lax.optimization_barrier(values)


def place(blocks, axis):
    me = lax.axis_index(axis)
    first = blocks[0]
    whole = jnp.zeros((len(blocks),) + first.shape, first.dtype)
    for r, block in enumerate(blocks):
        at = 0
        for piece in block if isinstance(block, list) else [block]:
            whole = lax.dynamic_update_slice(whole, piece[None], (me ^ r, at) + (0,) * (piece.ndim - 1))
            at += piece.shape[0]
    return whole


def near_blocks(x, axis):
    return list(together(cross(x, axis, 1), cross(x, axis, 2)))


def far_block(got, axis):
    mid = got[0].shape[0] // 2
    halves = together(got[0][:mid], got[1][mid:])
    return [cross(halves[0], axis, 2), cross(halves[1], axis, 1)]


def near(x, axis):
    got = near_blocks(x, axis)
    return [x] + got + [far_block(got, axis)]


def low(v):
    return v.astype(BF16)


def wide(v):
    return v.astype(F32)


def near_send(parts, axis):
    return together(cross(parts[0], axis, 1), cross(parts[1], axis, 2))


def near_middle(parts, got):
    rows = got[0].shape[0] // 2
    return together(low(wide(parts[2]) + wide(got[0][rows:])), low(wide(parts[3]) + wide(got[1][:rows])))


def near_second(sums, axis):
    return together(cross(sums[0], axis, 2), cross(sums[1], axis, 1))


def near_last(parts, got, more):
    rows = got[0].shape[0] // 2
    left = wide(parts[4]) + wide(got[0][:rows]) + wide(more[0])
    right = wide(parts[5]) + wide(got[1][rows:]) + wide(more[1])
    return jnp.concatenate([left, right], axis=1)


def gather_in_turn(arrays, ready):
    if lax.axis_size("fsdp") != SQUARE:
        return [lax.all_gather(x, "fsdp", axis=0) for x in arrays], ready
    results = []
    for x in arrays:
        if results:
            x, results[-1] = together(x, results[-1])
        got = near_blocks(x, "fsdp")
        if not results:
            got, ready = together(got, ready)
        results.append([x] + got + [far_block(got, "fsdp")])
    return results, ready


def rows_of(blocks, start, stop):
    if lax.axis_size("fsdp") != SQUARE:
        return blocks[:, :, start:stop].reshape(-1, blocks.shape[-1])
    cut = lambda v: v[:, start:stop]
    whole = place([[cut(v) for v in block] if isinstance(block, list) else cut(block) for block in blocks], "fsdp")
    return whole.reshape(-1, whole.shape[-1])


def token_pieces(x):
    axis = token_axes()[0]
    theirs = swap(x, "tp")
    got = near_blocks(x, axis)
    far = far_block(got, axis)
    got_theirs = [swap(v, "tp") for v in got]
    far_theirs = [swap(v, "tp") for v in far]
    return [got[0], *far, got[1], x, got_theirs[0], *far_theirs, got_theirs[1], theirs]


def token_parts(first, theirs):
    rows, cols = first.shape[0] // SQUARE, first.shape[1] // 2

    def part(start, stop, half):
        here = (slice(start * rows, stop * rows), slice(half * cols, (half + 1) * cols))
        return low(wide(first[here]) + wide(theirs[here]))

    return [part(0, 2, 0), part(1, 3, 1)], [part(2, 3, 0), part(0, 1, 1), part(3, 4, 0), part(3, 4, 1)]


def trade(pieces):
    axis = token_axes()[0]
    me = lax.axis_index(axis)
    return place([pieces(me)] + [cross(pieces(me ^ r), axis, r) for r in range(1, SQUARE)], axis)


def gather_feed(local):
    _, along = token_axes()
    whole = lax.all_gather(local, along, axis=1 if along == "ctx" else 0, tiled=True)
    return whole.reshape(-1, local.shape[2])


def scatter_feed(grad):
    _, along = token_axes()
    if along == "ctx":
        grad = grad.reshape(SQUARE, -1, grad.shape[1])
        return lax.psum_scatter(grad, along, scatter_dimension=1, tiled=True)
    part = lax.psum_scatter(grad, along, scatter_dimension=0, tiled=True)
    return part.reshape(SQUARE, -1, grad.shape[1])


def rms(values):
    return lax.rsqrt(jnp.mean(values * values, axis=-1, keepdims=True) + EPSILON)


def rms_back(values, inverse, gain, grad):
    u = grad * gain
    inner = jnp.mean(values * u, axis=-1, keepdims=True)
    gain_grad = jnp.sum(grad * values * inverse, axis=0)
    return inverse * u - values * (inverse * inverse * inverse) * inner, gain_grad


def shards(
    block_input, segments, token_mask, cotangent, norm_gains, conv_taps, conv_offset, gate_offset,
    decay_logit, intake, gate_blocks, outlet, expand, contract,
):
    rows, length, width = block_input.shape
    depth = intake.shape[0]
    units = intake.shape[2]
    gate_rows = gate_blocks.shape[0]
    hidden_units = contract.shape[1]
    tokens = rows * length
    ctx, tp = lax.axis_size("ctx"), lax.axis_size("tp")
    mine = lax.axis_index("tp")
    half = tokens // tp
    share = -(-hidden_units // (SQUARE * 256)) * 256
    padding = SQUARE * share - hidden_units

    def own(x):
        return lax.dynamic_slice_in_dim(x, mine * half, half, 0)

    def other(x):
        return lax.dynamic_slice_in_dim(x, (1 - mine) * half, half, 0)

    def join(x):
        theirs = swap(x, "tp")
        return jnp.concatenate(
            [jnp.where(mine == 0, x, theirs), jnp.where(mine == 0, theirs, x)], axis=0
        )

    first = jnp.concatenate([intake[:, 1], gate_blocks.reshape(2 * gate_rows, units)], axis=0)
    first = lax.all_gather(first, "ctx", axis=0)
    second = lax.all_gather(jnp.concatenate([intake[:, 0], outlet], axis=0), "ctx", axis=0)

    def cut(w):
        w = jnp.pad(w, ((0, 0), (0, padding)))
        return lambda p: lax.dynamic_slice_in_dim(w, p * share, share, 1)

    down, gate_in, up_in = cut(contract), cut(expand[:, 0]), cut(expand[:, 1])
    local_feed = trade(lambda p: jnp.concatenate([gate_in(p), up_in(p), down(p)], axis=1))

    mask_rows = token_mask.astype(F32).reshape(tokens, 1)
    out_grad = own(cotangent.reshape(tokens, width)).astype(F32) * own(mask_rows)
    local_feed_grad = out_grad.astype(BF16)

    (got_first, got_gelu, got_outlet), local_feed = gather_in_turn(
        [first, second[:, :depth], second[:, depth:]], local_feed
    )
    w_feed = gather_feed(local_feed)
    w_branch = rows_of(got_first, 0, depth)
    blocks = rows_of(got_first, depth, first.shape[1]).reshape(HEAD_W, 2, units).transpose(1, 0, 2)
    w_gelu = rows_of(got_gelu, 0, depth)
    w_outlet = rows_of(got_outlet, 0, depth)

    seg_next = segments + 1
    seg_before = shifted(seg_next[:, -3:], "ctx", 1)
    seg_ext = jnp.concatenate([seg_before, seg_next], axis=1)
    masks = jnp.stack(
        [(seg_ext[:, 3 - k : 3 - k + length] == seg_next).astype(F32) for k in (1, 1, 2, 3)]
        + [jnp.zeros(segments.shape, F32)] * 4,
        axis=2,
    )
    params = jnp.concatenate(
        [
            conv_taps,
            conv_offset[None],
            gate_offset,
            jax.nn.softplus(-decay_logit)[None],
            jax.nn.sigmoid(-decay_logit)[None],
            jnp.zeros((PARAM_ROWS - 9, units), F32),
        ],
        axis=0,
    )

    x = block_input.reshape(tokens, width).astype(F32)
    inverse_one = rms(x)
    normed = (x * inverse_one * norm_gains[0]).astype(BF16)
    x_branch = dot(normed, w_branch, ((1,), (0,))).astype(BF16).reshape(rows, length, units)
    gelu_in = dot(normed, w_gelu, ((1,), (0,))).reshape(rows, length, units)
    x_before = shifted(x_branch[:, -3:], "ctx", 1)
    halo = jnp.pad(x_before, ((0, 0), (5, 0), (0, 0))).astype(F32)
    conv_low, r, i, coef, prod, total = recurrent_forward(x_branch, halo, masks, params, blocks)
    ends = jnp.stack([prod[:, -1], total[:, -1]])
    entering = carried(ends, "ctx", 1)
    state_in = jnp.broadcast_to(entering[:, None], (rows, 8, units))
    states = total + prod * entering[:, None]
    recurrent = (states * jax.nn.gelu(gelu_in, approximate=True)).astype(BF16).reshape(tokens, units)

    sent = swap(dot(other(recurrent), w_outlet, ((1,), (1,))), "tp")
    branch = dot(own(recurrent), w_outlet, ((1,), (1,))) + sent
    residual = own(x) + branch
    inverse_two = rms(residual)
    normed_two = token_pieces((residual * inverse_two * norm_gains[1]).astype(BF16))

    def to_owners(part):
        return trade(lambda p: lax.dynamic_index_in_dim(part, p, 0, keepdims=False))

    local_feed_grad, normed_two = together(local_feed_grad, normed_two)
    feed_grad = jnp.concatenate(token_pieces(local_feed_grad), axis=0)
    normed_two, hidden, by_gate, by_up = feed_forward(normed_two, w_feed)
    down_grad = weight_grad(feed_grad, hidden)
    by_gate, down_grad = after(by_gate, down_grad)
    down_part = scatter_feed(down_grad)
    expand_low, n2g_own, n2g_other = feed_backward(feed_grad, by_gate, by_up, w_feed)

    group = token_axes()[0]
    theirs = swap(n2g_other, "tp")
    parts, kept = token_parts(n2g_own, theirs)
    parts, expand_low = after(parts, expand_low)
    got = near_send(parts, group)
    parts = parts + kept
    expand_all = weight_grad(normed_two, expand_low)
    got, expand_all = after(got, expand_all)
    sums, hidden = after(near_middle(parts, got), hidden)
    more = near_second(sums, group)
    feed_own, feed_other = feed_down(hidden, w_feed)
    more, (feed_own, feed_other) = after(more, (feed_own, feed_other))
    normed_two_grad = near_last(parts, got, more)
    expand_all, down_part = after(expand_all, down_part)
    expand_part = scatter_feed(expand_all)
    feed_theirs = swap(feed_other, "tp")

    norm_part, gain_two = rms_back(residual, inverse_two, norm_gains[1], normed_two_grad)
    residual_grad = out_grad + norm_part
    branch_grad = join(residual_grad.astype(BF16))

    square = lax.axis_size("fsdp") == SQUARE
    places = lax.axis_index("fsdp").astype(jnp.int32) ^ jnp.array(ORDER, jnp.int32)
    if square:
        outlet_parts = weight_grad_parts(branch_grad, recurrent, places)
    else:
        outlet_parts = weight_grad(branch_grad, recurrent)
    outlet_parts, branch_grad = after(outlet_parts, branch_grad)
    outlet_got = near_send(outlet_parts, "fsdp") if square else outlet_parts
    rec_grad = dot(branch_grad, w_outlet, ((1,), (0,))).reshape(rows, length, units)
    gelu_grad, tprod, tsum = recurrent_adjoint(rec_grad, gelu_in, coef, prod, total, state_in)
    gelu_low = gelu_grad.reshape(tokens, units)
    if square:
        gelu_parts = weight_grad_parts(normed, gelu_low, places)
    else:
        gelu_parts = weight_grad(normed, gelu_low)
    outlet_got, gelu_parts, tprod, tsum = together(outlet_got, gelu_parts, tprod, tsum)
    if square:
        outlet_sums, gelu_parts, tprod = together(near_middle(outlet_parts, outlet_got), gelu_parts, tprod)
        outlet_more, gelu_got = near_second(outlet_sums, "fsdp"), near_send(gelu_parts, "fsdp")
    heads = jnp.stack([coef[:, 0] * tprod[:, 0], coef[:, 0] * tsum[:, 0]])
    leaving = carried(heads, "ctx", -1)
    leaving = jnp.broadcast_to(leaving[:, None], (rows, 8, units))
    branch_x, before, small, blocks_grad = recurrent_backward(
        tprod, tsum, leaving, prod, total, state_in, coef, r, i, conv_low, x_branch, halo, masks, params, blocks
    )
    from_next = shifted(before[:, 5:], "ctx", -1)
    branch_x = branch_x + jnp.pad(from_next, ((0, 0), (length - 3, 0), (0, 0)))
    branch_low = branch_x.astype(BF16).reshape(tokens, units)
    blocks_rows = blocks_grad.transpose(1, 0, 2).reshape(2 * HEAD_W, units)
    if square:
        branch_parts = weight_grad_parts(normed, branch_low, places, blocks_rows)
        gelu_got, outlet_more, branch_parts, branch_low = together(gelu_got, outlet_more, branch_parts, branch_low)
        gelu_sums, branch_parts, branch_low = together(near_middle(gelu_parts, gelu_got), branch_parts, branch_low)
        gelu_more, branch_got = near_second(gelu_sums, "fsdp"), near_send(branch_parts, "fsdp")
        outlet_part = low(near_last(outlet_parts, outlet_got, outlet_more))
    else:
        branch_parts = weight_grad(normed, branch_low)
        outlet_part, gelu_part = [
            lax.psum_scatter(v, "fsdp", scatter_dimension=0, tiled=True) for v in (outlet_got, gelu_parts)
        ]
        branch_got = branch_parts
    theirs, ours = unit_terms(
        [(branch_low, w_branch), (gelu_low, w_gelu)], jnp.stack([1 - mine, mine]).astype(jnp.int32)
    )
    def scatter_ctx(v):
        return lax.psum_scatter(v, "ctx", scatter_dimension=0, tiled=False)

    outlet_part, expand_part = after(outlet_part, expand_part)
    outlet_part = scatter_ctx(outlet_part.reshape(ctx, depth, units))
    if square:
        gelu_more, branch_got, theirs, ours, outlet_part = together(gelu_more, branch_got, theirs, ours, outlet_part)
        gelu_part = low(near_last(gelu_parts, gelu_got, gelu_more))
        late_sums, gelu_part = after(near_middle(branch_parts, branch_got), gelu_part)
        late_more = near_second(late_sums, "fsdp")
    else:
        gelu_part, outlet_part = after(gelu_part, outlet_part)
    gelu_part = scatter_ctx(gelu_part.reshape(ctx, depth, units))
    if square:
        late = low(near_last(branch_parts, branch_got, late_more))
        late = [late[: ctx * depth], late[ctx * depth :]]
    else:
        late = [lax.psum_scatter(v, "fsdp", scatter_dimension=0, tiled=True) for v in (branch_got, blocks_rows)]
    late = jnp.concatenate([v.reshape(ctx, -1, units) for v in late], axis=1)
    normed_grad = ours + swap(theirs, "tp")
    norm_part, gain_one = rms_back(own(x), own(inverse_one), norm_gains[0], normed_grad)
    input_own = residual_grad + norm_part
    late, gelu_part, expand_part, down_part, input_own, gain_one, feed_own, feed_theirs = together(
        late, gelu_part, expand_part, down_part, input_own, gain_one, feed_own, feed_theirs
    )
    late = wide(scatter_ctx(late))
    feed_parts, feed_kept = token_parts(feed_own, feed_theirs)
    feed_got = near_send(feed_parts, group)
    feed_parts = feed_parts + feed_kept
    feed_sums = near_middle(feed_parts, feed_got)
    input_grad = join(input_own).reshape(rows, length, width)
    feed_out = near_last(feed_parts, feed_got, near_second(feed_sums, group))
    block_output = join(low(residual + feed_out)).reshape(rows, length, width)

    down_part = to_owners(down_part)
    expand_part = to_owners(expand_part)

    def columns(part, n):
        return jnp.concatenate([part[p, :, n * share : (n + 1) * share] for p in range(SQUARE)], axis=1)[
            :, :hidden_units
        ].astype(F32)

    contract_grad = columns(down_part, 0)
    expand_grad = jnp.stack([columns(expand_part, 0), columns(expand_part, 1)], axis=1)

    gains = jnp.concatenate([gain_one, gain_two]).reshape(-1, units)
    small = total_over(total_over(jnp.concatenate([small, gains], axis=0), "fsdp"), "ctx")
    gains = total_over(small[8:], "tp").reshape(2, width)
    return (
        block_output,
        input_grad,
        gains,
        small[0:4],
        small[4],
        small[5:7],
        small[7],
        jnp.stack([wide(gelu_part), late[:depth]], axis=1),
        late[depth:].reshape(gate_rows, 2, units),
        wide(outlet_part),
        expand_grad,
        contract_grad,
    )


def solution(mesh):
    placed = (
        P("fsdp", "ctx", None),
        P("fsdp", "ctx"),
        P("fsdp", "ctx"),
        P("fsdp", "ctx", None),
        P(),
        P(None, "tp"),
        P("tp"),
        P(None, "tp"),
        P("tp"),
        P(("fsdp", "ctx"), None, "tp"),
        P(("fsdp", "ctx"), None, "tp"),
        P(("fsdp", "ctx"), "tp"),
        P(("fsdp", "ctx"), None, "tp"),
        P(("fsdp", "ctx"), "tp"),
    )
    return jax.shard_map(
        shards,
        mesh=mesh,
        in_specs=placed,
        out_specs=(
            P("fsdp", "ctx", None),
            P("fsdp", "ctx", None),
            P(),
            P(None, "tp"),
            P("tp"),
            P(None, "tp"),
            P("tp"),
            P(("fsdp", "ctx"), None, "tp"),
            P(("fsdp", "ctx"), None, "tp"),
            P(("fsdp", "ctx"), "tp"),
            P(("fsdp", "ctx"), None, "tp"),
            P(("fsdp", "ctx"), "tp"),
        ),
        check_vma=False,
    )
```

```python
import jax
import jax.numpy as jnp
from jax import lax
from jax.experimental import pallas as pl
from jax.experimental.pallas import tpu as pltpu
from jax.sharding import PartitionSpec as P

HEAD_W = 256
LANES = 128
CHUNKS = 8

EPSILON = 1e-06
DECAY_SCALE = 8.0
GELU_C = 0.7978845608028654
GELU_A = 0.044715

F32 = jnp.float32
BF16 = jnp.bfloat16

TAP0, OFFSET, RATE_OFF, INLET_OFF, SOFTPLUS, NEG_SIG, PARAM_ROWS = 0, 4, 5, 6, 7, 8, 16


def shifted(x, axis, by):
    length = lax.axis_size(axis)
    pairs = [(i, i + by) for i in range(length) if 0 <= i + by < length]
    return lax.ppermute(x, axis, pairs)


def swap(x, axis):
    length = lax.axis_size(axis)
    return lax.ppermute(x, axis, [(i, (i + 1) % length) for i in range(length)])


def gelu_pair(v):
    t = jnp.tanh(GELU_C * (v + GELU_A * v * v * v))
    value = 0.5 * v * (1.0 + t)
    slope = 0.5 * (1.0 + t) + 0.5 * v * (1.0 - t * t) * GELU_C * (1.0 + 3.0 * GELU_A * v * v)
    return value, slope


def one_minus_exp(x):
    s = 1.0 + x / 7.0
    for n in (6.0, 5.0, 4.0, 3.0, 2.0):
        s = 1.0 + x / n * s
    return jnp.where(x > -0.5, -x * s, 1.0 - jnp.exp(x))


def sigmoid(v):
    return 1.0 / (1.0 + jnp.exp(-v))


def dot(a, b, dims):
    return lax.dot_general(a, b, (dims, ((), ())), preferred_element_type=F32)


def lane_scan(load_a, load_b, store, length, reverse):
    steps = length // CHUNKS
    prod = jnp.ones((CHUNKS, LANES), F32)
    total = jnp.zeros((CHUNKS, LANES), F32)
    for n in range(steps):
        s = steps - 1 - n if reverse else n
        coef = load_a(s)
        total = coef * total + load_b(s)
        prod = coef * prod
        store(s, prod, total)
    return prod, total


def chunk_carries(prod, total, reverse):
    order = range(CHUNKS - 1, -1, -1) if reverse else range(CHUNKS)
    run_p = jnp.ones((1, LANES), F32)
    run_s = jnp.zeros((1, LANES), F32)
    carries = [None] * CHUNKS
    for c in order:
        carries[c] = (run_p, run_s)
        run_s = prod[c : c + 1] * run_s + total[c : c + 1]
        run_p = prod[c : c + 1] * run_p
    return carries


def sweep(a_scr, b_scr, p_scr, s_scr, prod_ref, sum_ref, rows, length, reverse, shift):
    steps = length // CHUNKS
    for b in range(rows):
        for j in range(HEAD_W // LANES):
            av, bv, pv, sv = (a_scr.at[b, j], b_scr.at[b, j], p_scr.at[b, j], s_scr.at[b, j])

            def store(s, prod, total):
                pv[pl.ds(s, CHUNKS, stride=steps), :] = prod
                sv[pl.ds(s, CHUNKS, stride=steps), :] = total

            prod, total = lane_scan(
                lambda s: av[pl.ds(s + shift, CHUNKS, stride=steps), :],
                lambda s: bv[pl.ds(s, CHUNKS, stride=steps), :],
                store,
                length,
                reverse,
            )
            carries = chunk_carries(prod, total, reverse)
            lanes = slice(j * LANES, (j + 1) * LANES)
            for c in range(CHUNKS):
                here = slice(c * steps, (c + 1) * steps)
                p = pv[here, :]
                prod_ref[b, here, lanes] = p * carries[c][0]
                sum_ref[b, here, lanes] = sv[here, :] + p * carries[c][1]


def to_lanes(ref, b, at, value):
    for j in range(HEAD_W // LANES):
        ref[b, j, pl.ds(at, value.shape[0]), :] = value[:, j * LANES : (j + 1) * LANES]


def forward_kernel(
    x_ref, halo_ref, mask_ref, par_ref, w_ref,
    conv_ref, r_ref, i_ref, a_ref, prod_ref, sum_ref,
    ext, a_scr, b_scr, p_scr, s_scr,
):
    rows, length, _ = x_ref.shape
    par = par_ref[...]
    w0, w1 = w_ref[0], w_ref[1]
    for b in range(rows):
        ext[b, pl.ds(0, 8), :] = halo_ref[b]
        ext[b, pl.ds(8, length), :] = x_ref[b].astype(F32)
        conv = ext[b, pl.ds(8, length), :] * par[TAP0 : TAP0 + 1] + par[OFFSET : OFFSET + 1]
        for k in range(1, 4):
            match = mask_ref[b, :, k : k + 1]
            conv = conv + par[TAP0 + k : TAP0 + k + 1] * ext[b, pl.ds(8 - k, length), :] * match
        conv_low = conv.astype(BF16)
        conv_ref[b] = conv_low
        conv = conv_low.astype(F32)
        r = sigmoid(dot(conv_low, w0, ((1,), (0,))) + par[RATE_OFF : RATE_OFF + 1])
        i = sigmoid(dot(conv_low, w1, ((1,), (0,))) + par[INLET_OFF : INLET_OFF + 1])
        r_ref[b] = r
        i_ref[b] = i
        log_keep = -DECAY_SCALE * r * par[SOFTPLUS : SOFTPLUS + 1]
        going = mask_ref[b, :, 0:1]
        a = jnp.exp(log_keep) * going
        a_ref[b] = a
        scale = jnp.where(going > 0.5, jnp.sqrt(one_minus_exp(2.0 * log_keep)), 1.0)
        to_lanes(a_scr, b, 0, a)
        to_lanes(b_scr, b, 0, i * conv * scale)
    sweep(a_scr, b_scr, p_scr, s_scr, prod_ref, sum_ref, rows, length, False, 0)


def head_spec(rows, length):
    return pl.BlockSpec((rows, length, HEAD_W), lambda h: (0, 0, h))


def recurrent_forward(x_branch, halo, masks, params, blocks):
    rows, length, units = x_branch.shape
    full = head_spec(rows, length)
    scan = pltpu.VMEM((rows, HEAD_W // LANES, length, LANES), F32)
    big = jax.ShapeDtypeStruct((rows, length, units), F32)
    return pl.pallas_call(
        forward_kernel,
        grid=(units // HEAD_W,),
        in_specs=[
            full,
            head_spec(rows, 8),
            pl.BlockSpec((rows, length, 8), lambda h: (0, 0, 0)),
            pl.BlockSpec((PARAM_ROWS, HEAD_W), lambda h: (0, h)),
            pl.BlockSpec((2, HEAD_W, HEAD_W), lambda h: (0, 0, h)),
        ],
        out_specs=[full] * 6,
        out_shape=[jax.ShapeDtypeStruct((rows, length, units), BF16)] + [big] * 5,
        scratch_shapes=[pltpu.VMEM((rows, length + 8, HEAD_W), F32), scan, scan, scan, scan],
        compiler_params=pltpu.CompilerParams(vmem_limit_bytes=48 * 1024 * 1024),
        cost_estimate=cost(),
        name="recurrent_forward",
    )(x_branch, halo, masks, params, blocks)


def adjoint_kernel(
    rg_ref, gelu_ref, a_ref, prod_ref, sum_ref, in_ref,
    gg_ref, tprod_ref, tsum_ref,
    a_scr, b_scr, p_scr, s_scr,
):
    rows, length, _ = rg_ref.shape
    for b in range(rows):
        states = sum_ref[b] + prod_ref[b] * in_ref[b, 0:1]
        value, slope = gelu_pair(gelu_ref[b])
        rg = rg_ref[b]
        gg_ref[b] = (rg * states * slope).astype(BF16)
        to_lanes(a_scr, b, 0, a_ref[b])
        to_lanes(a_scr, b, length, jnp.ones((8, HEAD_W), F32))
        to_lanes(b_scr, b, 0, rg * value)
    sweep(a_scr, b_scr, p_scr, s_scr, tprod_ref, tsum_ref, rows, length, True, 1)


def recurrent_adjoint(rec_grad, gelu_in, coef, prod, total, state_in):
    rows, length, units = rec_grad.shape
    full = head_spec(rows, length)
    scan = pltpu.VMEM((rows, HEAD_W // LANES, length, LANES), F32)
    longer = pltpu.VMEM((rows, HEAD_W // LANES, length + 8, LANES), F32)
    big = jax.ShapeDtypeStruct((rows, length, units), F32)
    return pl.pallas_call(
        adjoint_kernel,
        grid=(units // HEAD_W,),
        in_specs=[full] * 5 + [head_spec(rows, 8)],
        out_specs=[full] * 3,
        out_shape=[jax.ShapeDtypeStruct((rows, length, units), BF16), big, big],
        scratch_shapes=[longer, scan, scan, scan],
        compiler_params=pltpu.CompilerParams(vmem_limit_bytes=48 * 1024 * 1024),
        cost_estimate=cost(),
        name="recurrent_adjoint",
    )(rec_grad, gelu_in, coef, prod, total, state_in)


def backward_kernel(
    tprod_ref, tsum_ref, leave_ref, prod_ref, sum_ref, in_ref, a_ref, r_ref, i_ref, conv_ref,
    x_ref, halo_ref, mask_ref, par_ref, w_ref,
    bx_ref, before_ref, small_ref, blocks_ref,
    ext, st_ext, g_ext,
):
    rows, length, _ = tprod_ref.shape
    par = par_ref[...]
    w0, w1 = w_ref[0], w_ref[1]
    sums = [jnp.zeros((1, HEAD_W), F32) for _ in range(8)]
    blocks = [jnp.zeros((HEAD_W, HEAD_W), F32) for _ in range(2)]

    def add(n, value):
        sums[n] = sums[n] + jnp.sum(value, axis=0, keepdims=True)

    for b in range(rows):
        adjoint = tsum_ref[b] + tprod_ref[b] * leave_ref[b, 0:1]
        st_ext[b, pl.ds(0, 8), :] = in_ref[b]
        st_ext[b, pl.ds(8, length), :] = sum_ref[b] + prod_ref[b] * in_ref[b, 0:1]
        prev = st_ext[b, pl.ds(7, length), :]
        r, i, a = r_ref[b], i_ref[b], a_ref[b]
        conv_low = conv_ref[b]
        conv = conv_low.astype(F32)
        going = mask_ref[b, :, 0:1]
        log_keep = -DECAY_SCALE * r * par[SOFTPLUS : SOFTPLUS + 1]
        scale = jnp.where(going > 0.5, jnp.sqrt(one_minus_exp(2.0 * log_keep)), 1.0)
        log_grad = adjoint * prev * a - adjoint * i * conv * (a * a) / scale
        rate = log_grad * (-DECAY_SCALE * par[SOFTPLUS : SOFTPLUS + 1]) * r * (1.0 - r)
        spread = adjoint * scale
        inlet = spread * conv * i * (1.0 - i)
        add(5, rate)
        add(6, inlet)
        add(7, log_grad * r)
        rate_low = rate.astype(BF16)
        inlet_low = inlet.astype(BF16)
        grad = spread * i + dot(rate_low, w0, ((1,), (1,))) + dot(inlet_low, w1, ((1,), (1,)))
        blocks[0] = blocks[0] + dot(conv_low, rate_low, ((0,), (0,)))
        blocks[1] = blocks[1] + dot(conv_low, inlet_low, ((0,), (0,)))
        ext[b, pl.ds(0, 8), :] = halo_ref[b]
        ext[b, pl.ds(8, length), :] = x_ref[b].astype(F32)
        add(4, grad)
        add(0, grad * ext[b, pl.ds(8, length), :])
        bx = grad * par[TAP0 : TAP0 + 1]
        g_ext[b, pl.ds(0, 8), :] = jnp.zeros((8, HEAD_W), F32)
        g_ext[b, pl.ds(8 + length, 8), :] = jnp.zeros((8, HEAD_W), F32)
        before = jnp.zeros((8, HEAD_W), F32)
        for k in range(1, 4):
            masked = grad * mask_ref[b, :, k : k + 1]
            add(k, masked * ext[b, pl.ds(8 - k, length), :])
            g_ext[b, pl.ds(8, length), :] = masked
            tap = par[TAP0 + k : TAP0 + k + 1]
            bx = bx + tap * g_ext[b, pl.ds(8 + k, length), :]
            before = before + tap * g_ext[b, pl.ds(k, 8), :]
        bx_ref[b] = bx
        before_ref[b] = before
    sums[7] = sums[7] * (DECAY_SCALE * par[NEG_SIG : NEG_SIG + 1])
    for n in range(8):
        small_ref[pl.ds(n, 1), :] = sums[n]
    blocks_ref[0] = blocks[0].astype(blocks_ref.dtype)
    blocks_ref[1] = blocks[1].astype(blocks_ref.dtype)


def recurrent_backward(tprod, tsum, leaving, prod, total, state_in, coef, r, i, conv_low, x_branch, halo, masks, params, blocks):
    rows, length, units = tprod.shape
    full = head_spec(rows, length)
    edge = head_spec(rows, 8)
    return pl.pallas_call(
        backward_kernel,
        grid=(units // HEAD_W,),
        in_specs=[
            full, full, edge, full, full, edge, full, full, full, full, full, edge,
            pl.BlockSpec((rows, length, 8), lambda h: (0, 0, 0)),
            pl.BlockSpec((PARAM_ROWS, HEAD_W), lambda h: (0, h)),
            pl.BlockSpec((2, HEAD_W, HEAD_W), lambda h: (0, 0, h)),
        ],
        out_specs=[
            full,
            edge,
            pl.BlockSpec((8, HEAD_W), lambda h: (0, h)),
            pl.BlockSpec((2, HEAD_W, HEAD_W), lambda h: (0, 0, h)),
        ],
        out_shape=[
            jax.ShapeDtypeStruct((rows, length, units), F32),
            jax.ShapeDtypeStruct((rows, 8, units), F32),
            jax.ShapeDtypeStruct((8, units), F32),
            jax.ShapeDtypeStruct((2, HEAD_W, units), BF16),
        ],
        scratch_shapes=[
            pltpu.VMEM((rows, length + 8, HEAD_W), F32),
            pltpu.VMEM((rows, length + 8, HEAD_W), F32),
            pltpu.VMEM((rows, length + 16, HEAD_W), F32),
        ],
        compiler_params=pltpu.CompilerParams(vmem_limit_bytes=48 * 1024 * 1024),
        cost_estimate=cost(),
        name="recurrent_backward",
    )(tprod, tsum, leaving, prod, total, state_in, coef, r, i, conv_low, x_branch, halo, masks, params, blocks)


TILE = 256


def tokens_spec(columns, tiles, first):
    return pl.BlockSpec((TILE, columns), lambda m: ((m + first) % tiles, 0))


def held(rows, columns, at=0):
    return pl.BlockSpec((rows, columns), lambda m: (0, at), pipeline_mode=pl.Buffered(1))


def half_specs(columns, tiles):
    mid = tiles // 2
    return [
        pl.BlockSpec((TILE, columns), lambda m: (jnp.maximum(m - mid, 0), 0)),
        pl.BlockSpec((TILE, columns), lambda m: (jnp.minimum(m, mid - 1), 0)),
    ]


def store_half(first_ref, second_ref, tiles, value):
    m = pl.program_id(0)

    @pl.when(m < tiles // 2)
    def _():
        second_ref[...] = value

    @pl.when(m >= tiles // 2)
    def _():
        first_ref[...] = value


def feed_params():
    return pltpu.CompilerParams(vmem_limit_bytes=56 * 1024 * 1024)


def cost():
    return pl.CostEstimate(flops=1, bytes_accessed=1, transcendentals=0)


def feed_forward(pieces, w_feed):
    width = pieces[0].shape[1]
    share = w_feed.shape[1] // 3
    part = TILE // 2
    halves = []
    for n, piece in enumerate(pieces):
        halves += [(n, at) for at in range(0, piece.shape[0], part)]
    tiles = len(halves) // 2
    count = tiles * TILE

    def body(*refs):
        xs, (w_ref, all_ref, hidden_ref, by_gate_ref, by_up_ref, held_x, sems) = refs[: len(pieces)], refs[len(pieces) :]
        m = pl.program_id(0)

        def fetch(tile, slot):
            for at in range(tiles):

                @pl.when(tile == at)
                def _():
                    for h in range(2):
                        n, row = halves[2 * at + h]
                        pltpu.make_async_copy(
                            xs[n].at[pl.ds(row, part)], held_x.at[slot, pl.ds(h * part, part)], sems.at[slot, h]
                        ).start()

        @pl.when(m == 0)
        def _():
            fetch(0, 0)

        @pl.when(m + 1 < tiles)
        def _():
            fetch(m + 1, (m + 1) % 2)

        slot = m % 2
        for h in range(2):
            pltpu.make_async_copy(
                xs[0].at[pl.ds(0, part)], held_x.at[slot, pl.ds(h * part, part)], sems.at[slot, h]
            ).wait()
        x = held_x[slot]
        all_ref[...] = x
        value, slope = gelu_pair(dot(x, w_ref[:, :share], ((1,), (0,))))
        up = dot(x, w_ref[:, share:], ((1,), (0,)))
        hidden_ref[...] = (value * up).astype(BF16)
        by_gate_ref[...] = up * slope
        by_up_ref[...] = value

    tile = tokens_spec(share, tiles, 0)
    return pl.pallas_call(
        body,
        grid=(tiles,),
        in_specs=[pl.BlockSpec(memory_space=pl.ANY)] * len(pieces) + [held(width, 2 * share)],
        out_specs=[tokens_spec(width, tiles, 0)] + [tile] * 3,
        out_shape=[
            jax.ShapeDtypeStruct((count, width), BF16),
            jax.ShapeDtypeStruct((count, share), BF16),
            jax.ShapeDtypeStruct((count, share), F32),
            jax.ShapeDtypeStruct((count, share), F32),
        ],
        scratch_shapes=[pltpu.VMEM((2, TILE, width), BF16), pltpu.SemaphoreType.DMA((2, 2))],
        compiler_params=feed_params(),
        cost_estimate=cost(),
        name="feed_forward",
    )(*pieces, w_feed)


def feed_backward(feed_grad, by_gate, by_up, w_feed):
    count, width = feed_grad.shape
    share = w_feed.shape[1] // 3
    tiles = count // TILE
    mid = tiles // 2

    def body(fg_ref, gate_ref, up_ref, wd_ref, we_ref, low_ref, first_ref, second_ref):
        grad = dot(fg_ref[...], wd_ref[...], ((1,), (0,)))
        gate = (grad * gate_ref[...]).astype(BF16)
        up = (grad * up_ref[...]).astype(BF16)
        low_ref[:, :share] = gate
        low_ref[:, share:] = up
        terms = dot(gate, we_ref[:, :share], ((1,), (1,))) + dot(up, we_ref[:, share:], ((1,), (1,)))
        store_half(first_ref, second_ref, tiles, terms.astype(BF16))

    tile = tokens_spec(share, tiles, mid)
    return pl.pallas_call(
        body,
        grid=(tiles,),
        in_specs=[tokens_spec(width, tiles, mid), tile, tile, held(width, share, 2), held(width, 2 * share)],
        out_specs=[tokens_spec(2 * share, tiles, mid)] + half_specs(width, tiles),
        out_shape=[
            jax.ShapeDtypeStruct((count, 2 * share), BF16),
            jax.ShapeDtypeStruct((count // 2, width), BF16),
            jax.ShapeDtypeStruct((count // 2, width), BF16),
        ],
        compiler_params=feed_params(),
        cost_estimate=cost(),
        name="feed_backward",
    )(feed_grad, by_gate, by_up, w_feed, w_feed)


def feed_down(hidden, w_feed):
    count, share = hidden.shape
    width = w_feed.shape[0]
    tiles = count // TILE

    def body(h_ref, w_ref, first_ref, second_ref):
        store_half(first_ref, second_ref, tiles, dot(h_ref[...], w_ref[...], ((1,), (1,))).astype(BF16))

    return pl.pallas_call(
        body,
        grid=(tiles,),
        in_specs=[tokens_spec(share, tiles, tiles // 2), held(width, share, 2)],
        out_specs=half_specs(width, tiles),
        out_shape=[jax.ShapeDtypeStruct((count // 2, width), BF16)] * 2,
        compiler_params=feed_params(),
        cost_estimate=cost(),
        name="feed_down",
    )(hidden, w_feed)


def weight_grad(x, grad, into=None, at=0, blocks=1):
    count, width = x.shape
    columns = grad.shape[1]
    deep, wide = 512 if count > 1024 else width // 2, columns // blocks

    def body(x_ref, g_ref, *rest):
        rest[-1][...] = dot(x_ref[...], g_ref[...], ((0,), (0,))).astype(BF16)

    return pl.pallas_call(
        body,
        grid=(width // deep,),
        in_specs=[
            pl.BlockSpec((count, deep), lambda m: (0, m)),
            pl.BlockSpec((count, wide), lambda m: (0, at), pipeline_mode=pl.Buffered(1)),
        ]
        + ([] if into is None else [pl.BlockSpec(memory_space=pl.ANY)]),
        out_specs=pl.BlockSpec((deep, wide), lambda m: (m, at)),
        out_shape=jax.ShapeDtypeStruct((width, columns), BF16),
        input_output_aliases={} if into is None else {2: 0},
        compiler_params=feed_params(),
        cost_estimate=cost(),
        name="weight_grad",
    )(x, grad, *([] if into is None else [into]))


def unit_terms(pairs, order):
    count = pairs[0][0].shape[0] // 2
    units, width = pairs[0][0].shape[1], pairs[0][1].shape[0]
    refs = 2 * len(pairs)

    def body(order_ref, *rest):
        total = dot(rest[0][...], rest[1][...], ((1,), (1,)))
        for n in range(2, refs, 2):
            total = total + dot(rest[n][...], rest[n + 1][...], ((1,), (1,)))
        for n in range(2):

            @pl.when(pl.program_id(0) == n)
            def _():
                rest[refs + n][...] = total

    rows = pl.BlockSpec((count, units), lambda n, order_ref: (order_ref[n], 0))
    weights = pl.BlockSpec((width, units), lambda n, order_ref: (0, 0), pipeline_mode=pl.Buffered(1))
    return pl.pallas_call(
        body,
        grid_spec=pltpu.PrefetchScalarGridSpec(
            num_scalar_prefetch=1,
            grid=(2,),
            in_specs=[rows, weights] * len(pairs),
            out_specs=[pl.BlockSpec((count, width), lambda n, order_ref: (0, 0))] * 2,
        ),
        out_shape=[jax.ShapeDtypeStruct((count, width), F32)] * 2,
        compiler_params=feed_params(),
        cost_estimate=cost(),
        name="unit_terms",
    )(order, *[v for pair in pairs for v in pair])


ORDER = (1, 3, 2, 0)


def weight_grad_parts(x, grad, places, extra=None):
    count, width = x.shape
    columns = grad.shape[1]
    rows, cols = width // SQUARE, columns // 2
    more = 0 if extra is None else extra.shape[0] // SQUARE
    each = rows + more

    def body(places_ref, x_ref, g_ref, *rest):
        left_ref, right_ref, two_ref, one_ref, own_left, own_right = rest[-6:]
        targets = [
            ((left_ref, 0), (one_ref, 0)),
            ((left_ref, each), (right_ref, 0)),
            ((two_ref, 0), (right_ref, each)),
            ((own_left, 0), (own_right, 0)),
        ]
        value = dot(x_ref[...], g_ref[...], ((0,), (0,))).astype(BF16)
        for n in range(SQUARE):

            @pl.when(pl.program_id(0) == n)
            def _():
                for h, (ref, at) in enumerate(targets[n]):
                    ref[pl.ds(at, rows), :] = value[:, h * cols : (h + 1) * cols]
                    if more:
                        ref[pl.ds(at + rows, more), :] = rest[0][:, h * cols : (h + 1) * cols]

    sizes = [2 * each, 2 * each] + [each] * 4
    return pl.pallas_call(
        body,
        grid_spec=pltpu.PrefetchScalarGridSpec(
            num_scalar_prefetch=1,
            grid=(SQUARE,),
            in_specs=[
                pl.BlockSpec((count, rows), lambda n, places_ref: (0, places_ref[n])),
                pl.BlockSpec((count, columns), lambda n, places_ref: (0, 0)),
            ]
            + ([pl.BlockSpec((more, columns), lambda n, places_ref: (places_ref[n], 0))] if more else []),
            out_specs=[pl.BlockSpec((size, cols), lambda n, places_ref: (0, 0)) for size in sizes],
        ),
        out_shape=[jax.ShapeDtypeStruct((size, cols), BF16) for size in sizes],
        compiler_params=feed_params(),
        cost_estimate=cost(),
        name="weight_grad_parts",
    )(places, x, grad, *([extra] if more else []))


def carried(own, axis, step):
    near_map = shifted(own, axis, step)
    both = jnp.stack([near_map[0] * own[0], own[0] * near_map[1] + own[1]])
    result, reach = near_map, 2
    while reach < lax.axis_size(axis):
        far = shifted(both, axis, step * reach)
        result = jnp.stack([result[0] * far[0], result[0] * far[1] + result[1]])
        both = jnp.stack([both[0] * far[0], both[0] * far[1] + both[1]])
        reach *= 2
    return result[1]


def cross(x, axis, r):
    return lax.ppermute(x, axis, [(i, i ^ r) for i in range(lax.axis_size(axis))])


def total_over(x, axis):
    r = 1
    while r < lax.axis_size(axis):
        x = x + cross(x, axis, r)
        r *= 2
    return x


def after(x, done):
    return lax.optimization_barrier((x, done))


SQUARE = 4


def token_axes():
    return ("fsdp", "ctx") if lax.axis_size("fsdp") == SQUARE else ("ctx", "fsdp")


def together(*values):
    return lax.optimization_barrier(values)


def place(blocks, axis):
    me = lax.axis_index(axis)
    first = blocks[0]
    whole = jnp.zeros((len(blocks),) + first.shape, first.dtype)
    for r, block in enumerate(blocks):
        at = 0
        for piece in block if isinstance(block, list) else [block]:
            whole = lax.dynamic_update_slice(whole, piece[None], (me ^ r, at) + (0,) * (piece.ndim - 1))
            at += piece.shape[0]
    return whole


def near_blocks(x, axis):
    return list(together(cross(x, axis, 1), cross(x, axis, 2)))


def far_block(got, axis):
    mid = got[0].shape[0] // 2
    halves = together(got[0][:mid], got[1][mid:])
    return [cross(halves[0], axis, 2), cross(halves[1], axis, 1)]


def near(x, axis):
    got = near_blocks(x, axis)
    return [x] + got + [far_block(got, axis)]


def low(v):
    return v.astype(BF16)


def wide(v):
    return v.astype(F32)


def near_send(parts, axis):
    return together(cross(parts[0], axis, 1), cross(parts[1], axis, 2))


def near_middle(parts, got):
    rows = got[0].shape[0] // 2
    return together(low(wide(parts[2]) + wide(got[0][rows:])), low(wide(parts[3]) + wide(got[1][:rows])))


def near_second(sums, axis):
    return together(cross(sums[0], axis, 2), cross(sums[1], axis, 1))


def near_last(parts, got, more):
    rows = got[0].shape[0] // 2
    left = wide(parts[4]) + wide(got[0][:rows]) + wide(more[0])
    right = wide(parts[5]) + wide(got[1][rows:]) + wide(more[1])
    return jnp.concatenate([left, right], axis=1)


def gather_in_turn(arrays, ready):
    if lax.axis_size("fsdp") != SQUARE:
        return [lax.all_gather(x, "fsdp", axis=0) for x in arrays], ready
    results = []
    for x in arrays:
        if results:
            x, results[-1] = together(x, results[-1])
        got = near_blocks(x, "fsdp")
        if not results:
            got, ready = together(got, ready)
        results.append([x] + got + [far_block(got, "fsdp")])
    return results, ready


def rows_of(blocks, start, stop):
    if lax.axis_size("fsdp") != SQUARE:
        return blocks[:, :, start:stop].reshape(-1, blocks.shape[-1])
    cut = lambda v: v[:, start:stop]
    whole = place([[cut(v) for v in block] if isinstance(block, list) else cut(block) for block in blocks], "fsdp")
    return whole.reshape(-1, whole.shape[-1])


def token_pieces(x):
    axis = token_axes()[0]
    theirs = swap(x, "tp")
    got = near_blocks(x, axis)
    far = far_block(got, axis)
    got_theirs = [swap(v, "tp") for v in got]
    far_theirs = [swap(v, "tp") for v in far]
    return [got[0], *far, got[1], x, got_theirs[0], *far_theirs, got_theirs[1], theirs]


def token_parts(first, theirs):
    rows, cols = first.shape[0] // SQUARE, first.shape[1] // 2

    def part(start, stop, half):
        here = (slice(start * rows, stop * rows), slice(half * cols, (half + 1) * cols))
        return low(wide(first[here]) + wide(theirs[here]))

    return [part(0, 2, 0), part(1, 3, 1)], [part(2, 3, 0), part(0, 1, 1), part(3, 4, 0), part(3, 4, 1)]


def trade(pieces):
    axis = token_axes()[0]
    me = lax.axis_index(axis)
    return place([pieces(me)] + [cross(pieces(me ^ r), axis, r) for r in range(1, SQUARE)], axis)


def gather_feed(local):
    _, along = token_axes()
    whole = lax.all_gather(local, along, axis=1 if along == "ctx" else 0, tiled=True)
    return whole.reshape(-1, local.shape[2])


def scatter_feed(grad):
    _, along = token_axes()
    if along == "ctx":
        grad = grad.reshape(SQUARE, -1, grad.shape[1])
        return lax.psum_scatter(grad, along, scatter_dimension=1, tiled=True)
    part = lax.psum_scatter(grad, along, scatter_dimension=0, tiled=True)
    return part.reshape(SQUARE, -1, grad.shape[1])


def rms(values):
    return lax.rsqrt(jnp.mean(values * values, axis=-1, keepdims=True) + EPSILON)


def rms_back(values, inverse, gain, grad):
    u = grad * gain
    inner = jnp.mean(values * u, axis=-1, keepdims=True)
    gain_grad = jnp.sum(grad * values * inverse, axis=0)
    return inverse * u - values * (inverse * inverse * inverse) * inner, gain_grad


def shards(
    block_input, segments, token_mask, cotangent, norm_gains, conv_taps, conv_offset, gate_offset,
    decay_logit, intake, gate_blocks, outlet, expand, contract,
):
    rows, length, width = block_input.shape
    depth = intake.shape[0]
    units = intake.shape[2]
    gate_rows = gate_blocks.shape[0]
    hidden_units = contract.shape[1]
    tokens = rows * length
    ctx, tp = lax.axis_size("ctx"), lax.axis_size("tp")
    mine = lax.axis_index("tp")
    half = tokens // tp
    share = -(-hidden_units // (SQUARE * 256)) * 256
    padding = SQUARE * share - hidden_units

    def own(x):
        return lax.dynamic_slice_in_dim(x, mine * half, half, 0)

    def other(x):
        return lax.dynamic_slice_in_dim(x, (1 - mine) * half, half, 0)

    def join(x):
        theirs = swap(x, "tp")
        return jnp.concatenate(
            [jnp.where(mine == 0, x, theirs), jnp.where(mine == 0, theirs, x)], axis=0
        )

    first = jnp.concatenate([intake[:, 1], gate_blocks.reshape(2 * gate_rows, units)], axis=0)
    first = lax.all_gather(first, "ctx", axis=0)
    second = lax.all_gather(jnp.concatenate([intake[:, 0], outlet], axis=0), "ctx", axis=0)

    def cut(w):
        w = jnp.pad(w, ((0, 0), (0, padding)))
        return lambda p: lax.dynamic_slice_in_dim(w, p * share, share, 1)

    down, gate_in, up_in = cut(contract), cut(expand[:, 0]), cut(expand[:, 1])
    local_feed = trade(lambda p: jnp.concatenate([gate_in(p), up_in(p), down(p)], axis=1))

    mask_rows = token_mask.astype(F32).reshape(tokens, 1)
    out_grad = own(cotangent.reshape(tokens, width)).astype(F32) * own(mask_rows)
    local_feed_grad = out_grad.astype(BF16)

    (got_first, got_gelu, got_outlet), local_feed = gather_in_turn(
        [first, second[:, :depth], second[:, depth:]], local_feed
    )
    w_feed = gather_feed(local_feed)
    w_branch = rows_of(got_first, 0, depth)
    blocks = rows_of(got_first, depth, first.shape[1]).reshape(HEAD_W, 2, units).transpose(1, 0, 2)
    w_gelu = rows_of(got_gelu, 0, depth)
    w_outlet = rows_of(got_outlet, 0, depth)

    seg_next = segments + 1
    seg_before = shifted(seg_next[:, -3:], "ctx", 1)
    seg_ext = jnp.concatenate([seg_before, seg_next], axis=1)
    masks = jnp.stack(
        [(seg_ext[:, 3 - k : 3 - k + length] == seg_next).astype(F32) for k in (1, 1, 2, 3)]
        + [jnp.zeros(segments.shape, F32)] * 4,
        axis=2,
    )
    params = jnp.concatenate(
        [
            conv_taps,
            conv_offset[None],
            gate_offset,
            jax.nn.softplus(-decay_logit)[None],
            jax.nn.sigmoid(-decay_logit)[None],
            jnp.zeros((PARAM_ROWS - 9, units), F32),
        ],
        axis=0,
    )

    x = block_input.reshape(tokens, width).astype(F32)
    inverse_one = rms(x)
    normed = (x * inverse_one * norm_gains[0]).astype(BF16)
    x_branch = dot(normed, w_branch, ((1,), (0,))).astype(BF16).reshape(rows, length, units)
    gelu_in = dot(normed, w_gelu, ((1,), (0,))).reshape(rows, length, units)
    x_before = shifted(x_branch[:, -3:], "ctx", 1)
    halo = jnp.pad(x_before, ((0, 0), (5, 0), (0, 0))).astype(F32)
    conv_low, r, i, coef, prod, total = recurrent_forward(x_branch, halo, masks, params, blocks)
    ends = jnp.stack([prod[:, -1], total[:, -1]])
    entering = carried(ends, "ctx", 1)
    state_in = jnp.broadcast_to(entering[:, None], (rows, 8, units))
    states = total + prod * entering[:, None]
    recurrent = (states * jax.nn.gelu(gelu_in, approximate=True)).astype(BF16).reshape(tokens, units)

    sent = swap(dot(other(recurrent), w_outlet, ((1,), (1,))), "tp")
    branch = dot(own(recurrent), w_outlet, ((1,), (1,))) + sent
    residual = own(x) + branch
    inverse_two = rms(residual)
    normed_two = token_pieces((residual * inverse_two * norm_gains[1]).astype(BF16))

    def to_owners(part):
        return trade(lambda p: lax.dynamic_index_in_dim(part, p, 0, keepdims=False))

    local_feed_grad, normed_two = together(local_feed_grad, normed_two)
    feed_grad = jnp.concatenate(token_pieces(local_feed_grad), axis=0)
    normed_two, hidden, by_gate, by_up = feed_forward(normed_two, w_feed)
    down_grad = weight_grad(feed_grad, hidden)
    by_gate, down_grad = after(by_gate, down_grad)
    down_part = scatter_feed(down_grad)
    expand_low, n2g_own, n2g_other = feed_backward(feed_grad, by_gate, by_up, w_feed)

    group = token_axes()[0]
    theirs = swap(n2g_other, "tp")
    parts, kept = token_parts(n2g_own, theirs)
    parts, expand_low = after(parts, expand_low)
    got = near_send(parts, group)
    parts = parts + kept
    expand_all = weight_grad(normed_two, expand_low)
    got, expand_all = after(got, expand_all)
    sums, hidden = after(near_middle(parts, got), hidden)
    more = near_second(sums, group)
    feed_own, feed_other = feed_down(hidden, w_feed)
    more, (feed_own, feed_other) = after(more, (feed_own, feed_other))
    normed_two_grad = near_last(parts, got, more)
    expand_all, down_part = after(expand_all, down_part)
    expand_part = scatter_feed(expand_all)
    feed_theirs = swap(feed_other, "tp")

    norm_part, gain_two = rms_back(residual, inverse_two, norm_gains[1], normed_two_grad)
    residual_grad = out_grad + norm_part
    branch_grad = join(residual_grad.astype(BF16))

    square = lax.axis_size("fsdp") == SQUARE
    places = lax.axis_index("fsdp").astype(jnp.int32) ^ jnp.array(ORDER, jnp.int32)
    feed_parts, feed_kept = token_parts(feed_own, feed_theirs)
    feed_parts, branch_grad = after(feed_parts, branch_grad)
    feed_got = near_send(feed_parts, group)
    feed_parts = feed_parts + feed_kept
    if square:
        outlet_parts = weight_grad_parts(branch_grad, recurrent, places)
    else:
        outlet_parts = weight_grad(branch_grad, recurrent)
    outlet_parts, branch_grad = after(outlet_parts, branch_grad)
    outlet_got = near_send(outlet_parts, "fsdp") if square else outlet_parts
    rec_grad = dot(branch_grad, w_outlet, ((1,), (0,))).reshape(rows, length, units)
    gelu_grad, tprod, tsum = recurrent_adjoint(rec_grad, gelu_in, coef, prod, total, state_in)
    gelu_low = gelu_grad.reshape(tokens, units)
    if square:
        gelu_parts = weight_grad_parts(normed, gelu_low, places)
    else:
        gelu_parts = weight_grad(normed, gelu_low)
    feed_got, outlet_got, gelu_parts, tprod, tsum = together(feed_got, outlet_got, gelu_parts, tprod, tsum)
    feed_sums = near_middle(feed_parts, feed_got)
    if square:
        outlet_sums, gelu_parts, tprod = together(near_middle(outlet_parts, outlet_got), gelu_parts, tprod)
        outlet_more, gelu_got = near_second(outlet_sums, "fsdp"), near_send(gelu_parts, "fsdp")
    heads = jnp.stack([coef[:, 0] * tprod[:, 0], coef[:, 0] * tsum[:, 0]])
    leaving = carried(heads, "ctx", -1)
    leaving = jnp.broadcast_to(leaving[:, None], (rows, 8, units))
    branch_x, before, small, blocks_grad = recurrent_backward(
        tprod, tsum, leaving, prod, total, state_in, coef, r, i, conv_low, x_branch, halo, masks, params, blocks
    )
    from_next = shifted(before[:, 5:], "ctx", -1)
    branch_x = branch_x + jnp.pad(from_next, ((0, 0), (length - 3, 0), (0, 0)))
    branch_low = branch_x.astype(BF16).reshape(tokens, units)
    blocks_rows = blocks_grad.transpose(1, 0, 2).reshape(2 * HEAD_W, units)
    if square:
        branch_parts = weight_grad_parts(normed, branch_low, places, blocks_rows)
        gelu_got, outlet_more, branch_parts, branch_low = together(gelu_got, outlet_more, branch_parts, branch_low)
        gelu_sums, branch_parts, branch_low = together(near_middle(gelu_parts, gelu_got), branch_parts, branch_low)
        gelu_more, branch_got = near_second(gelu_sums, "fsdp"), near_send(branch_parts, "fsdp")
        outlet_part = low(near_last(outlet_parts, outlet_got, outlet_more))
    else:
        branch_parts = weight_grad(normed, branch_low)
        outlet_part, gelu_part = [
            lax.psum_scatter(v, "fsdp", scatter_dimension=0, tiled=True) for v in (outlet_got, gelu_parts)
        ]
        branch_got = branch_parts
    theirs, ours = unit_terms(
        [(branch_low, w_branch), (gelu_low, w_gelu)], jnp.stack([1 - mine, mine]).astype(jnp.int32)
    )
    def scatter_ctx(v):
        return lax.psum_scatter(v, "ctx", scatter_dimension=0, tiled=False)

    outlet_part, expand_part = after(outlet_part, expand_part)
    outlet_part = scatter_ctx(outlet_part.reshape(ctx, depth, units))
    if square:
        gelu_more, branch_got, theirs, ours, outlet_part = together(gelu_more, branch_got, theirs, ours, outlet_part)
        gelu_part = low(near_last(gelu_parts, gelu_got, gelu_more))
        late_sums, gelu_part, down_part = together(near_middle(branch_parts, branch_got), gelu_part, down_part)
        late_more = near_second(late_sums, "fsdp")
    else:
        gelu_part, outlet_part = after(gelu_part, outlet_part)
    gelu_part = scatter_ctx(gelu_part.reshape(ctx, depth, units))
    if square:
        late = low(near_last(branch_parts, branch_got, late_more))
        late = [late[: ctx * depth], late[ctx * depth :]]
    else:
        late = [lax.psum_scatter(v, "fsdp", scatter_dimension=0, tiled=True) for v in (branch_got, blocks_rows)]
    late = jnp.concatenate([v.reshape(ctx, -1, units) for v in late], axis=1)
    normed_grad = ours + swap(theirs, "tp")
    norm_part, gain_one = rms_back(own(x), own(inverse_one), norm_gains[0], normed_grad)
    input_own = residual_grad + norm_part
    down_part = to_owners(down_part)
    late, gelu_part, expand_part, down_part, input_own, gain_one, feed_sums = together(
        late, gelu_part, expand_part, down_part, input_own, gain_one, feed_sums
    )
    late = wide(scatter_ctx(late))
    input_grad = join(input_own).reshape(rows, length, width)
    feed_out = near_last(feed_parts, feed_got, near_second(feed_sums, group))
    block_output = join(low(residual + feed_out)).reshape(rows, length, width)

    expand_part = to_owners(expand_part)

    def columns(part, n):
        return jnp.concatenate([part[p, :, n * share : (n + 1) * share] for p in range(SQUARE)], axis=1)[
            :, :hidden_units
        ].astype(F32)

    contract_grad = columns(down_part, 0)
    expand_grad = jnp.stack([columns(expand_part, 0), columns(expand_part, 1)], axis=1)

    gains = jnp.concatenate([gain_one, gain_two]).reshape(-1, units)
    small = total_over(total_over(jnp.concatenate([small, gains], axis=0), "fsdp"), "ctx")
    gains = total_over(small[8:], "tp").reshape(2, width)
    return (
        block_output,
        input_grad,
        gains,
        small[0:4],
        small[4],
        small[5:7],
        small[7],
        jnp.stack([wide(gelu_part), late[:depth]], axis=1),
        late[depth:].reshape(gate_rows, 2, units),
        wide(outlet_part),
        expand_grad,
        contract_grad,
    )


def solution(mesh):
    placed = (
        P("fsdp", "ctx", None),
        P("fsdp", "ctx"),
        P("fsdp", "ctx"),
        P("fsdp", "ctx", None),
        P(),
        P(None, "tp"),
        P("tp"),
        P(None, "tp"),
        P("tp"),
        P(("fsdp", "ctx"), None, "tp"),
        P(("fsdp", "ctx"), None, "tp"),
        P(("fsdp", "ctx"), "tp"),
        P(("fsdp", "ctx"), None, "tp"),
        P(("fsdp", "ctx"), "tp"),
    )
    return jax.shard_map(
        shards,
        mesh=mesh,
        in_specs=placed,
        out_specs=(
            P("fsdp", "ctx", None),
            P("fsdp", "ctx", None),
            P(),
            P(None, "tp"),
            P("tp"),
            P(None, "tp"),
            P("tp"),
            P(("fsdp", "ctx"), None, "tp"),
            P(("fsdp", "ctx"), None, "tp"),
            P(("fsdp", "ctx"), "tp"),
            P(("fsdp", "ctx"), None, "tp"),
            P(("fsdp", "ctx"), "tp"),
        ),
        check_vma=False,
    )
```
